32 devices in a mesh: seq: 16 (over z, y, x), tp: 2 (over core).
Axes of the slice: x: 2, y: 2, z: 4, core: 2. Of those that a mesh axis runs over, the one named last changes fastest.
Arguments:
- stream: float32 [2048, 2048], P('seq'), may hold values from -6 to 6
- doc_ids: int32 [2048], P('seq'), may hold values from 0 to 4, as said below
- project: bfloat16 [2048, 3, 2048], P('seq', None, 'tp'), may hold values from -0.125 to 0.125
- project_bias: float32 [3, 2048], P(None, 'tp'), may hold values from -3 to 3
- combine: bfloat16 [2048, 2048], P('seq', 'tp'), may hold values from -0.125 to 0.125
- combine_bias: float32 [2048], replicated, may hold values from -3 to 3
- expand: bfloat16 [2048, 8192], P('seq', 'tp'), may hold values from -0.125 to 0.125
- expand_bias: float32 [8192], P('tp'), may hold values from -3 to 3
- shrink: bfloat16 [2048, 8192], P('seq', 'tp'), may hold values from -0.0625 to 0.0625
- shrink_bias: float32 [2048], replicated, may hold values from -3 to 3
- first_gain: float32 [2048], replicated, may hold values from 0.25 to 1.75
- first_bias: float32 [2048], replicated, may hold values from -2 to 2
- inner_gain: float32 [2048], P('tp'), may hold values from 0.25 to 1.75
- inner_bias: float32 [2048], P('tp'), may hold values from -2 to 2
- second_gain: float32 [2048], replicated, may hold values from 0.25 to 1.75
- second_bias: float32 [2048], replicated, may hold values from -2 to 2
- hidden_gain: float32 [8192], P('tp'), may hold values from 0.25 to 1.75
- hidden_bias: float32 [8192], P('tp'), may hold values from -2 to 2
- out_grad: float32 [2048, 2048], P('seq'), may hold values from -18 to 18
Outputs:
- output: float32 [2048, 2048], P('seq')
- stream_grad: float32 [2048, 2048], P('seq')
- project_grad: float32 [2048, 3, 2048], P('seq', None, 'tp')
- project_bias_grad: float32 [3, 2048], P(None, 'tp')
- combine_grad: float32 [2048, 2048], P('seq', 'tp')
- combine_bias_grad: float32 [2048], replicated
- expand_grad: float32 [2048, 8192], P('seq', 'tp')
- expand_bias_grad: float32 [8192], P('tp')
- shrink_grad: float32 [2048, 8192], P('seq', 'tp')
- shrink_bias_grad: float32 [2048], replicated
- first_gain_grad: float32 [2048], replicated
- first_bias_grad: float32 [2048], replicated
- inner_gain_grad: float32 [2048], P('tp')
- inner_bias_grad: float32 [2048], P('tp')
- second_gain_grad: float32 [2048], replicated
- second_bias_grad: float32 [2048], replicated
- hidden_gain_grad: float32 [8192], P('tp')
- hidden_bias_grad: float32 [8192], P('tp')
The draws below stay inside these ranges and needn't reach their ends.
Inputs may be any that keep to these rules, and one draw needn't show every extreme that they name: `doc_ids`: never falling along the stream; every number of 0 to 4 occurs; document 2 begins within the first 128 tokens and ends within the last 128.
All inputs are finite; a program needn't handle non-finite values.
Results may differ from the reference program's by a relative error of at most 0.015.
Values may be sent and summed in bfloat16 or wider, within the bound.
No kernel may reach another device: no remote copies, remote signals or barrier semaphores. Data moves between devices by JAX's collectives and lax.ppermute only.
A program may use at most 320 MiB of HBM per device.

```python
import math
from functools import partial
import jax
import jax.numpy as jnp
from jax import lax

D = 2048
HEADS = 32
HDIM = 64
FF = 8192
TOK_DEV = 128
DOCS = 5
SCALE_BASE = 512
TOKENS = 2048
CENTER = 1024


def draw_doc_ids(key, part):
    key = jax.random.fold_in(key, 11)
    splits = jax.random.split(key, 4)
    quarter = max(TOK_DEV // 4, 2)
    first_cut = jax.random.randint(splits[0], (), 1, quarter)
    second_cut = first_cut + jax.random.randint(splits[1], (), 1, quarter)
    fourth_cut = TOKENS - jax.random.randint(splits[2], (), 1, quarter)
    third_cut = fourth_cut - jax.random.randint(splits[3], (), 1, quarter)
    column = jnp.arange(TOKENS, dtype=jnp.int32)
    result = (column >= first_cut).astype(jnp.int32) + (column >= second_cut).astype(jnp.int32)
    result = result + (column >= third_cut).astype(jnp.int32) + (column >= fourth_cut).astype(jnp.int32)
    return result.astype(jnp.int32)


def draw_out_grad(key, part):
    key = jax.random.fold_in(key, 23)
    value_key, pair_key = jax.random.split(key, 2)
    block_count = TOKENS // TOK_DEV
    base = jnp.clip(jax.random.normal(value_key, (TOKENS, D), jnp.float32), -6.0, 6.0)
    row_place = jnp.arange(TOKENS, dtype=jnp.float32)
    rising = 0.33 + 0.67 * row_place / (TOKENS - 1)
    pairing = jax.random.permutation(pair_key, block_count)
    row_block = jnp.arange(TOKENS, dtype=jnp.int32) // TOK_DEV
    column_block = jnp.arange(D, dtype=jnp.int32) // (D // block_count)
    paired = pairing[row_block][:, None] == column_block[None, :]
    factor = jnp.where(paired, 3.0, 1.0)
    return (base * rising[:, None] * factor).astype(jnp.float32)


def block_scale(rng, dims, cuts, low, largest):
    gain, own = 1.0, jax.random.fold_in(rng, 6)
    for position, shards_of in cuts:
        heights = jnp.exp(jax.random.uniform(jax.random.fold_in(own, position), (shards_of,), jnp.float32, low / len(cuts), largest / len(cuts)))
        gain = gain * jnp.repeat(heights, dims[position] // shards_of).reshape([-1 if axis == position else 1 for axis in range(len(dims))])
    return gain


def gaussian(key, dims, scale, reach, cuts=(), kind=jnp.bfloat16):
    entries = jax.random.normal(key, dims, jnp.float32) * scale
    if len(cuts) > 0:
        entries = block_scale(key, dims, cuts, -0.22, 0.18) * entries
    return jnp.clip(entries, min=-reach, max=reach).astype(kind)


def setup_inputs(seed: int = 0) -> dict:
    streams_of = jax.random.split(jax.random.key(seed), 20)
    return {
        "stream": gaussian(streams_of[0], (TOKENS, D), 1.0, 6.0, ((0, 16),), jnp.float32),
        "doc_ids": draw_doc_ids(jax.random.fold_in(streams_of[19], 71), 0),
        "project": gaussian(streams_of[2], (D, 3, D), D ** -0.5, 0.125, ((0, 16), (2, 2))),
        "project_bias": gaussian(streams_of[3], (3, D), 0.5, 3.0, ((1, 2),), jnp.float32),
        "combine": gaussian(streams_of[4], (D, D), D ** -0.5, 0.125, ((0, 16), (1, 2))),
        "combine_bias": gaussian(streams_of[5], (D,), 0.5, 3.0, (), jnp.float32),
        "expand": gaussian(streams_of[6], (D, FF), D ** -0.5, 0.125, ((0, 16), (1, 2))),
        "expand_bias": gaussian(streams_of[7], (FF,), 0.5, 3.0, ((0, 2),), jnp.float32),
        "shrink": gaussian(streams_of[8], (D, FF), FF ** -0.5, 0.0625, ((0, 16), (1, 2))),
        "shrink_bias": gaussian(streams_of[9], (D,), 0.5, 3.0, (), jnp.float32),
        "first_gain": jnp.clip(1.0 + 0.15 * jax.random.normal(streams_of[10], (D,), jnp.float32), 0.25, 1.75),
        "first_bias": gaussian(streams_of[11], (D,), 0.3, 2.0, (), jnp.float32),
        "inner_gain": jnp.clip(1.0 + 0.15 * jax.random.normal(streams_of[12], (D,), jnp.float32), 0.25, 1.75),
        "inner_bias": gaussian(streams_of[13], (D,), 0.3, 2.0, ((0, 2),), jnp.float32),
        "second_gain": jnp.clip(1.0 + 0.15 * jax.random.normal(streams_of[14], (D,), jnp.float32), 0.25, 1.75),
        "second_bias": gaussian(streams_of[15], (D,), 0.3, 2.0, (), jnp.float32),
        "hidden_gain": jnp.clip(1.0 + 0.15 * jax.random.normal(streams_of[16], (FF,), jnp.float32), 0.25, 1.75),
        "hidden_bias": gaussian(streams_of[17], (FF,), 0.3, 2.0, ((0, 2),), jnp.float32),
        "out_grad": draw_out_grad(jax.random.fold_in(streams_of[19], 71), 0),
    }


@jax.custom_vjp
def low(v):
    return lax.optimization_barrier(v.astype(jnp.bfloat16)).astype(jnp.float32)

@jax.custom_vjp
def low_back(v):
    return v

def low_keep(v):
    return (low(v), None)

def low_pass(kept, grad):
    return (grad,)

def back_keep(v):
    return (v, None)

def back_low(kept, grad):
    return (low(grad),)
low.defvjp(low_keep, low_pass)
low_back.defvjp(back_keep, back_low)
EPSILON = 1e-05
NEGATIVE = -1e+30
HIGH = lax.Precision.HIGHEST

def layer_norm(values, gain_vector, shift_vector):
    average = lax.optimization_barrier(jnp.mean(values, axis=-1, keepdims=True))
    inv_scale = lax.rsqrt(lax.optimization_barrier(jnp.mean(values * values, axis=-1, keepdims=True)) - average * average + EPSILON)
    return (values - average) * inv_scale * gain_vector + shift_vector

def doubled(values_in):
    return jnp.concatenate([values_in, values_in], axis=-1)

def tables(positions, center):
    half_dim = HDIM // 2
    column = jnp.arange(half_dim, dtype=jnp.float32)
    frequency = jnp.exp(column * (-2.0 * math.log(10000.0) / HDIM))
    base_ratio = (2.0 * column + 0.4 * HDIM) / (1.4 * HDIM)
    location = positions.astype(jnp.float32)
    phase_angle = location[:, None] * frequency[None, :]
    exponent = ((location - center) / SCALE_BASE)[:, None] * jnp.log(base_ratio)[None, :]
    return (doubled(jnp.cos(phase_angle)), doubled(jnp.sin(phase_angle)), doubled(jnp.exp(exponent)))

def turn_pairs(values, cosine, sine_table):
    half_dim = values.shape[-1] // 2
    swapped = jnp.concatenate([-values[..., half_dim:], values[..., :half_dim]], axis=-1)
    return values * cosine[:, None, :] + swapped * sine_table[:, None, :]

def place_query(values, cosine, sine_table, growth):
    return turn_pairs(values, cosine, sine_table) * growth[:, None, :] * HDIM ** (-0.5)

def place_key(values, cosine, sine_table, growth):
    return turn_pairs(values, cosine, sine_table) / growth[:, None, :]

def attention(queries, keyed, valued, doc_ids):
    total_rows = queries.shape[0]
    block_rows = math.gcd(total_rows, 512)
    token_rows = jnp.arange(total_rows, dtype=jnp.int32)

    def one_block(pieces):
        query_block, row_block, doc_block = pieces
        scores = low_back(jnp.einsum('qhd,khd->hqk', query_block, keyed, precision=HIGH))
        allowed = (token_rows[None, :] <= row_block[:, None]) & (doc_ids[None, :] == doc_block[:, None])
        scores = jnp.where(allowed[None], scores, NEGATIVE)
        running_max = lax.optimization_barrier(jnp.max(scores, axis=-1, keepdims=True))
        weights_raw = jnp.where(allowed[None], jnp.exp(scores - running_max), 0.0)
        probability = low(weights_raw / lax.optimization_barrier(jnp.sum(weights_raw, axis=-1, keepdims=True)))
        return jnp.einsum('hqk,khd->qhd', probability, valued, precision=HIGH)
    block_count = total_rows // block_rows
    result = lax.map(jax.checkpoint(one_block), (queries.reshape(block_count, block_rows, HEADS, HDIM), token_rows.reshape(block_count, block_rows), doc_ids.reshape(block_count, block_rows)))
    return result.reshape(total_rows, HEADS * HDIM)

def forward(cosine, sine_table, growth, doc_ids, stream, project, project_bias, combine, combine_bias, expand, expand_bias, shrink, shrink_bias, first_gain, first_bias, inner_gain, inner_bias, second_gain, second_bias, hidden_gain, hidden_bias):
    total_rows = stream.shape[0]
    head_shape = (total_rows, HEADS, HDIM)
    normed_in = low(layer_norm(stream, first_gain, first_bias))
    triple = low_back(jnp.einsum('td,dch->tch', normed_in, project, precision=HIGH)) + project_bias[None]
    queries = low(place_query(triple[:, 0].reshape(head_shape), cosine, sine_table, growth))
    keyed = low(place_key(triple[:, 1].reshape(head_shape), cosine, sine_table, growth))
    valued = low(triple[:, 2].reshape(head_shape))
    mixture = low_back(attention(queries, keyed, valued, doc_ids))
    combined_in = low(layer_norm(mixture, inner_gain, inner_bias))
    middle = stream + low_back(jnp.dot(combined_in, combine.T, precision=HIGH)) + combine_bias
    expand_in = low(layer_norm(middle, second_gain, second_bias))
    raised = low_back(jnp.dot(expand_in, expand, precision=HIGH)) + expand_bias
    active = jax.nn.gelu(raised, approximate=False)
    shrink_in = low(layer_norm(active, hidden_gain, hidden_bias))
    return middle + low_back(jnp.dot(shrink_in, shrink.T, precision=HIGH)) + shrink_bias

def reference(stream, doc_ids, project, project_bias, combine, combine_bias, expand, expand_bias, shrink, shrink_bias, first_gain, first_bias, inner_gain, inner_bias, second_gain, second_bias, hidden_gain, hidden_bias, out_grad):
    total_rows = stream.shape[0]
    member = (doc_ids[:, None] == jnp.arange(DOCS, dtype=jnp.int32)[None, :]).astype(jnp.int32)
    counts = lax.optimization_barrier(jnp.sum(member, axis=0))
    starts = jnp.cumsum(counts) - counts
    positions = jnp.arange(total_rows, dtype=jnp.int32) - lax.optimization_barrier(jnp.sum(member * starts[None, :], axis=1))
    cosine, sine_table, growth = tables(positions, CENTER)
    params = (stream, project.astype(jnp.float32), project_bias, combine.astype(jnp.float32), combine_bias, expand.astype(jnp.float32), expand_bias, shrink.astype(jnp.float32), shrink_bias, first_gain, first_bias, inner_gain, inner_bias, second_gain, second_bias, hidden_gain, hidden_bias)
    output, pullback = jax.vjp(partial(forward, cosine, sine_table, growth, doc_ids), *params)
    stream_grad, project_grad, project_bias_grad, combine_grad, combine_bias_grad, expand_grad, expand_bias_grad, shrink_grad, shrink_bias_grad, first_gain_grad, first_bias_grad, inner_gain_grad, inner_bias_grad, second_gain_grad, second_bias_grad, hidden_gain_grad, hidden_bias_grad = pullback(out_grad)
    return (output, stream_grad, project_grad, project_bias_grad, combine_grad, combine_bias_grad, expand_grad, expand_bias_grad, shrink_grad, shrink_bias_grad, first_gain_grad, first_bias_grad, inner_gain_grad, inner_bias_grad, second_gain_grad, second_bias_grad, hidden_gain_grad, hidden_bias_grad)
```

```python
from functools import partial
import math

import jax
import jax.numpy as jnp
from jax import lax
from jax.experimental import pallas as pl
from jax.experimental.pallas import tpu as pltpu
from jax.sharding import PartitionSpec as P

D = 2048
HDIM = 64
FF = 8192
DOCS = 5
SCALE_BASE = 512


EPSILON = 1e-05
NEGATIVE = -1e30
CONTRACT_LAST = (((1,), (1,)), ((), ()))
CONTRACT_FIRST = (((0,), (0,)), ((), ()))


def doubled(values_in):
    return jnp.concatenate([values_in, values_in], axis=-1)


def tables(positions, center):
    half_dim = HDIM // 2
    column = jnp.arange(half_dim, dtype=jnp.float32)
    frequency = jnp.exp(column * (-2.0 * math.log(10000.0) / HDIM))
    base_ratio = (2.0 * column + 0.4 * HDIM) / (1.4 * HDIM)
    location = positions.astype(jnp.float32)
    phase_angle = location[:, None] * frequency[None, :]
    exponent = ((location - center) / SCALE_BASE)[:, None] * jnp.log(base_ratio)[None, :]
    return (
        doubled(jnp.cos(phase_angle)),
        doubled(jnp.sin(phase_angle)),
        doubled(jnp.exp(exponent)),
    )


def turn_pairs(values, cosine, sine_table):
    half_dim = values.shape[-1] // 2
    swapped = jnp.concatenate([-values[..., half_dim:], values[..., :half_dim]], axis=-1)
    return values * cosine[:, None, :] + swapped * sine_table[:, None, :]


def place_query(values, cosine, sine_table, growth):
    return turn_pairs(values, cosine, sine_table) * growth[:, None, :] * HDIM ** (-0.5)


def place_key(values, cosine, sine_table, growth):
    return turn_pairs(values, cosine, sine_table) / growth[:, None, :]


def norm_full(values, gain_vector, shift_vector):
    average = jnp.mean(values, axis=-1, keepdims=True)
    inv_scale = lax.rsqrt(
        jnp.mean(values * values, axis=-1, keepdims=True) - average * average + EPSILON
    )
    normed = (values - average) * inv_scale
    return (normed * gain_vector + shift_vector, normed, inv_scale)


def norm_full_back(incoming, normed, inv_scale, gain_vector):
    scaled_grad = incoming * gain_vector
    first_mean = jnp.mean(scaled_grad, axis=-1, keepdims=True)
    cross_mean = jnp.mean(scaled_grad * normed, axis=-1, keepdims=True)
    return inv_scale * (scaled_grad - first_mean - normed * cross_mean)


def split_sums(first_term, second_term):
    return lax.psum((first_term, second_term), "tp")


def norm_split(values, gain_vector, shift_vector, full_width):
    totals, squares = split_sums(
        jnp.sum(values, axis=-1, keepdims=True), jnp.sum(values * values, axis=-1, keepdims=True)
    )
    average = totals / full_width
    inv_scale = lax.rsqrt(squares / full_width - average * average + EPSILON)
    normed = (values - average) * inv_scale
    return (normed * gain_vector + shift_vector, normed, inv_scale)


def norm_split_back(incoming, normed, inv_scale, gain_vector, full_width):
    scaled_grad = incoming * gain_vector
    totals, crossed = split_sums(
        jnp.sum(scaled_grad, axis=-1, keepdims=True),
        jnp.sum(scaled_grad * normed, axis=-1, keepdims=True),
    )
    return inv_scale * (scaled_grad - totals / full_width - normed * (crossed / full_width))


def branch_total(values):
    return lax.psum(values, "tp")


def doc_of(token_rows, starts):
    return jnp.sum((token_rows[:, None] >= starts[None, 1:]).astype(jnp.int32), axis=1)


def keep_state(state_in):
    return state_in


def gelu_exact(values):
    return jax.nn.gelu(values, approximate=False)


def shards(
    stream,
    doc_ids,
    project,
    project_bias,
    combine,
    combine_bias,
    expand,
    expand_bias,
    shrink,
    shrink_bias,
    first_gain,
    first_bias,
    inner_gain,
    inner_bias,
    second_gain,
    second_bias,
    hidden_gain,
    hidden_bias,
    out_grad,
):
    local_count = stream.shape[0]
    head_width = project.shape[2]
    head_count = head_width // HDIM
    token_rows = lax.axis_index("seq") * local_count + jnp.arange(local_count, dtype=jnp.int32)
    center = lax.axis_size("seq") * local_count // 2
    member = (doc_ids[:, None] == jnp.arange(DOCS, dtype=jnp.int32)[None, :]).astype(jnp.int32)
    counts = lax.psum(jnp.sum(member, axis=0), "seq")
    starts = jnp.cumsum(counts) - counts
    positions = token_rows - jnp.sum(member * starts[None, :], axis=1)
    cosine, sine_table, growth = tables(positions, center)
    first_row = token_rows[0]
    last_row = token_rows[local_count - 1]
    first_doc = doc_ids[0]
    last_doc = doc_ids[local_count - 1]
    full_project, full_combine, full_expand, full_shrink = (
        lax.all_gather(project, "seq", axis=0, tiled=True),
        lax.all_gather(combine, "seq", axis=0, tiled=True),
        lax.all_gather(expand, "seq", axis=0, tiled=True),
        lax.all_gather(shrink, "seq", axis=0, tiled=True),
    )
    first_out, first_normed, first_scale = norm_full(stream, first_gain, first_bias)
    normed_in = first_out.astype(jnp.bfloat16)
    triple = (
        jnp.einsum("td,dch->tch", normed_in, full_project, preferred_element_type=jnp.float32)
        + project_bias[None]
    )
    head_shape = (local_count, head_count, HDIM)
    query_raw = triple[:, 0].reshape(head_shape)
    key_raw = triple[:, 1].reshape(head_shape)
    queries = place_query(query_raw, cosine, sine_table, growth).astype(jnp.bfloat16)
    keyed = place_key(key_raw, cosine, sine_table, growth).astype(jnp.bfloat16)
    valued = triple[:, 2].reshape(head_shape).astype(jnp.bfloat16)
    start_state = (
        jnp.full((head_count, local_count), NEGATIVE, jnp.float32),
        jnp.zeros((head_count, local_count), jnp.float32),
        jnp.zeros((head_count, local_count, HDIM), jnp.float32),
    )
    key_part = lax.all_gather(keyed.reshape(local_count, head_width), "seq", axis=0, tiled=True)
    value_part = lax.all_gather(valued.reshape(local_count, head_width), "seq", axis=0, tiled=True)
    piece_rows = key_part.shape[0]
    key_rows = jnp.arange(piece_rows, dtype=jnp.int32)
    key_docs = doc_of(key_rows, starts)
    skipped = (jnp.int32(0) > last_row) | (key_docs[piece_rows - 1] < first_doc)

    def attend_compute(state):
        running_max, running_sum, summed = state
        key_block = key_part.reshape(piece_rows, head_count, HDIM)
        value_block = value_part.reshape(piece_rows, head_count, HDIM)
        allowed = (
            (key_rows[None, :] <= token_rows[:, None]) & (key_docs[None, :] == doc_ids[:, None])
        )[None]
        scores = jnp.einsum("qhd,khd->hqk", queries, key_block, preferred_element_type=jnp.float32)
        scores = jnp.where(allowed, scores, NEGATIVE)
        newest = jnp.maximum(running_max, jnp.max(scores, axis=-1))
        weights_raw = jnp.where(allowed, jnp.exp(scores - newest[..., None]), 0.0)
        running_sum = jnp.sum(weights_raw, axis=-1)
        summed = jnp.einsum(
            "hqk,khd->hqd",
            weights_raw.astype(jnp.bfloat16),
            value_block,
            preferred_element_type=jnp.float32,
        )
        return (newest, running_sum, summed)

    running_max, running_sum, summed = lax.cond(skipped, keep_state, attend_compute, start_state)
    mixture = jnp.transpose(summed / running_sum[..., None], (1, 0, 2)).reshape(
        local_count, head_width
    )
    log_total = running_max + jnp.log(running_sum)
    inner_out, inner_normed, inner_scale = norm_split(mixture, inner_gain, inner_bias, D)
    combined_in = inner_out.astype(jnp.bfloat16)
    middle = (
        stream
        + branch_total(
            lax.dot_general(
                combined_in, full_combine, CONTRACT_LAST, preferred_element_type=jnp.float32
            )
        )
        + combine_bias
    )
    second_out, second_normed, second_scale = norm_full(middle, second_gain, second_bias)
    expand_in = second_out.astype(jnp.bfloat16)
    raised = jnp.dot(expand_in, full_expand, preferred_element_type=jnp.float32) + expand_bias
    active, gelu_back = jax.vjp(gelu_exact, raised)
    hidden_out, hidden_normed, hidden_scale = norm_split(active, hidden_gain, hidden_bias, FF)
    shrink_in = hidden_out.astype(jnp.bfloat16)
    output = (
        middle
        + branch_total(
            lax.dot_general(
                shrink_in, full_shrink, CONTRACT_LAST, preferred_element_type=jnp.float32
            )
        )
        + shrink_bias
    )
    back_project, back_combine, back_expand, back_shrink = (
        lax.all_gather(project, "seq", axis=0, tiled=True),
        lax.all_gather(combine, "seq", axis=0, tiled=True),
        lax.all_gather(expand, "seq", axis=0, tiled=True),
        lax.all_gather(shrink, "seq", axis=0, tiled=True),
    )
    shrink_bias_grad = jnp.sum(out_grad, axis=0)
    low_out = out_grad.astype(jnp.bfloat16)
    shrink_term = lax.dot_general(
        low_out, shrink_in, CONTRACT_FIRST, preferred_element_type=jnp.float32
    )
    hidden_grad = jnp.dot(low_out, back_shrink, preferred_element_type=jnp.float32)
    hidden_gain_grad = jnp.sum(hidden_grad * hidden_normed, axis=0)
    hidden_bias_grad = jnp.sum(hidden_grad, axis=0)
    active_grad = norm_split_back(hidden_grad, hidden_normed, hidden_scale, hidden_gain, FF)
    (raised_grad,) = gelu_back(active_grad)
    expand_bias_grad = jnp.sum(raised_grad, axis=0)
    low_raised = raised_grad.astype(jnp.bfloat16)
    expand_term = lax.dot_general(
        expand_in, low_raised, CONTRACT_FIRST, preferred_element_type=jnp.float32
    )
    second_grad = branch_total(
        lax.dot_general(low_raised, back_expand, CONTRACT_LAST, preferred_element_type=jnp.float32)
    )
    second_gain_grad = jnp.sum(second_grad * second_normed, axis=0)
    second_bias_grad = jnp.sum(second_grad, axis=0)
    middle_grad = out_grad + norm_full_back(second_grad, second_normed, second_scale, second_gain)
    combine_bias_grad = jnp.sum(middle_grad, axis=0)
    low_middle = middle_grad.astype(jnp.bfloat16)
    combine_term = lax.dot_general(
        low_middle, combined_in, CONTRACT_FIRST, preferred_element_type=jnp.float32
    )
    inner_grad = jnp.dot(low_middle, back_combine, preferred_element_type=jnp.float32)
    inner_gain_grad = jnp.sum(inner_grad * inner_normed, axis=0)
    inner_bias_grad = jnp.sum(inner_grad, axis=0)
    mixture_grad = norm_split_back(inner_grad, inner_normed, inner_scale, inner_gain, D)
    low_mixture = mixture_grad.astype(jnp.bfloat16)
    low_mixture3 = low_mixture.reshape(head_shape)
    delta = jnp.sum(low_mixture3.astype(jnp.float32) * mixture.reshape(head_shape), axis=-1)
    delta_heads = delta.T
    zero_heads = jnp.zeros(head_shape, jnp.float32)
    query_key_part = lax.all_gather(
        keyed.reshape(local_count, head_width), "seq", axis=0, tiled=True
    )
    query_value_part = lax.all_gather(
        valued.reshape(local_count, head_width), "seq", axis=0, tiled=True
    )
    query_piece_rows = query_key_part.shape[0]
    query_key_rows = jnp.arange(query_piece_rows, dtype=jnp.int32)
    query_key_docs = doc_of(query_key_rows, starts)
    skipped = (jnp.int32(0) > last_row) | (query_key_docs[query_piece_rows - 1] < first_doc)

    def query_compute(gathered):
        key_block = query_key_part.reshape(query_piece_rows, head_count, HDIM)
        value_block = query_value_part.reshape(query_piece_rows, head_count, HDIM)
        allowed = (
            (query_key_rows[None, :] <= token_rows[:, None])
            & (query_key_docs[None, :] == doc_ids[:, None])
        )[None]
        scores = jnp.einsum("qhd,khd->hqk", queries, key_block, preferred_element_type=jnp.float32)
        probability = jnp.where(allowed, jnp.exp(scores - log_total[..., None]), 0.0)
        pushes = jnp.einsum(
            "qhd,khd->hqk", low_mixture3, value_block, preferred_element_type=jnp.float32
        )
        dscore = (probability * (pushes - delta_heads[..., None])).astype(jnp.bfloat16)
        return jnp.einsum("hqk,khd->qhd", dscore, key_block, preferred_element_type=jnp.float32)

    query_grad3 = lax.cond(skipped, keep_state, query_compute, zero_heads)
    query_part = lax.all_gather(
        queries.astype(jnp.float32).reshape(local_count, head_width), "seq", axis=0, tiled=True
    )
    pull_part = lax.all_gather(low_mixture.astype(jnp.float32), "seq", axis=0, tiled=True)
    total_part = lax.all_gather(log_total.T, "seq", axis=0, tiled=True)
    delta_part = lax.all_gather(delta, "seq", axis=0, tiled=True)
    key_piece_rows = query_part.shape[0]
    query_rows = jnp.arange(key_piece_rows, dtype=jnp.int32)
    query_docs = doc_of(query_rows, starts)
    skipped = (query_rows[key_piece_rows - 1] < first_row) | (query_docs[0] > last_doc)

    def key_compute(state):
        query_block = query_part.astype(jnp.bfloat16).reshape(key_piece_rows, head_count, HDIM)
        pull_block = pull_part.astype(jnp.bfloat16).reshape(key_piece_rows, head_count, HDIM)
        allowed = (
            (token_rows[None, :] <= query_rows[:, None]) & (doc_ids[None, :] == query_docs[:, None])
        )[None]
        scores = jnp.einsum("qhd,khd->hqk", query_block, keyed, preferred_element_type=jnp.float32)
        probability = jnp.where(allowed, jnp.exp(scores - total_part.T[..., None]), 0.0)
        pushes = jnp.einsum("qhd,khd->hqk", pull_block, valued, preferred_element_type=jnp.float32)
        dscore = (probability * (pushes - delta_part.T[..., None])).astype(jnp.bfloat16)
        key_acc = jnp.einsum(
            "hqk,qhd->khd", dscore, query_block, preferred_element_type=jnp.float32
        )
        value_acc = jnp.einsum(
            "hqk,qhd->khd",
            probability.astype(jnp.bfloat16),
            pull_block,
            preferred_element_type=jnp.float32,
        )
        return (key_acc, value_acc)

    key_grad3, value_grad3 = lax.cond(skipped, keep_state, key_compute, (zero_heads, zero_heads))
    _, query_back = jax.vjp(
        partial(place_query, cosine=cosine, sine_table=sine_table, growth=growth), query_raw
    )
    _, key_back = jax.vjp(
        partial(place_key, cosine=cosine, sine_table=sine_table, growth=growth), key_raw
    )
    (query_grad,) = query_back(query_grad3)
    (key_grad,) = key_back(key_grad3)
    triple_grad = jnp.stack(
        [
            query_grad.reshape(local_count, head_width),
            key_grad.reshape(local_count, head_width),
            value_grad3.reshape(local_count, head_width),
        ],
        axis=1,
    )
    project_bias_grad = jnp.sum(triple_grad, axis=0)
    low_triple = triple_grad.astype(jnp.bfloat16)
    project_term = jnp.einsum(
        "td,tch->dch", normed_in, low_triple, preferred_element_type=jnp.float32
    )
    first_grad = branch_total(
        jnp.einsum("tch,dch->td", low_triple, back_project, preferred_element_type=jnp.float32)
    )
    first_gain_grad = jnp.sum(first_grad * first_normed, axis=0)
    first_bias_grad = jnp.sum(first_grad, axis=0)
    stream_grad = middle_grad + norm_full_back(first_grad, first_normed, first_scale, first_gain)
    project_grad, combine_grad, expand_grad, shrink_grad = (
        lax.psum_scatter(project_term, "seq", scatter_dimension=0, tiled=True),
        lax.psum_scatter(combine_term, "seq", scatter_dimension=0, tiled=True),
        lax.psum_scatter(expand_term, "seq", scatter_dimension=0, tiled=True),
        lax.psum_scatter(shrink_term, "seq", scatter_dimension=0, tiled=True),
    )
    (
        first_gain_grad,
        first_bias_grad,
        project_bias_grad,
        inner_gain_grad,
        inner_bias_grad,
        combine_bias_grad,
        second_gain_grad,
        second_bias_grad,
        expand_bias_grad,
        hidden_gain_grad,
        hidden_bias_grad,
        shrink_bias_grad,
    ) = lax.psum(
        (
            first_gain_grad,
            first_bias_grad,
            project_bias_grad,
            inner_gain_grad,
            inner_bias_grad,
            combine_bias_grad,
            second_gain_grad,
            second_bias_grad,
            expand_bias_grad,
            hidden_gain_grad,
            hidden_bias_grad,
            shrink_bias_grad,
        ),
        "seq",
    )
    return (
        output,
        stream_grad,
        project_grad,
        project_bias_grad,
        combine_grad,
        combine_bias_grad,
        expand_grad,
        expand_bias_grad,
        shrink_grad,
        shrink_bias_grad,
        first_gain_grad,
        first_bias_grad,
        inner_gain_grad,
        inner_bias_grad,
        second_gain_grad,
        second_bias_grad,
        hidden_gain_grad,
        hidden_bias_grad,
    )


BF = jnp.bfloat16
F32 = jnp.float32
GRID = (4, 2, 2)
SEQ = 16
ALIGNED = (((0,), (0,)), ((), ()))
PLAIN = (((1,), (0,)), ((), ()))
HOPS = {
    "x": [(i, i ^ 1) for i in range(SEQ)],
    "y": [(i, i ^ 2) for i in range(SEQ)],
    "z": [(i, (i + 4) % SEQ) for i in range(SEQ)],
    "back": [((i + 4) % SEQ, i) for i in range(SEQ)],
    "far": [(i, (i + 8) % SEQ) for i in range(SEQ)],
}


def fits_heads(mesh):
    return mesh.shape["seq"] == SEQ and mesh.shape["tp"] == 2


def hop(values, way):
    if way == "t":
        return lax.ppermute(values, "tp", [(0, 1), (1, 0)])
    return lax.ppermute(values, "seq", HOPS[way])


def gather_along(values, way, axis):
    parts = [values]
    for _ in range(3 if way == "z" else 1):
        parts.append(hop(parts[-1], way))
    return jnp.stack(parts, axis=axis)


def gather_zxy(values):
    return gather_along(gather_along(gather_along(values, "z", 0), "x", 1), "y", 1)


def gather_yxz(values):
    return gather_along(gather_along(gather_along(values, "y", 0), "x", 1), "z", 0)


def add_low(first, second):
    return (first.astype(F32) + second.astype(F32)).astype(BF)


def fold(values, way, axis, add=add_low):
    def part(i):
        return lax.index_in_dim(values, i, axis, keepdims=False)

    if way != "z":
        return add(part(0), hop(part(1), way))
    total = part(3)
    for i in (2, 1):
        total = add(part(i), hop(total, "back"))
    return add(part(0), hop(total, "back"))


def add_wide(first, second):
    return first.astype(F32) + second.astype(F32)


def scatter_yxz(values):
    return fold(fold(fold(values, "y", 1), "x", 1), "z", 0, add_wide)


def scatter_zxy(values):
    return fold(fold(fold(values, "z", 0), "x", 1), "y", 0, add_wide)


def gather_rows(own):
    half = own.shape[1] // 2
    mine = [gather_zxy(own[:, :half]), gather_yxz(own[:, half:])]
    mine = [piece.reshape(-1, half) for piece in mine]
    return mine + [hop(piece, "t") for piece in mine]


def scatter_rows(pieces):
    first = add_low(pieces[0], hop(pieces[2], "t"))
    second = add_low(pieces[1], hop(pieces[3], "t"))
    shape = GRID + (-1, first.shape[1])
    return jnp.concatenate(
        [scatter_yxz(first.reshape(shape)), scatter_zxy(second.reshape(shape))], axis=1
    )


def swap_by(flag, values, axis):
    return jnp.where(flag == 0, values, jnp.flip(values, axis))


def own_half(side, values, axis=-1):
    left, right = jnp.split(values, 2, axis=axis)
    return jnp.where(side == 0, left, right)


def join_halves(side, mine, other, axis=-1):
    return jnp.concatenate(
        [jnp.where(side == 0, mine, other), jnp.where(side == 0, other, mine)], axis=axis
    )


def turn_halves(side, values, axis=0):
    left, right = jnp.split(values, 2, axis=axis)
    return jnp.concatenate(
        [jnp.where(side == 0, left, right), jnp.where(side == 0, right, left)], axis=axis
    )


def token_sum(values):
    shape = values.shape
    values = (values + hop(values, "t")).reshape((shape[0],) + GRID + (-1,))
    values = values + jnp.flip(hop(values, "x"), 3)
    values = values + jnp.flip(hop(values, "y"), 2)
    values = values + jnp.roll(hop(values, "z"), 1, 1)
    values = values + jnp.roll(hop(values, "far"), 2, 1)
    return values.reshape(shape)


def seq_sum(values):
    for way in ("x", "y", "z", "far"):
        values = values + hop(values, way)
    return values


def pair_sum(values):
    return values + hop(values, "t")


def dot(first, second, dims):
    return lax.dot_general(first, second, dims, preferred_element_type=F32)


BLOCK = 512
KERNEL_BYTES = 48 * 1024 * 1024


def attend_kernel(
    order_ref, raw_ref, bias_ref, cosine_ref, sine_ref, growth_ref, begin_ref,
    kept_ref, mixture_ref, log_ref, wide,
):
    tokens = raw_ref.shape[1]
    half = HDIM // 2
    rows = tokens // SEQ
    for block in range(SEQ):
        place = pl.ds(pl.multiple_of(order_ref[block] * rows, rows), rows)
        wide[:, block * rows : (block + 1) * rows] = raw_ref[:, place] + bias_ref[...]
    cosine, sine, growth = cosine_ref[...], sine_ref[...], growth_ref[...]
    first, second = wide[0:half, :], wide[half:HDIM, :]
    scaled = growth * HDIM ** (-0.5)
    kept_ref[0:half, :] = ((first * cosine - second * sine) * scaled).astype(BF)
    kept_ref[half:HDIM, :] = ((second * cosine + first * sine) * scaled).astype(BF)
    first, second = wide[HDIM : HDIM + half, :], wide[HDIM + half : 2 * HDIM, :]
    kept_ref[HDIM : HDIM + half, :] = ((first * cosine - second * sine) / growth).astype(BF)
    kept_ref[HDIM + half : 2 * HDIM, :] = ((second * cosine + first * sine) / growth).astype(BF)
    kept_ref[2 * HDIM :, :] = wide[2 * HDIM :, :].astype(BF)
    key_rows = lax.broadcasted_iota(jnp.int32, (BLOCK, BLOCK), 0)
    query_rows = lax.broadcasted_iota(jnp.int32, (BLOCK, BLOCK), 1)
    for i in range(tokens // BLOCK):
        columns = slice(i * BLOCK, (i + 1) * BLOCK)
        queries = kept_ref[0:HDIM, columns]
        begin = begin_ref[:, columns]
        largest = jnp.full((1, BLOCK), NEGATIVE, F32)
        total = jnp.zeros((1, BLOCK), F32)
        summed = jnp.zeros((HDIM, BLOCK), F32)
        for j in range(i, -1, -1):
            place = slice(j * BLOCK, (j + 1) * BLOCK)
            scores = dot(kept_ref[HDIM : 2 * HDIM, place], queries, ALIGNED)
            allowed = key_rows + j * BLOCK >= begin
            if j == i:
                allowed = allowed & (key_rows <= query_rows)
            scores = jnp.where(allowed, scores, NEGATIVE)
            newest = jnp.maximum(largest, jnp.max(scores, axis=0, keepdims=True))
            weights = jnp.exp(scores - newest)
            shrunk = jnp.exp(largest - newest)
            total = total * shrunk + jnp.sum(weights, axis=0, keepdims=True)
            summed = summed * shrunk + dot(
                kept_ref[2 * HDIM :, place], weights.astype(BF), PLAIN
            )
            largest = newest
        mixture = summed / total
        for block in range(BLOCK // rows):
            mixture_ref[i * (BLOCK // rows) + block] = mixture[:, block * rows : (block + 1) * rows]
        log_ref[:, columns] = largest + jnp.log(total)


def retreat_kernel(
    order_ref, kept_ref, pull_ref, mixture_ref, log_ref, cosine_ref, sine_ref, growth_ref, begin_ref,
    low_ref, bias_ref, pulls, delta, query_sum, key_sum, value_sum,
):
    tokens = kept_ref.shape[1]
    half = HDIM // 2
    rows = tokens // SEQ
    for block in range(SEQ):
        place = slice(block * rows, (block + 1) * rows)
        pulls[:, place] = pull_ref[block]
        delta[:, place] = jnp.sum(
            pull_ref[block].astype(F32) * mixture_ref[block], axis=0, keepdims=True
        )
    key_rows = lax.broadcasted_iota(jnp.int32, (BLOCK, BLOCK), 0)
    query_rows = lax.broadcasted_iota(jnp.int32, (BLOCK, BLOCK), 1)
    for i in range(tokens // BLOCK):
        columns = slice(i * BLOCK, (i + 1) * BLOCK)
        queries = kept_ref[0:HDIM, columns]
        pull = pulls[:, columns]
        begin = begin_ref[:, columns]
        logs = log_ref[:, columns]
        offset = delta[:, columns]
        query_part = jnp.zeros((HDIM, BLOCK), F32)
        for j in range(i + 1):
            place = slice(j * BLOCK, (j + 1) * BLOCK)
            keys = kept_ref[HDIM : 2 * HDIM, place]
            scores = dot(keys, queries, ALIGNED)
            allowed = key_rows + j * BLOCK >= begin
            if j == i:
                allowed = allowed & (key_rows <= query_rows)
            chance = jnp.where(allowed, jnp.exp(scores - logs), 0.0)
            pushes = dot(kept_ref[2 * HDIM :, place], pull, ALIGNED)
            dscore = (chance * (pushes - offset)).astype(BF)
            query_part = query_part + dot(keys, dscore, PLAIN)
            key_part = dot(queries, dscore, CONTRACT_LAST)
            value_part = dot(pull, chance.astype(BF), CONTRACT_LAST)
            if j == i:
                key_sum[:, place] = key_part
                value_sum[:, place] = value_part
            else:
                key_sum[:, place] += key_part
                value_sum[:, place] += value_part
        query_sum[:, columns] = query_part
    cosine, sine, growth = cosine_ref[...], sine_ref[...], growth_ref[...]
    scaled = growth * HDIM ** (-0.5)
    first, second = query_sum[0:half, :] * scaled, query_sum[half:, :] * scaled
    pieces = [first * cosine + second * sine, second * cosine - first * sine]
    first, second = key_sum[0:half, :] / growth, key_sum[half:, :] / growth
    pieces += [first * cosine + second * sine, second * cosine - first * sine]
    pieces += [value_sum[0:half, :], value_sum[half:, :]]
    for index, piece in enumerate(pieces):
        lanes = slice(index * half, (index + 1) * half)
        bias_ref[lanes, :] = jnp.sum(piece, axis=1, keepdims=True)
        low = piece.astype(BF)
        for block in range(SEQ):
            place = pl.ds(pl.multiple_of(order_ref[block] * rows, rows), rows)
            low_ref[lanes, place] = low[:, block * rows : (block + 1) * rows]


def whole(count):
    return [pl.BlockSpec(memory_space=pltpu.VMEM) for _ in range(count)]


def attend(order, raw, bias, cosine, sine, growth, begin):
    tokens = raw.shape[1]
    return pl.pallas_call(
        attend_kernel,
        out_shape=(
            jax.ShapeDtypeStruct((3 * HDIM, tokens), BF),
            jax.ShapeDtypeStruct((SEQ, HDIM, tokens // SEQ), F32),
            jax.ShapeDtypeStruct((1, tokens), F32),
        ),
        in_specs=[pl.BlockSpec(memory_space=pltpu.SMEM)] + whole(6),
        out_specs=tuple(whole(3)),
        scratch_shapes=[pltpu.VMEM((3 * HDIM, tokens), F32)],
        compiler_params=pltpu.CompilerParams(vmem_limit_bytes=KERNEL_BYTES),
        cost_estimate=pl.CostEstimate(
            flops=2 * tokens * tokens * HDIM, bytes_accessed=8 * 192 * tokens,
            transcendentals=tokens * tokens // 2,
        ),
    )(order, raw, bias, cosine, sine, growth, begin)


def retreat(order, kept, pull, mixture, logs, cosine, sine, growth, begin):
    tokens = kept.shape[1]
    return pl.pallas_call(
        retreat_kernel,
        out_shape=(
            jax.ShapeDtypeStruct((3 * HDIM, tokens), BF),
            jax.ShapeDtypeStruct((3 * HDIM, 1), F32),
        ),
        in_specs=[pl.BlockSpec(memory_space=pltpu.SMEM)] + whole(8),
        out_specs=tuple(whole(2)),
        scratch_shapes=[
            pltpu.VMEM((HDIM, tokens), BF),
            pltpu.VMEM((1, tokens), F32),
            pltpu.VMEM((HDIM, tokens), F32),
            pltpu.VMEM((HDIM, tokens), F32),
            pltpu.VMEM((HDIM, tokens), F32),
        ],
        compiler_params=pltpu.CompilerParams(vmem_limit_bytes=KERNEL_BYTES),
        cost_estimate=pl.CostEstimate(
            flops=5 * tokens * tokens * HDIM, bytes_accessed=8 * 192 * tokens,
            transcendentals=tokens * tokens // 2,
        ),
    )(order, kept, pull, mixture, logs, cosine, sine, growth, begin)


def to_owners(values):
    return lax.all_to_all(values, "seq", split_axis=0, concat_axis=0, tiled=True)


def column_owners(weights, rows, side):
    width = weights.shape[1] // SEQ
    moved = to_owners(jnp.transpose(weights.reshape(rows, SEQ, width), (1, 0, 2)))
    return turn_halves(side, moved.reshape(SEQ * rows, width))


def row_owners(pieces, rows, side):
    full = turn_halves(side, jnp.concatenate(pieces, axis=0).astype(BF))
    width = full.shape[1]
    moved = to_owners(full.reshape(SEQ, rows, width))
    return jnp.transpose(moved, (1, 0, 2)).reshape(rows, SEQ * width).astype(F32)


def head_shards(
    stream,
    doc_ids,
    project,
    project_bias,
    combine,
    combine_bias,
    expand,
    expand_bias,
    shrink,
    shrink_bias,
    first_gain,
    first_bias,
    inner_gain,
    inner_bias,
    second_gain,
    second_bias,
    hidden_gain,
    hidden_bias,
    out_grad,
):
    rows = stream.shape[0]
    tokens = SEQ * rows
    head_width = project.shape[2]
    width = expand.shape[1] // SEQ
    spot = lax.axis_index("seq")
    side = lax.axis_index("tp")
    spot_z, spot_y, spot_x = spot // 4, (spot // 2) % 2, spot % 2
    blocks = jnp.arange(SEQ, dtype=jnp.int32)
    order = (
        ((spot_z - blocks // 4) % 4) * 4 + (spot_y ^ ((blocks // 2) % 2)) * 2 + (spot_x ^ (blocks % 2))
    )

    def mine(values, axis=-1):
        return own_half(side, values, axis)

    def my_units(vector, size):
        return lax.dynamic_slice_in_dim(vector, spot * size, size, axis=-1)

    first_out, first_normed, first_scale = norm_full(stream, first_gain, first_bias)
    normed_pieces = gather_rows(mine(first_out.astype(BF)))
    docs_near = gather_zxy(doc_ids[None, :]).reshape(SEQ, rows)
    project_moved = to_owners(
        jnp.transpose(project.reshape(rows, 3, SEQ, HDIM), (2, 1, 3, 0)).reshape(SEQ, 3 * HDIM, rows)
    )
    project_mine = turn_halves(
        side, jnp.transpose(project_moved, (1, 0, 2)).reshape(3 * HDIM, tokens), axis=1
    )
    project_pieces = jnp.split(project_mine, 4, axis=1)

    docs = docs_near[order].reshape(tokens)
    member = (docs[:, None] == jnp.arange(DOCS, dtype=jnp.int32)[None, :]).astype(jnp.int32)
    counts = jnp.sum(member, axis=0)
    starts = jnp.cumsum(counts) - counts
    begin = jnp.sum(member * starts[None, :], axis=1)
    positions = jnp.arange(tokens, dtype=jnp.int32) - begin
    column = jnp.arange(HDIM // 2, dtype=F32)
    frequency = jnp.exp(column * (-2.0 * math.log(10000.0) / HDIM))
    base_ratio = (2.0 * column + 0.4 * HDIM) / (1.4 * HDIM)
    location = positions.astype(F32)
    phase_angle = frequency[:, None] * location[None, :]
    cosine, sine = jnp.cos(phase_angle), jnp.sin(phase_angle)
    growth = jnp.exp(
        jnp.log(base_ratio)[:, None] * ((location - tokens // 2) / SCALE_BASE)[None, :]
    )
    begin = begin[None, :]

    raw = sum(
        dot(weights, piece, CONTRACT_LAST)
        for weights, piece in zip(project_pieces, normed_pieces, strict=True)
    )
    head_bias = my_units(project_bias, HDIM).reshape(3 * HDIM, 1)
    kept, mixture, logs = attend(order, raw, head_bias, cosine, sine, growth, begin)

    spread = to_owners(mixture).reshape(head_width, rows)
    full_combine = lax.all_gather(combine, "seq", axis=0, tiled=True)
    sums = pair_sum(jnp.stack([jnp.sum(spread, axis=0), jnp.sum(spread * spread, axis=0)]))
    average = sums[0:1] / D
    inner_scale = lax.rsqrt(sums[1:2] / D - average * average + EPSILON)
    inner_normed = (spread - average) * inner_scale
    combined_in = (inner_normed * inner_gain[:, None] + inner_bias[:, None]).astype(BF)
    branch = dot(combined_in, full_combine, (((0,), (1,)), ((), ())))
    left, right = jnp.split(branch, 2, axis=1)
    branch = jnp.where(side == 0, left, right) + hop(jnp.where(side == 0, right, left), "t")
    middle = mine(stream) + branch + mine(combine_bias)
    sums = pair_sum(jnp.stack([jnp.sum(middle, axis=1), jnp.sum(middle * middle, axis=1)]))
    average = (sums[0] / D)[:, None]
    second_scale = lax.rsqrt((sums[1] / D)[:, None] - average * average + EPSILON)
    second_normed = (middle - average) * second_scale
    gain_half, bias_half = mine(second_gain), mine(second_bias)
    expand_pieces = gather_rows((second_normed * gain_half + bias_half).astype(BF))

    out_grad_mine = mine(out_grad)
    low_out_pieces = gather_rows(out_grad_mine.astype(BF))
    expand_mine = jnp.split(column_owners(expand, rows, side), 4, axis=0)
    shrink_mine = jnp.split(column_owners(shrink, rows, side), 4, axis=0)
    unit_gain, unit_bias = my_units(hidden_gain, width), my_units(hidden_bias, width)
    hidden_grad = sum(
        dot(piece, weights, PLAIN)
        for piece, weights in zip(low_out_pieces, shrink_mine, strict=True)
    )
    raised = sum(
        dot(piece, weights, PLAIN)
        for piece, weights in zip(expand_pieces, expand_mine, strict=True)
    ) + my_units(expand_bias, width)
    active, gelu_back = jax.vjp(gelu_exact, raised)
    scaled_grad = hidden_grad * unit_gain
    sums = token_sum(
        jnp.stack(
            [
                jnp.sum(active, axis=1),
                jnp.sum(active * active, axis=1),
                jnp.sum(scaled_grad, axis=1),
                jnp.sum(scaled_grad * active, axis=1),
            ]
        )
    )
    average = (sums[0] / FF)[:, None]
    hidden_scale = lax.rsqrt((sums[1] / FF)[:, None] - average * average + EPSILON)
    hidden_normed = (active - average) * hidden_scale
    shrink_in = (hidden_normed * unit_gain + unit_bias).astype(BF)
    grad_mean = (sums[2] / FF)[:, None]
    cross_mean = hidden_scale * ((sums[3] / FF)[:, None] - average * grad_mean)
    active_grad = hidden_scale * (scaled_grad - grad_mean - hidden_normed * cross_mean)
    (raised_grad,) = gelu_back(active_grad)
    low_raised = raised_grad.astype(BF)
    second_grad = scatter_rows(
        [dot(low_raised, weights, CONTRACT_LAST).astype(BF) for weights in expand_mine]
    )
    output_sum = scatter_rows(
        [dot(shrink_in, weights, CONTRACT_LAST).astype(BF) for weights in shrink_mine]
    )
    output = middle + output_sum + mine(shrink_bias)
    shrink_grad = row_owners(
        [dot(piece, shrink_in, CONTRACT_FIRST) for piece in low_out_pieces], rows, side
    )
    expand_grad = row_owners(
        [dot(piece, low_raised, CONTRACT_FIRST) for piece in expand_pieces], rows, side
    )
    unit_sums = jnp.stack(
        [
            jnp.sum(hidden_grad * hidden_normed, axis=0),
            jnp.sum(hidden_grad, axis=0),
            jnp.sum(raised_grad, axis=0),
        ]
    )

    scaled = second_grad * gain_half
    sums = pair_sum(jnp.stack([jnp.sum(scaled, axis=1), jnp.sum(scaled * second_normed, axis=1)]))
    middle_grad = out_grad_mine + second_scale * (
        scaled - (sums[0] / D)[:, None] - second_normed * (sums[1] / D)[:, None]
    )
    low_middle = middle_grad.astype(BF)
    low_middle = join_halves(side, low_middle, hop(low_middle, "t"))
    inner_grad = dot(full_combine, low_middle, (((0,), (1,)), ((), ())))
    scaled = inner_grad * inner_gain[:, None]
    sums = pair_sum(jnp.stack([jnp.sum(scaled, axis=0), jnp.sum(scaled * inner_normed, axis=0)]))
    mixture_grad = inner_scale * (scaled - sums[0:1] / D - inner_normed * (sums[1:2] / D))
    pull = to_owners(mixture_grad.astype(BF).reshape(SEQ, HDIM, rows))
    combine_term = dot(low_middle, combined_in, (((0,), (1,)), ((), ()))).astype(BF)
    combine_grad = lax.psum_scatter(
        combine_term, "seq", scatter_dimension=0, tiled=True
    ).astype(F32)

    low_triple, head_sums = retreat(
        order, kept, pull, mixture, logs, cosine, sine, growth, begin
    )
    first_grad = scatter_rows(
        [dot(low_triple, weights, CONTRACT_FIRST).astype(BF) for weights in project_pieces]
    )
    term = turn_halves(
        side,
        jnp.concatenate([dot(low_triple, piece, PLAIN) for piece in normed_pieces], axis=1),
        axis=1,
    ).astype(BF)
    moved = to_owners(jnp.transpose(term.reshape(3 * HDIM, SEQ, rows), (1, 0, 2)))
    project_grad = jnp.transpose(moved.reshape(SEQ, 3, HDIM, rows), (3, 1, 0, 2)).reshape(
        rows, 3, head_width
    ).astype(F32)
    normed_half = mine(first_normed)
    scaled = first_grad * mine(first_gain)
    sums = pair_sum(jnp.stack([jnp.sum(scaled, axis=1), jnp.sum(scaled * normed_half, axis=1)]))
    stream_grad = middle_grad + first_scale * (
        scaled - (sums[0] / D)[:, None] - normed_half * (sums[1] / D)[:, None]
    )

    early = seq_sum(
        jnp.stack(
            [
                jnp.sum(out_grad_mine, axis=0),
                jnp.sum(second_grad * second_normed, axis=0),
                jnp.sum(second_grad, axis=0),
                jnp.sum(middle_grad, axis=0),
                jnp.sum(inner_grad * inner_normed, axis=1),
                jnp.sum(inner_grad, axis=1),
            ]
        )
    )
    late = seq_sum(jnp.stack([jnp.sum(first_grad * normed_half, axis=0), jnp.sum(first_grad, axis=0)]))
    halves = jnp.concatenate([early[:4], late])
    halves = join_halves(side, halves, hop(halves, "t"))
    unit_sums = gather_zxy(unit_sums).reshape(SEQ, 3, width)[order]
    unit_sums = jnp.transpose(unit_sums, (1, 0, 2)).reshape(3, SEQ * width)
    head_sums = gather_zxy(head_sums.reshape(3, HDIM)).reshape(SEQ, 3, HDIM)[order]
    project_bias_grad = jnp.transpose(head_sums, (1, 0, 2)).reshape(3, head_width)
    return (
        join_halves(side, output, hop(output, "t")),
        join_halves(side, stream_grad, hop(stream_grad, "t")),
        project_grad,
        project_bias_grad,
        combine_grad,
        halves[3],
        expand_grad,
        unit_sums[2],
        shrink_grad,
        halves[0],
        halves[4],
        halves[5],
        early[4],
        early[5],
        halves[1],
        halves[2],
        unit_sums[0],
        unit_sums[1],
    )


def solution(mesh):
    plan = head_shards if fits_heads(mesh) else shards
    return jax.shard_map(
        plan,
        mesh=mesh,
        in_specs=(
            P("seq", None),
            P("seq"),
            P("seq", None, "tp"),
            P(None, "tp"),
            P("seq", "tp"),
            P(),
            P("seq", "tp"),
            P("tp"),
            P("seq", "tp"),
            P(),
            P(),
            P(),
            P("tp"),
            P("tp"),
            P(),
            P(),
            P("tp"),
            P("tp"),
            P("seq", None),
        ),
        out_specs=(
            P("seq", None),
            P("seq", None),
            P("seq", None, "tp"),
            P(None, "tp"),
            P("seq", "tp"),
            P(),
            P("seq", "tp"),
            P("tp"),
            P("seq", "tp"),
            P(),
            P(),
            P(),
            P("tp"),
            P("tp"),
            P(),
            P(),
            P("tp"),
            P("tp"),
        ),
        check_vma=False,
    )
```

```python
from functools import partial
import math

import jax
import jax.numpy as jnp
from jax import lax
from jax.experimental import pallas as pl
from jax.experimental.pallas import tpu as pltpu
from jax.sharding import PartitionSpec as P

D = 2048
HDIM = 64
FF = 8192
DOCS = 5
SCALE_BASE = 512


EPSILON = 1e-05
NEGATIVE = -1e30
CONTRACT_LAST = (((1,), (1,)), ((), ()))
CONTRACT_FIRST = (((0,), (0,)), ((), ()))


def doubled(values_in):
    return jnp.concatenate([values_in, values_in], axis=-1)


def tables(positions, center):
    half_dim = HDIM // 2
    column = jnp.arange(half_dim, dtype=jnp.float32)
    frequency = jnp.exp(column * (-2.0 * math.log(10000.0) / HDIM))
    base_ratio = (2.0 * column + 0.4 * HDIM) / (1.4 * HDIM)
    location = positions.astype(jnp.float32)
    phase_angle = location[:, None] * frequency[None, :]
    exponent = ((location - center) / SCALE_BASE)[:, None] * jnp.log(base_ratio)[None, :]
    return (
        doubled(jnp.cos(phase_angle)),
        doubled(jnp.sin(phase_angle)),
        doubled(jnp.exp(exponent)),
    )


def turn_pairs(values, cosine, sine_table):
    half_dim = values.shape[-1] // 2
    swapped = jnp.concatenate([-values[..., half_dim:], values[..., :half_dim]], axis=-1)
    return values * cosine[:, None, :] + swapped * sine_table[:, None, :]


def place_query(values, cosine, sine_table, growth):
    return turn_pairs(values, cosine, sine_table) * growth[:, None, :] * HDIM ** (-0.5)


def place_key(values, cosine, sine_table, growth):
    return turn_pairs(values, cosine, sine_table) / growth[:, None, :]


def norm_full(values, gain_vector, shift_vector):
    average = jnp.mean(values, axis=-1, keepdims=True)
    inv_scale = lax.rsqrt(
        jnp.mean(values * values, axis=-1, keepdims=True) - average * average + EPSILON
    )
    normed = (values - average) * inv_scale
    return (normed * gain_vector + shift_vector, normed, inv_scale)


def norm_full_back(incoming, normed, inv_scale, gain_vector):
    scaled_grad = incoming * gain_vector
    first_mean = jnp.mean(scaled_grad, axis=-1, keepdims=True)
    cross_mean = jnp.mean(scaled_grad * normed, axis=-1, keepdims=True)
    return inv_scale * (scaled_grad - first_mean - normed * cross_mean)


def split_sums(first_term, second_term):
    return lax.psum((first_term, second_term), "tp")


def norm_split(values, gain_vector, shift_vector, full_width):
    totals, squares = split_sums(
        jnp.sum(values, axis=-1, keepdims=True), jnp.sum(values * values, axis=-1, keepdims=True)
    )
    average = totals / full_width
    inv_scale = lax.rsqrt(squares / full_width - average * average + EPSILON)
    normed = (values - average) * inv_scale
    return (normed * gain_vector + shift_vector, normed, inv_scale)


def norm_split_back(incoming, normed, inv_scale, gain_vector, full_width):
    scaled_grad = incoming * gain_vector
    totals, crossed = split_sums(
        jnp.sum(scaled_grad, axis=-1, keepdims=True),
        jnp.sum(scaled_grad * normed, axis=-1, keepdims=True),
    )
    return inv_scale * (scaled_grad - totals / full_width - normed * (crossed / full_width))


def branch_total(values):
    return lax.psum(values, "tp")


def doc_of(token_rows, starts):
    return jnp.sum((token_rows[:, None] >= starts[None, 1:]).astype(jnp.int32), axis=1)


def keep_state(state_in):
    return state_in


def gelu_exact(values):
    return jax.nn.gelu(values, approximate=False)


def shards(
    stream,
    doc_ids,
    project,
    project_bias,
    combine,
    combine_bias,
    expand,
    expand_bias,
    shrink,
    shrink_bias,
    first_gain,
    first_bias,
    inner_gain,
    inner_bias,
    second_gain,
    second_bias,
    hidden_gain,
    hidden_bias,
    out_grad,
):
    local_count = stream.shape[0]
    head_width = project.shape[2]
    head_count = head_width // HDIM
    token_rows = lax.axis_index("seq") * local_count + jnp.arange(local_count, dtype=jnp.int32)
    center = lax.axis_size("seq") * local_count // 2
    member = (doc_ids[:, None] == jnp.arange(DOCS, dtype=jnp.int32)[None, :]).astype(jnp.int32)
    counts = lax.psum(jnp.sum(member, axis=0), "seq")
    starts = jnp.cumsum(counts) - counts
    positions = token_rows - jnp.sum(member * starts[None, :], axis=1)
    cosine, sine_table, growth = tables(positions, center)
    first_row = token_rows[0]
    last_row = token_rows[local_count - 1]
    first_doc = doc_ids[0]
    last_doc = doc_ids[local_count - 1]
    full_project, full_combine, full_expand, full_shrink = (
        lax.all_gather(project, "seq", axis=0, tiled=True),
        lax.all_gather(combine, "seq", axis=0, tiled=True),
        lax.all_gather(expand, "seq", axis=0, tiled=True),
        lax.all_gather(shrink, "seq", axis=0, tiled=True),
    )
    first_out, first_normed, first_scale = norm_full(stream, first_gain, first_bias)
    normed_in = first_out.astype(jnp.bfloat16)
    triple = (
        jnp.einsum("td,dch->tch", normed_in, full_project, preferred_element_type=jnp.float32)
        + project_bias[None]
    )
    head_shape = (local_count, head_count, HDIM)
    query_raw = triple[:, 0].reshape(head_shape)
    key_raw = triple[:, 1].reshape(head_shape)
    queries = place_query(query_raw, cosine, sine_table, growth).astype(jnp.bfloat16)
    keyed = place_key(key_raw, cosine, sine_table, growth).astype(jnp.bfloat16)
    valued = triple[:, 2].reshape(head_shape).astype(jnp.bfloat16)
    start_state = (
        jnp.full((head_count, local_count), NEGATIVE, jnp.float32),
        jnp.zeros((head_count, local_count), jnp.float32),
        jnp.zeros((head_count, local_count, HDIM), jnp.float32),
    )
    key_part = lax.all_gather(keyed.reshape(local_count, head_width), "seq", axis=0, tiled=True)
    value_part = lax.all_gather(valued.reshape(local_count, head_width), "seq", axis=0, tiled=True)
    piece_rows = key_part.shape[0]
    key_rows = jnp.arange(piece_rows, dtype=jnp.int32)
    key_docs = doc_of(key_rows, starts)
    skipped = (jnp.int32(0) > last_row) | (key_docs[piece_rows - 1] < first_doc)

    def attend_compute(state):
        running_max, running_sum, summed = state
        key_block = key_part.reshape(piece_rows, head_count, HDIM)
        value_block = value_part.reshape(piece_rows, head_count, HDIM)
        allowed = (
            (key_rows[None, :] <= token_rows[:, None]) & (key_docs[None, :] == doc_ids[:, None])
        )[None]
        scores = jnp.einsum("qhd,khd->hqk", queries, key_block, preferred_element_type=jnp.float32)
        scores = jnp.where(allowed, scores, NEGATIVE)
        newest = jnp.maximum(running_max, jnp.max(scores, axis=-1))
        weights_raw = jnp.where(allowed, jnp.exp(scores - newest[..., None]), 0.0)
        running_sum = jnp.sum(weights_raw, axis=-1)
        summed = jnp.einsum(
            "hqk,khd->hqd",
            weights_raw.astype(jnp.bfloat16),
            value_block,
            preferred_element_type=jnp.float32,
        )
        return (newest, running_sum, summed)

    running_max, running_sum, summed = lax.cond(skipped, keep_state, attend_compute, start_state)
    mixture = jnp.transpose(summed / running_sum[..., None], (1, 0, 2)).reshape(
        local_count, head_width
    )
    log_total = running_max + jnp.log(running_sum)
    inner_out, inner_normed, inner_scale = norm_split(mixture, inner_gain, inner_bias, D)
    combined_in = inner_out.astype(jnp.bfloat16)
    middle = (
        stream
        + branch_total(
            lax.dot_general(
                combined_in, full_combine, CONTRACT_LAST, preferred_element_type=jnp.float32
            )
        )
        + combine_bias
    )
    second_out, second_normed, second_scale = norm_full(middle, second_gain, second_bias)
    expand_in = second_out.astype(jnp.bfloat16)
    raised = jnp.dot(expand_in, full_expand, preferred_element_type=jnp.float32) + expand_bias
    active, gelu_back = jax.vjp(gelu_exact, raised)
    hidden_out, hidden_normed, hidden_scale = norm_split(active, hidden_gain, hidden_bias, FF)
    shrink_in = hidden_out.astype(jnp.bfloat16)
    output = (
        middle
        + branch_total(
            lax.dot_general(
                shrink_in, full_shrink, CONTRACT_LAST, preferred_element_type=jnp.float32
            )
        )
        + shrink_bias
    )
    back_project, back_combine, back_expand, back_shrink = (
        lax.all_gather(project, "seq", axis=0, tiled=True),
        lax.all_gather(combine, "seq", axis=0, tiled=True),
        lax.all_gather(expand, "seq", axis=0, tiled=True),
        lax.all_gather(shrink, "seq", axis=0, tiled=True),
    )
    shrink_bias_grad = jnp.sum(out_grad, axis=0)
    low_out = out_grad.astype(jnp.bfloat16)
    shrink_term = lax.dot_general(
        low_out, shrink_in, CONTRACT_FIRST, preferred_element_type=jnp.float32
    )
    hidden_grad = jnp.dot(low_out, back_shrink, preferred_element_type=jnp.float32)
    hidden_gain_grad = jnp.sum(hidden_grad * hidden_normed, axis=0)
    hidden_bias_grad = jnp.sum(hidden_grad, axis=0)
    active_grad = norm_split_back(hidden_grad, hidden_normed, hidden_scale, hidden_gain, FF)
    (raised_grad,) = gelu_back(active_grad)
    expand_bias_grad = jnp.sum(raised_grad, axis=0)
    low_raised = raised_grad.astype(jnp.bfloat16)
    expand_term = lax.dot_general(
        expand_in, low_raised, CONTRACT_FIRST, preferred_element_type=jnp.float32
    )
    second_grad = branch_total(
        lax.dot_general(low_raised, back_expand, CONTRACT_LAST, preferred_element_type=jnp.float32)
    )
    second_gain_grad = jnp.sum(second_grad * second_normed, axis=0)
    second_bias_grad = jnp.sum(second_grad, axis=0)
    middle_grad = out_grad + norm_full_back(second_grad, second_normed, second_scale, second_gain)
    combine_bias_grad = jnp.sum(middle_grad, axis=0)
    low_middle = middle_grad.astype(jnp.bfloat16)
    combine_term = lax.dot_general(
        low_middle, combined_in, CONTRACT_FIRST, preferred_element_type=jnp.float32
    )
    inner_grad = jnp.dot(low_middle, back_combine, preferred_element_type=jnp.float32)
    inner_gain_grad = jnp.sum(inner_grad * inner_normed, axis=0)
    inner_bias_grad = jnp.sum(inner_grad, axis=0)
    mixture_grad = norm_split_back(inner_grad, inner_normed, inner_scale, inner_gain, D)
    low_mixture = mixture_grad.astype(jnp.bfloat16)
    low_mixture3 = low_mixture.reshape(head_shape)
    delta = jnp.sum(low_mixture3.astype(jnp.float32) * mixture.reshape(head_shape), axis=-1)
    delta_heads = delta.T
    zero_heads = jnp.zeros(head_shape, jnp.float32)
    query_key_part = lax.all_gather(
        keyed.reshape(local_count, head_width), "seq", axis=0, tiled=True
    )
    query_value_part = lax.all_gather(
        valued.reshape(local_count, head_width), "seq", axis=0, tiled=True
    )
    query_piece_rows = query_key_part.shape[0]
    query_key_rows = jnp.arange(query_piece_rows, dtype=jnp.int32)
    query_key_docs = doc_of(query_key_rows, starts)
    skipped = (jnp.int32(0) > last_row) | (query_key_docs[query_piece_rows - 1] < first_doc)

    def query_compute(gathered):
        key_block = query_key_part.reshape(query_piece_rows, head_count, HDIM)
        value_block = query_value_part.reshape(query_piece_rows, head_count, HDIM)
        allowed = (
            (query_key_rows[None, :] <= token_rows[:, None])
            & (query_key_docs[None, :] == doc_ids[:, None])
        )[None]
        scores = jnp.einsum("qhd,khd->hqk", queries, key_block, preferred_element_type=jnp.float32)
        probability = jnp.where(allowed, jnp.exp(scores - log_total[..., None]), 0.0)
        pushes = jnp.einsum(
            "qhd,khd->hqk", low_mixture3, value_block, preferred_element_type=jnp.float32
        )
        dscore = (probability * (pushes - delta_heads[..., None])).astype(jnp.bfloat16)
        return jnp.einsum("hqk,khd->qhd", dscore, key_block, preferred_element_type=jnp.float32)

    query_grad3 = lax.cond(skipped, keep_state, query_compute, zero_heads)
    query_part = lax.all_gather(
        queries.astype(jnp.float32).reshape(local_count, head_width), "seq", axis=0, tiled=True
    )
    pull_part = lax.all_gather(low_mixture.astype(jnp.float32), "seq", axis=0, tiled=True)
    total_part = lax.all_gather(log_total.T, "seq", axis=0, tiled=True)
    delta_part = lax.all_gather(delta, "seq", axis=0, tiled=True)
    key_piece_rows = query_part.shape[0]
    query_rows = jnp.arange(key_piece_rows, dtype=jnp.int32)
    query_docs = doc_of(query_rows, starts)
    skipped = (query_rows[key_piece_rows - 1] < first_row) | (query_docs[0] > last_doc)

    def key_compute(state):
        query_block = query_part.astype(jnp.bfloat16).reshape(key_piece_rows, head_count, HDIM)
        pull_block = pull_part.astype(jnp.bfloat16).reshape(key_piece_rows, head_count, HDIM)
        allowed = (
            (token_rows[None, :] <= query_rows[:, None]) & (doc_ids[None, :] == query_docs[:, None])
        )[None]
        scores = jnp.einsum("qhd,khd->hqk", query_block, keyed, preferred_element_type=jnp.float32)
        probability = jnp.where(allowed, jnp.exp(scores - total_part.T[..., None]), 0.0)
        pushes = jnp.einsum("qhd,khd->hqk", pull_block, valued, preferred_element_type=jnp.float32)
        dscore = (probability * (pushes - delta_part.T[..., None])).astype(jnp.bfloat16)
        key_acc = jnp.einsum(
            "hqk,qhd->khd", dscore, query_block, preferred_element_type=jnp.float32
        )
        value_acc = jnp.einsum(
            "hqk,qhd->khd",
            probability.astype(jnp.bfloat16),
            pull_block,
            preferred_element_type=jnp.float32,
        )
        return (key_acc, value_acc)

    key_grad3, value_grad3 = lax.cond(skipped, keep_state, key_compute, (zero_heads, zero_heads))
    _, query_back = jax.vjp(
        partial(place_query, cosine=cosine, sine_table=sine_table, growth=growth), query_raw
    )
    _, key_back = jax.vjp(
        partial(place_key, cosine=cosine, sine_table=sine_table, growth=growth), key_raw
    )
    (query_grad,) = query_back(query_grad3)
    (key_grad,) = key_back(key_grad3)
    triple_grad = jnp.stack(
        [
            query_grad.reshape(local_count, head_width),
            key_grad.reshape(local_count, head_width),
            value_grad3.reshape(local_count, head_width),
        ],
        axis=1,
    )
    project_bias_grad = jnp.sum(triple_grad, axis=0)
    low_triple = triple_grad.astype(jnp.bfloat16)
    project_term = jnp.einsum(
        "td,tch->dch", normed_in, low_triple, preferred_element_type=jnp.float32
    )
    first_grad = branch_total(
        jnp.einsum("tch,dch->td", low_triple, back_project, preferred_element_type=jnp.float32)
    )
    first_gain_grad = jnp.sum(first_grad * first_normed, axis=0)
    first_bias_grad = jnp.sum(first_grad, axis=0)
    stream_grad = middle_grad + norm_full_back(first_grad, first_normed, first_scale, first_gain)
    project_grad, combine_grad, expand_grad, shrink_grad = (
        lax.psum_scatter(project_term, "seq", scatter_dimension=0, tiled=True),
        lax.psum_scatter(combine_term, "seq", scatter_dimension=0, tiled=True),
        lax.psum_scatter(expand_term, "seq", scatter_dimension=0, tiled=True),
        lax.psum_scatter(shrink_term, "seq", scatter_dimension=0, tiled=True),
    )
    (
        first_gain_grad,
        first_bias_grad,
        project_bias_grad,
        inner_gain_grad,
        inner_bias_grad,
        combine_bias_grad,
        second_gain_grad,
        second_bias_grad,
        expand_bias_grad,
        hidden_gain_grad,
        hidden_bias_grad,
        shrink_bias_grad,
    ) = lax.psum(
        (
            first_gain_grad,
            first_bias_grad,
            project_bias_grad,
            inner_gain_grad,
            inner_bias_grad,
            combine_bias_grad,
            second_gain_grad,
            second_bias_grad,
            expand_bias_grad,
            hidden_gain_grad,
            hidden_bias_grad,
            shrink_bias_grad,
        ),
        "seq",
    )
    return (
        output,
        stream_grad,
        project_grad,
        project_bias_grad,
        combine_grad,
        combine_bias_grad,
        expand_grad,
        expand_bias_grad,
        shrink_grad,
        shrink_bias_grad,
        first_gain_grad,
        first_bias_grad,
        inner_gain_grad,
        inner_bias_grad,
        second_gain_grad,
        second_bias_grad,
        hidden_gain_grad,
        hidden_bias_grad,
    )


BF = jnp.bfloat16
F32 = jnp.float32
GRID = (4, 2, 2)
SEQ = 16
ALIGNED = (((0,), (0,)), ((), ()))
PLAIN = (((1,), (0,)), ((), ()))
HOPS = {
    "x": [(i, i ^ 1) for i in range(SEQ)],
    "y": [(i, i ^ 2) for i in range(SEQ)],
    "xy": [(i, i ^ 3) for i in range(SEQ)],
    "z1": [(i, (i + 4) % SEQ) for i in range(SEQ)],
    "z2": [(i, (i + 8) % SEQ) for i in range(SEQ)],
    "z3": [(i, (i + 12) % SEQ) for i in range(SEQ)],
}
COLUMN = ("z1", "z2", "z3")


def fits_heads(mesh):
    return mesh.shape["seq"] == SEQ and mesh.shape["tp"] == 2


def hop(values, way):
    if way == "t":
        return lax.ppermute(values, "tp", [(0, 1), (1, 0)])
    return lax.ppermute(values, "seq", HOPS[way])


def after(first, *later):
    return lax.optimization_barrier((first,) + later)


def gather_along(values, way, axis):
    return jnp.stack([values, hop(values, way)], axis=axis)


def gather_column(own):
    return jnp.stack([own] + [hop(own, way) for way in COLUMN])


def gather_plane(column, midway=None):
    half = column.shape[2] // 2
    left = gather_along(column[:, :, :half], "x", 1)
    right = gather_along(column[:, :, half:], "y", 1)
    done = None
    if midway is not None:
        left, right, done = midway(left, right)
    mine = [gather_along(left, "y", 1), gather_along(right, "x", 2)]
    mine = [piece.reshape(-1, half) for piece in mine]
    if midway is not None:
        mine[0], mine[1], *done = after(mine[0], mine[1], *done)
    return mine + [hop(piece, "t") for piece in mine], done


def gather_small(values):
    return gather_along(gather_along(gather_column(values), "x", 1), "y", 1)


def add_low(first, second):
    return (first.astype(F32) + second.astype(F32)).astype(BF)


def fold(values, way, axis):
    near = lax.index_in_dim(values, 0, axis, keepdims=False)
    far = lax.index_in_dim(values, 1, axis, keepdims=False)
    return add_low(near, hop(far, way))


def scatter_pair(low, own, others):
    return [
        (dot(low, weights, own[0]) + hop(other, "t").astype(F32)).astype(BF)
        for weights, other in zip(own[1], others, strict=True)
    ]


def scatter_wide(pair):
    shape = GRID + (-1, pair[0].shape[1])
    return [fold(pair[0].reshape(shape), "y", 1), fold(pair[1].reshape(shape), "x", 2)]


def scatter_narrow(halves):
    return jnp.concatenate([fold(halves[0], "x", 1), fold(halves[1], "y", 1)], axis=2)


def scatter_plane(pair):
    return scatter_narrow(scatter_wide(pair))


def scatter_column(slabs):
    total = slabs[0].astype(F32)
    for i in range(1, 4):
        total = total + lax.optimization_barrier(hop(slabs[i], COLUMN[3 - i])).astype(F32)
    return total


def swap_by(flag, values, axis):
    return jnp.where(flag == 0, values, jnp.flip(values, axis))


def own_half(side, values, axis=-1):
    left, right = jnp.split(values, 2, axis=axis)
    return jnp.where(side == 0, left, right)


def join_halves(side, mine, other, axis=-1):
    return jnp.concatenate(
        [jnp.where(side == 0, mine, other), jnp.where(side == 0, other, mine)], axis=axis
    )


def turn_halves(side, values, axis=0):
    left, right = jnp.split(values, 2, axis=axis)
    return jnp.concatenate(
        [jnp.where(side == 0, left, right), jnp.where(side == 0, right, left)], axis=axis
    )


def token_sum(values):
    shape = values.shape
    values = (values + hop(values, "t")).reshape((shape[0],) + GRID + (-1,))
    moved = [jnp.flip(hop(values, "x"), 3), jnp.flip(hop(values, "y"), 2)]
    values = values + moved[0] + moved[1] + jnp.flip(hop(values, "xy"), (2, 3))
    moved = [jnp.roll(hop(values, COLUMN[i]), i + 1, 1) for i in range(3)]
    return (values + moved[0] + moved[1] + moved[2]).reshape(shape)


def seq_sum(values):
    values = values + hop(values, "x") + hop(values, "y") + hop(values, "xy")
    return values + hop(values, "z1") + hop(values, "z2") + hop(values, "z3")


def pair_sum(values):
    return values + hop(values, "t")


def dot(first, second, dims):
    return lax.dot_general(first, second, dims, preferred_element_type=F32)


BLOCK = 512
CHUNK = 256
KERNEL_BYTES = 48 * 1024 * 1024


def attend_kernel(
    order_ref, first_ref, second_ref, third_ref, fourth_ref, weights_ref, bias_ref,
    cosine_ref, sine_ref, growth_ref, begin_ref, kept_ref, mixture_ref, log_ref, wide,
):
    step = pl.program_id(0)
    part = first_ref.shape[1]
    rows = mixture_ref.shape[2]
    raw = bias_ref[...]
    for index, piece in enumerate((first_ref, second_ref, third_ref, fourth_ref)):
        raw = raw + dot(
            weights_ref[:, index * part : (index + 1) * part], piece[...], CONTRACT_LAST
        )
    for block in range(CHUNK // rows):
        place = order_ref[step * (CHUNK // rows) + block] * rows
        wide[:, pl.ds(pl.multiple_of(place, rows), rows)] = raw[:, block * rows : (block + 1) * rows]

    @pl.when(step == pl.num_programs(0) - 1)
    def _():
        attend_head(
            cosine_ref, sine_ref, growth_ref, begin_ref, kept_ref, mixture_ref, log_ref, wide
        )


def attend_head(cosine_ref, sine_ref, growth_ref, begin_ref, kept_ref, mixture_ref, log_ref, wide):
    tokens = wide.shape[1]
    half = HDIM // 2
    rows = tokens // SEQ
    cosine, sine, growth = cosine_ref[...], sine_ref[...], growth_ref[...]
    first, second = wide[0:half, :], wide[half:HDIM, :]
    scaled = growth * HDIM ** (-0.5)
    kept_ref[0:half, :] = ((first * cosine - second * sine) * scaled).astype(BF)
    kept_ref[half:HDIM, :] = ((second * cosine + first * sine) * scaled).astype(BF)
    first, second = wide[HDIM : HDIM + half, :], wide[HDIM + half : 2 * HDIM, :]
    kept_ref[HDIM : HDIM + half, :] = ((first * cosine - second * sine) / growth).astype(BF)
    kept_ref[HDIM + half : 2 * HDIM, :] = ((second * cosine + first * sine) / growth).astype(BF)
    kept_ref[2 * HDIM :, :] = wide[2 * HDIM :, :].astype(BF)
    key_rows = lax.broadcasted_iota(jnp.int32, (BLOCK, BLOCK), 0)
    query_rows = lax.broadcasted_iota(jnp.int32, (BLOCK, BLOCK), 1)
    for i in range(tokens // BLOCK):
        columns = slice(i * BLOCK, (i + 1) * BLOCK)
        queries = kept_ref[0:HDIM, columns]
        begin = begin_ref[:, columns]
        largest = jnp.full((1, BLOCK), NEGATIVE, F32)
        total = jnp.zeros((1, BLOCK), F32)
        summed = jnp.zeros((HDIM, BLOCK), F32)
        for j in range(i, -1, -1):
            place = slice(j * BLOCK, (j + 1) * BLOCK)
            scores = dot(kept_ref[HDIM : 2 * HDIM, place], queries, ALIGNED)
            allowed = key_rows + j * BLOCK >= begin
            if j == i:
                allowed = allowed & (key_rows <= query_rows)
            scores = jnp.where(allowed, scores, NEGATIVE)
            newest = jnp.maximum(largest, jnp.max(scores, axis=0, keepdims=True))
            weights = jnp.exp(scores - newest)
            shrunk = jnp.exp(largest - newest)
            total = total * shrunk + jnp.sum(weights, axis=0, keepdims=True)
            summed = summed * shrunk + dot(
                kept_ref[2 * HDIM :, place], weights.astype(BF), PLAIN
            )
            largest = newest
        mixture = summed / total
        for block in range(BLOCK // rows):
            mixture_ref[i * (BLOCK // rows) + block] = mixture[:, block * rows : (block + 1) * rows]
        log_ref[:, columns] = largest + jnp.log(total)


def retreat_kernel(
    order_ref, kept_ref, pull_ref, mixture_ref, log_ref, cosine_ref, sine_ref, growth_ref, begin_ref,
    low_ref, bias_ref, pulls, delta, query_sum, key_sum, value_sum,
):
    tokens = kept_ref.shape[1]
    half = HDIM // 2
    rows = tokens // SEQ
    for block in range(SEQ):
        place = slice(block * rows, (block + 1) * rows)
        pulls[:, place] = pull_ref[block]
        delta[:, place] = jnp.sum(
            pull_ref[block].astype(F32) * mixture_ref[block], axis=0, keepdims=True
        )
    key_rows = lax.broadcasted_iota(jnp.int32, (BLOCK, BLOCK), 0)
    query_rows = lax.broadcasted_iota(jnp.int32, (BLOCK, BLOCK), 1)
    for i in range(tokens // BLOCK):
        columns = slice(i * BLOCK, (i + 1) * BLOCK)
        queries = kept_ref[0:HDIM, columns]
        pull = pulls[:, columns]
        begin = begin_ref[:, columns]
        logs = log_ref[:, columns]
        offset = delta[:, columns]
        query_part = jnp.zeros((HDIM, BLOCK), F32)
        for j in range(i + 1):
            place = slice(j * BLOCK, (j + 1) * BLOCK)
            keys = kept_ref[HDIM : 2 * HDIM, place]
            scores = dot(keys, queries, ALIGNED)
            allowed = key_rows + j * BLOCK >= begin
            if j == i:
                allowed = allowed & (key_rows <= query_rows)
            chance = jnp.where(allowed, jnp.exp(scores - logs), 0.0)
            pushes = dot(kept_ref[2 * HDIM :, place], pull, ALIGNED)
            dscore = (chance * (pushes - offset)).astype(BF)
            query_part = query_part + dot(keys, dscore, PLAIN)
            key_part = dot(queries, dscore, CONTRACT_LAST)
            value_part = dot(pull, chance.astype(BF), CONTRACT_LAST)
            if j == i:
                key_sum[:, place] = key_part
                value_sum[:, place] = value_part
            else:
                key_sum[:, place] += key_part
                value_sum[:, place] += value_part
        query_sum[:, columns] = query_part
    cosine, sine, growth = cosine_ref[...], sine_ref[...], growth_ref[...]
    scaled = growth * HDIM ** (-0.5)
    first, second = query_sum[0:half, :] * scaled, query_sum[half:, :] * scaled
    pieces = [first * cosine + second * sine, second * cosine - first * sine]
    first, second = key_sum[0:half, :] / growth, key_sum[half:, :] / growth
    pieces += [first * cosine + second * sine, second * cosine - first * sine]
    pieces += [value_sum[0:half, :], value_sum[half:, :]]
    for index, piece in enumerate(pieces):
        lanes = slice(index * half, (index + 1) * half)
        bias_ref[lanes, :] = jnp.sum(piece, axis=1, keepdims=True)
        low = piece.astype(BF)
        for block in range(SEQ):
            place = pl.ds(pl.multiple_of(order_ref[block] * rows, rows), rows)
            low_ref[lanes, place] = low[:, block * rows : (block + 1) * rows]


def whole(count):
    return [pl.BlockSpec(memory_space=pltpu.VMEM) for _ in range(count)]


def attend(order, pieces, weights, bias, cosine, sine, growth, begin):
    tokens, part = pieces[0].shape
    depth = weights.shape[1]
    table = still((HDIM // 2, tokens))
    return pl.pallas_call(
        attend_kernel,
        grid_spec=pltpu.PrefetchScalarGridSpec(
            num_scalar_prefetch=1,
            grid=(tokens // CHUNK,),
            in_specs=[pl.BlockSpec((CHUNK, part), lambda i, order: (i, 0)) for _ in pieces]
            + [still((3 * HDIM, depth)), still((3 * HDIM, 1)), table, table, table, still((1, tokens))],
            out_specs=(
                still((3 * HDIM, tokens)),
                still((SEQ, HDIM, tokens // SEQ)),
                still((1, tokens)),
            ),
            scratch_shapes=[pltpu.VMEM((3 * HDIM, tokens), F32)],
        ),
        out_shape=(
            jax.ShapeDtypeStruct((3 * HDIM, tokens), BF),
            jax.ShapeDtypeStruct((SEQ, HDIM, tokens // SEQ), F32),
            jax.ShapeDtypeStruct((1, tokens), F32),
        ),
        compiler_params=pltpu.CompilerParams(vmem_limit_bytes=KERNEL_BYTES),
        cost_estimate=pl.CostEstimate(
            flops=2 * tokens * tokens * HDIM, bytes_accessed=2 * tokens * depth,
            transcendentals=tokens * tokens // 2,
        ),
    )(order, *pieces, weights, bias, cosine, sine, growth, begin)


def retreat(order, kept, pull, mixture, logs, cosine, sine, growth, begin):
    tokens = kept.shape[1]
    return pl.pallas_call(
        retreat_kernel,
        out_shape=(
            jax.ShapeDtypeStruct((3 * HDIM, tokens), BF),
            jax.ShapeDtypeStruct((3 * HDIM, 1), F32),
        ),
        in_specs=[pl.BlockSpec(memory_space=pltpu.SMEM)] + whole(8),
        out_specs=tuple(whole(2)),
        scratch_shapes=[
            pltpu.VMEM((HDIM, tokens), BF),
            pltpu.VMEM((1, tokens), F32),
            pltpu.VMEM((HDIM, tokens), F32),
            pltpu.VMEM((HDIM, tokens), F32),
            pltpu.VMEM((HDIM, tokens), F32),
        ],
        compiler_params=pltpu.CompilerParams(vmem_limit_bytes=KERNEL_BYTES),
        cost_estimate=pl.CostEstimate(
            flops=5 * tokens * tokens * HDIM, bytes_accessed=8 * 192 * tokens,
            transcendentals=tokens * tokens // 2,
        ),
    )(order, kept, pull, mixture, logs, cosine, sine, growth, begin)


def enter_kernel(
    first_ref, second_ref, third_ref, fourth_ref, grad_ref, expand_ref, shift_ref, gain_ref,
    active_ref, slope_ref, stats_ref,
):
    part = first_ref.shape[1]
    raised = shift_ref[...]
    for index, piece in enumerate((first_ref, second_ref, third_ref, fourth_ref)):
        raised = raised + dot(piece[...], expand_ref[index * part : (index + 1) * part, :], PLAIN)
    chance = 0.5 * (1.0 + lax.erf(raised * math.sqrt(0.5)))
    active = raised * chance
    active_ref[...] = active
    slope_ref[...] = chance + raised * jnp.exp(raised * raised * -0.5) * (1.0 / math.sqrt(2.0 * math.pi))
    scaled = grad_ref[...] * gain_ref[...]
    lane = lax.broadcasted_iota(jnp.int32, (CHUNK, 128), 1)
    columns = jnp.zeros((CHUNK, 128), F32)
    for index, values in enumerate((active, active * active, scaled, scaled * active)):
        columns = jnp.where(lane == index, jnp.sum(values, axis=1, keepdims=True), columns)
    stats_ref[...] = columns.T[0:8, :]


def leave_kernel(
    active_ref, slope_ref, grad_ref, stats_ref, expand_ref, gain_ref, shift_ref,
    shrunk_ref, low_ref, first_ref, second_ref, sums_ref,
):
    @pl.when(pl.program_id(0) == 0)
    def _():
        sums_ref[...] = jnp.zeros_like(sums_ref)

    columns = jnp.concatenate([stats_ref[...], jnp.zeros((120, CHUNK), F32)], axis=0).T
    average, scale, grad_mean, cross_mean = (columns[:, i : i + 1] for i in range(4))
    hidden_grad = grad_ref[...]
    normed = (active_ref[...] - average) * scale
    shrunk_ref[...] = (normed * gain_ref[...] + shift_ref[...]).astype(BF)
    raised_grad = (
        scale * (hidden_grad * gain_ref[...] - grad_mean - normed * cross_mean) * slope_ref[...]
    )
    low = raised_grad.astype(BF)
    low_ref[...] = low
    sums_ref[0:1, :] += jnp.sum(hidden_grad * normed, axis=0, keepdims=True)
    sums_ref[1:2, :] += jnp.sum(hidden_grad, axis=0, keepdims=True)
    sums_ref[2:3, :] += jnp.sum(raised_grad, axis=0, keepdims=True)
    part = first_ref.shape[1]
    for index, out_ref in enumerate((first_ref, second_ref)):
        out_ref[...] = dot(
            low, expand_ref[index * part : (index + 1) * part, :], CONTRACT_LAST
        ).astype(BF)


def still(shape):
    return pl.BlockSpec(shape, lambda *_: (0,) * len(shape))


def enter(pieces, grad, expand_mine, shift, gain):
    tokens, part = pieces[0].shape
    depth, units = expand_mine.shape
    block = pl.BlockSpec((CHUNK, units), lambda i: (i, 0))
    wide = jax.ShapeDtypeStruct((tokens, units), F32)
    return pl.pallas_call(
        enter_kernel,
        grid=(tokens // CHUNK,),
        in_specs=[pl.BlockSpec((CHUNK, part), lambda i: (i, 0)) for _ in pieces]
        + [block, still((depth, units)), still((1, units)), still((1, units))],
        out_specs=(block, block, pl.BlockSpec((8, CHUNK), lambda i: (0, i))),
        out_shape=(wide, wide, jax.ShapeDtypeStruct((8, tokens), F32)),
        compiler_params=pltpu.CompilerParams(vmem_limit_bytes=KERNEL_BYTES),
        cost_estimate=pl.CostEstimate(
            flops=2 * tokens * depth * units, bytes_accessed=6 * tokens * depth, transcendentals=0
        ),
    )(*pieces, grad, expand_mine, shift, gain)


def leave(active, slope, grad, stats, expand_other, gain, shift):
    tokens, units = active.shape
    depth = expand_other.shape[0]
    block = pl.BlockSpec((CHUNK, units), lambda i: (i, 0))
    piece = pl.BlockSpec((CHUNK, depth // 2), lambda i: (i, 0))
    low = jax.ShapeDtypeStruct((tokens, units), BF)
    partial_sum = jax.ShapeDtypeStruct((tokens, depth // 2), BF)
    return pl.pallas_call(
        leave_kernel,
        grid=(tokens // CHUNK,),
        in_specs=[block, block, block, pl.BlockSpec((8, CHUNK), lambda i: (0, i))]
        + [still((depth, units)), still((1, units)), still((1, units))],
        out_specs=(block, block, piece, piece, still((8, units))),
        out_shape=(low, low) + (partial_sum,) * 2 + (jax.ShapeDtypeStruct((8, units), F32),),
        compiler_params=pltpu.CompilerParams(vmem_limit_bytes=KERNEL_BYTES),
        cost_estimate=pl.CostEstimate(
            flops=2 * tokens * depth * units, bytes_accessed=6 * tokens * depth, transcendentals=0
        ),
    )(active, slope, grad, stats, expand_other, gain, shift)


def to_owners(values):
    return lax.all_to_all(values, "seq", split_axis=0, concat_axis=0, tiled=True)


def by_owner(weights, rows):
    return jnp.transpose(weights.reshape(rows, SEQ, -1), (1, 0, 2))


def columns_of(moved, side):
    return turn_halves(side, moved.reshape(-1, moved.shape[2]))


def by_row_owner(pieces, side):
    full = turn_halves(side, jnp.concatenate(pieces, axis=0))
    return full.reshape(SEQ, -1, full.shape[1])


def rows_of(moved):
    return jnp.transpose(moved, (1, 0, 2)).reshape(moved.shape[1], -1).astype(F32)


def head_shards(
    stream,
    doc_ids,
    project,
    project_bias,
    combine,
    combine_bias,
    expand,
    expand_bias,
    shrink,
    shrink_bias,
    first_gain,
    first_bias,
    inner_gain,
    inner_bias,
    second_gain,
    second_bias,
    hidden_gain,
    hidden_bias,
    out_grad,
):
    rows = stream.shape[0]
    tokens = SEQ * rows
    head_width = project.shape[2]
    width = expand.shape[1] // SEQ
    spot = lax.axis_index("seq")
    side = lax.axis_index("tp")
    spot_z, spot_y, spot_x = spot // 4, (spot // 2) % 2, spot % 2
    blocks = jnp.arange(SEQ, dtype=jnp.int32)
    order = (
        ((spot_z - blocks // 4) % 4) * 4 + (spot_y ^ ((blocks // 2) % 2)) * 2 + (spot_x ^ (blocks % 2))
    )

    def mine(values, axis=-1):
        return own_half(side, values, axis)

    def my_units(vector, size):
        return lax.dynamic_slice_in_dim(vector, spot * size, size, axis=-1)

    first_out, first_normed, first_scale = norm_full(stream, first_gain, first_bias)
    normed_column = gather_column(mine(first_out.astype(BF)))
    docs_near = gather_small(doc_ids[None, :]).reshape(SEQ, rows)
    full_combine = lax.all_gather(combine, "seq", axis=0, tiled=True)
    out_grad_mine = mine(out_grad)
    low_out = lax.all_gather(out_grad_mine.astype(BF), "seq", axis=0, tiled=True)
    normed_column, project_own = after(
        normed_column,
        jnp.transpose(project.reshape(rows, 3, SEQ, HDIM), (2, 1, 3, 0)).reshape(
            SEQ, 3 * HDIM, rows
        ),
    )
    normed_pieces, _ = gather_plane(normed_column)
    project_moved = to_owners(project_own)
    project_mine = turn_halves(
        side, jnp.transpose(project_moved, (1, 0, 2)).reshape(3 * HDIM, tokens), axis=1
    )
    project_pieces = jnp.split(project_mine, 4, axis=1)

    docs = docs_near[order].reshape(tokens)
    member = (docs[:, None] == jnp.arange(DOCS, dtype=jnp.int32)[None, :]).astype(jnp.int32)
    counts = jnp.sum(member, axis=0)
    starts = jnp.cumsum(counts) - counts
    begin = jnp.sum(member * starts[None, :], axis=1)
    positions = jnp.arange(tokens, dtype=jnp.int32) - begin
    column = jnp.arange(HDIM // 2, dtype=F32)
    frequency = jnp.exp(column * (-2.0 * math.log(10000.0) / HDIM))
    base_ratio = (2.0 * column + 0.4 * HDIM) / (1.4 * HDIM)
    location = positions.astype(F32)
    phase_angle = frequency[:, None] * location[None, :]
    cosine, sine = jnp.cos(phase_angle), jnp.sin(phase_angle)
    growth = jnp.exp(
        jnp.log(base_ratio)[:, None] * ((location - tokens // 2) / SCALE_BASE)[None, :]
    )
    begin = begin[None, :]

    head_bias = my_units(project_bias, HDIM).reshape(3 * HDIM, 1)
    kept, mixture, logs = attend(
        order, normed_pieces, project_mine, head_bias, cosine, sine, growth, begin
    )

    spread = to_owners(mixture).reshape(head_width, rows)
    sums = pair_sum(jnp.stack([jnp.sum(spread, axis=0), jnp.sum(spread * spread, axis=0)]))
    average = sums[0:1] / D
    inner_scale = lax.rsqrt(sums[1:2] / D - average * average + EPSILON)
    inner_normed = (spread - average) * inner_scale
    combined_in = (inner_normed * inner_gain[:, None] + inner_bias[:, None]).astype(BF)
    branch = dot(combined_in, full_combine, (((0,), (1,)), ((), ())))
    left, right = jnp.split(branch, 2, axis=1)
    branch = jnp.where(side == 0, left, right) + hop(jnp.where(side == 0, right, left), "t")
    middle = mine(stream) + branch + mine(combine_bias)
    sums = pair_sum(jnp.stack([jnp.sum(middle, axis=1), jnp.sum(middle * middle, axis=1)]))
    average = (sums[0] / D)[:, None]
    second_scale = lax.rsqrt((sums[1] / D)[:, None] - average * average + EPSILON)
    second_normed = (middle - average) * second_scale
    gain_half, bias_half = mine(second_gain), mine(second_bias)
    expand_column = gather_column((second_normed * gain_half + bias_half).astype(BF))
    expand_column, expand_own = after(expand_column, by_owner(expand, rows))
    expand_moved = to_owners(expand_own)

    def pull_back(left, right):
        left, right, units, shrink_own, near = after(
            left, right, expand_moved, by_owner(shrink, rows), low_out
        )
        shrink_mine = columns_of(to_owners(shrink_own), side)
        low = [near, hop(near, "t")]
        grad = sum(
            dot(piece, part, PLAIN)
            for piece, part in zip(low, jnp.split(shrink_mine, 2, axis=0), strict=True)
        )
        grad = grad.reshape(SEQ, rows, width)[order].reshape(tokens, width)
        return left, right, (low[0], low[1], grad, shrink_mine, columns_of(units, side))

    expand_pieces, midway = gather_plane(expand_column, pull_back)
    low_out, (hidden_grad, shrink_mine, expand_mine) = midway[:2], midway[2:]

    unit_gain, unit_bias = my_units(hidden_gain, width)[None, :], my_units(hidden_bias, width)[None, :]
    active, slope, sums = enter(
        expand_pieces, hidden_grad, expand_mine, my_units(expand_bias, width)[None, :], unit_gain
    )
    sums, combined_late = after(token_sum(sums[0:4]), combined_in.T)
    full_combined = lax.all_gather(combined_late, "seq", axis=0, tiled=True)
    average = sums[0:1] / FF
    hidden_scale = lax.rsqrt(sums[1:2] / FF - average * average + EPSILON)
    grad_mean = sums[2:3] / FF
    cross_mean = hidden_scale * (sums[3:4] / FF - average * grad_mean)
    stats = jnp.concatenate(
        [average, hidden_scale, grad_mean, cross_mean, jnp.zeros((4, tokens), F32)]
    )
    expand_parts = jnp.split(expand_mine, 4, axis=0)
    left = leave(
        active, slope, hidden_grad, stats, expand_mine[expand_mine.shape[0] // 2 :], unit_gain, unit_bias
    )
    pair, shrink_in, low_raised = after(
        scatter_pair(left[1], (CONTRACT_LAST, expand_parts[:2]), left[2:4]), left[0], left[1]
    )
    shrink_far = shrink_in.reshape(SEQ, rows, width)[order].reshape(tokens, width)
    shrink_term = by_row_owner(
        [dot(piece, shrink_far, CONTRACT_FIRST).astype(BF) for piece in low_out], side
    )
    slabs, shrink_moved = after(scatter_plane(pair), to_owners(shrink_term))
    shrink_grad = rows_of(shrink_moved)
    second_grad = scatter_column(slabs)
    expand_term = by_row_owner(
        [dot(piece, low_raised, CONTRACT_FIRST).astype(BF) for piece in expand_pieces], side
    )
    shrink_parts = jnp.split(shrink_mine, 4, axis=0)
    others = [dot(shrink_in, weights, CONTRACT_LAST).astype(BF) for weights in shrink_parts[2:]]
    output_pair = scatter_pair(shrink_in, (CONTRACT_LAST, shrink_parts[:2]), others)
    second_grad, expand_term, output_pair = after(second_grad, expand_term, output_pair)
    expand_moved = to_owners(expand_term)
    output_halves = scatter_wide(output_pair)

    scaled = second_grad * gain_half
    sums = pair_sum(jnp.stack([jnp.sum(scaled, axis=1), jnp.sum(scaled * second_normed, axis=1)]))
    middle_grad = out_grad_mine + second_scale * (
        scaled - (sums[0] / D)[:, None] - second_normed * (sums[1] / D)[:, None]
    )
    low_middle = middle_grad.astype(BF)
    low_middle = join_halves(side, low_middle, hop(low_middle, "t"))
    inner_grad = dot(full_combine, low_middle, (((0,), (1,)), ((), ())))
    scaled = inner_grad * inner_gain[:, None]
    sums = pair_sum(jnp.stack([jnp.sum(scaled, axis=0), jnp.sum(scaled * inner_normed, axis=0)]))
    mixture_grad = inner_scale * (scaled - sums[0:1] / D - inner_normed * (sums[1:2] / D))
    mixture_grad, expand_moved, output_halves, full_combined = after(
        mixture_grad.astype(BF).reshape(SEQ, HDIM, rows), expand_moved, output_halves, full_combined
    )
    expand_grad = rows_of(expand_moved)
    pull, low_middle, output_slabs = after(
        to_owners(mixture_grad), low_middle, scatter_narrow(output_halves)
    )
    output = middle + scatter_column(output_slabs) + mine(shrink_bias)
    moved = to_owners(by_owner(low_middle, rows))

    low_triple, head_sums = retreat(
        order, kept, pull, mixture, logs, cosine, sine, growth, begin
    )
    others = [dot(low_triple, weights, CONTRACT_FIRST).astype(BF) for weights in project_pieces[2:]]
    others, moved, output = after(others, moved, output)
    combine_grad = dot(moved.reshape(tokens, -1), full_combined, CONTRACT_FIRST)
    pair = scatter_pair(low_triple, (CONTRACT_FIRST, project_pieces[:2]), others)
    term = turn_halves(
        side,
        jnp.concatenate(
            [dot(low_triple, piece, PLAIN).astype(BF) for piece in normed_pieces], axis=1
        ),
        axis=1,
    )
    pair[0], term = after(pair[0], term)
    moved = to_owners(jnp.transpose(term.reshape(3 * HDIM, SEQ, rows), (1, 0, 2)))
    slabs, moved = after(scatter_plane(pair), moved)
    first_grad = scatter_column(slabs)
    project_grad = jnp.transpose(moved.reshape(SEQ, 3, HDIM, rows), (3, 1, 0, 2)).reshape(
        rows, 3, head_width
    ).astype(F32)
    normed_half = mine(first_normed)
    scaled = first_grad * mine(first_gain)
    sums = pair_sum(jnp.stack([jnp.sum(scaled, axis=1), jnp.sum(scaled * normed_half, axis=1)]))
    stream_grad = middle_grad + first_scale * (
        scaled - (sums[0] / D)[:, None] - normed_half * (sums[1] / D)[:, None]
    )

    unit_sums = lax.dynamic_update_slice(
        jnp.zeros((3, SEQ * width), F32), left[4][0:3], (0, spot * width)
    )
    head_sums = lax.dynamic_update_slice(
        jnp.zeros((3, head_width), F32), head_sums.reshape(3, HDIM), (0, spot * HDIM)
    )
    early = [
        jnp.sum(out_grad_mine, axis=0),
        jnp.sum(second_grad * second_normed, axis=0),
        jnp.sum(second_grad, axis=0),
        jnp.sum(middle_grad, axis=0),
        jnp.sum(inner_grad * inner_normed, axis=1),
        jnp.sum(inner_grad, axis=1),
    ]
    early = seq_sum(
        jnp.concatenate([jnp.stack(early), head_sums, unit_sums.reshape(-1, head_width)])
    )
    late = seq_sum(jnp.stack([jnp.sum(first_grad * normed_half, axis=0), jnp.sum(first_grad, axis=0)]))
    halves = join_halves(side, early[:4], hop(early[:4], "t"))
    late = join_halves(side, late, hop(late, "t"))
    project_bias_grad = early[6:9]
    unit_sums = early[9:].reshape(3, SEQ * width)
    return (
        join_halves(side, output, hop(output, "t")),
        join_halves(side, stream_grad, hop(stream_grad, "t")),
        project_grad,
        project_bias_grad,
        combine_grad,
        halves[3],
        expand_grad,
        unit_sums[2],
        shrink_grad,
        halves[0],
        late[0],
        late[1],
        early[4],
        early[5],
        halves[1],
        halves[2],
        unit_sums[0],
        unit_sums[1],
    )


def solution(mesh):
    plan = head_shards if fits_heads(mesh) else shards
    return jax.shard_map(
        plan,
        mesh=mesh,
        in_specs=(
            P("seq", None),
            P("seq"),
            P("seq", None, "tp"),
            P(None, "tp"),
            P("seq", "tp"),
            P(),
            P("seq", "tp"),
            P("tp"),
            P("seq", "tp"),
            P(),
            P(),
            P(),
            P("tp"),
            P("tp"),
            P(),
            P(),
            P("tp"),
            P("tp"),
            P("seq", None),
        ),
        out_specs=(
            P("seq", None),
            P("seq", None),
            P("seq", None, "tp"),
            P(None, "tp"),
            P("seq", "tp"),
            P(),
            P("seq", "tp"),
            P("tp"),
            P("seq", "tp"),
            P(),
            P(),
            P(),
            P("tp"),
            P("tp"),
            P(),
            P(),
            P("tp"),
            P("tp"),
        ),
        check_vma=False,
    )
```

```python
from functools import partial
import math

import jax
import jax.numpy as jnp
from jax import lax
from jax.experimental import pallas as pl
from jax.experimental.pallas import tpu as pltpu
from jax.sharding import PartitionSpec as P

D = 2048
HDIM = 64
FF = 8192
DOCS = 5
SCALE_BASE = 512


EPSILON = 1e-05
NEGATIVE = -1e30
CONTRACT_LAST = (((1,), (1,)), ((), ()))
CONTRACT_FIRST = (((0,), (0,)), ((), ()))


def doubled(values_in):
    return jnp.concatenate([values_in, values_in], axis=-1)


def tables(positions, center):
    half_dim = HDIM // 2
    column = jnp.arange(half_dim, dtype=jnp.float32)
    frequency = jnp.exp(column * (-2.0 * math.log(10000.0) / HDIM))
    base_ratio = (2.0 * column + 0.4 * HDIM) / (1.4 * HDIM)
    location = positions.astype(jnp.float32)
    phase_angle = location[:, None] * frequency[None, :]
    exponent = ((location - center) / SCALE_BASE)[:, None] * jnp.log(base_ratio)[None, :]
    return (
        doubled(jnp.cos(phase_angle)),
        doubled(jnp.sin(phase_angle)),
        doubled(jnp.exp(exponent)),
    )


def turn_pairs(values, cosine, sine_table):
    half_dim = values.shape[-1] // 2
    swapped = jnp.concatenate([-values[..., half_dim:], values[..., :half_dim]], axis=-1)
    return values * cosine[:, None, :] + swapped * sine_table[:, None, :]


def place_query(values, cosine, sine_table, growth):
    return turn_pairs(values, cosine, sine_table) * growth[:, None, :] * HDIM ** (-0.5)


def place_key(values, cosine, sine_table, growth):
    return turn_pairs(values, cosine, sine_table) / growth[:, None, :]


def norm_full(values, gain_vector, shift_vector):
    average = jnp.mean(values, axis=-1, keepdims=True)
    inv_scale = lax.rsqrt(
        jnp.mean(values * values, axis=-1, keepdims=True) - average * average + EPSILON
    )
    normed = (values - average) * inv_scale
    return (normed * gain_vector + shift_vector, normed, inv_scale)


def norm_full_back(incoming, normed, inv_scale, gain_vector):
    scaled_grad = incoming * gain_vector
    first_mean = jnp.mean(scaled_grad, axis=-1, keepdims=True)
    cross_mean = jnp.mean(scaled_grad * normed, axis=-1, keepdims=True)
    return inv_scale * (scaled_grad - first_mean - normed * cross_mean)


def split_sums(first_term, second_term):
    return lax.psum((first_term, second_term), "tp")


def norm_split(values, gain_vector, shift_vector, full_width):
    totals, squares = split_sums(
        jnp.sum(values, axis=-1, keepdims=True), jnp.sum(values * values, axis=-1, keepdims=True)
    )
    average = totals / full_width
    inv_scale = lax.rsqrt(squares / full_width - average * average + EPSILON)
    normed = (values - average) * inv_scale
    return (normed * gain_vector + shift_vector, normed, inv_scale)


def norm_split_back(incoming, normed, inv_scale, gain_vector, full_width):
    scaled_grad = incoming * gain_vector
    totals, crossed = split_sums(
        jnp.sum(scaled_grad, axis=-1, keepdims=True),
        jnp.sum(scaled_grad * normed, axis=-1, keepdims=True),
    )
    return inv_scale * (scaled_grad - totals / full_width - normed * (crossed / full_width))


def branch_total(values):
    return lax.psum(values, "tp")


def doc_of(token_rows, starts):
    return jnp.sum((token_rows[:, None] >= starts[None, 1:]).astype(jnp.int32), axis=1)


def keep_state(state_in):
    return state_in


def gelu_exact(values):
    return jax.nn.gelu(values, approximate=False)


def shards(
    stream,
    doc_ids,
    project,
    project_bias,
    combine,
    combine_bias,
    expand,
    expand_bias,
    shrink,
    shrink_bias,
    first_gain,
    first_bias,
    inner_gain,
    inner_bias,
    second_gain,
    second_bias,
    hidden_gain,
    hidden_bias,
    out_grad,
):
    local_count = stream.shape[0]
    head_width = project.shape[2]
    head_count = head_width // HDIM
    token_rows = lax.axis_index("seq") * local_count + jnp.arange(local_count, dtype=jnp.int32)
    center = lax.axis_size("seq") * local_count // 2
    member = (doc_ids[:, None] == jnp.arange(DOCS, dtype=jnp.int32)[None, :]).astype(jnp.int32)
    counts = lax.psum(jnp.sum(member, axis=0), "seq")
    starts = jnp.cumsum(counts) - counts
    positions = token_rows - jnp.sum(member * starts[None, :], axis=1)
    cosine, sine_table, growth = tables(positions, center)
    first_row = token_rows[0]
    last_row = token_rows[local_count - 1]
    first_doc = doc_ids[0]
    last_doc = doc_ids[local_count - 1]
    full_project, full_combine, full_expand, full_shrink = (
        lax.all_gather(project, "seq", axis=0, tiled=True),
        lax.all_gather(combine, "seq", axis=0, tiled=True),
        lax.all_gather(expand, "seq", axis=0, tiled=True),
        lax.all_gather(shrink, "seq", axis=0, tiled=True),
    )
    first_out, first_normed, first_scale = norm_full(stream, first_gain, first_bias)
    normed_in = first_out.astype(jnp.bfloat16)
    triple = (
        jnp.einsum("td,dch->tch", normed_in, full_project, preferred_element_type=jnp.float32)
        + project_bias[None]
    )
    head_shape = (local_count, head_count, HDIM)
    query_raw = triple[:, 0].reshape(head_shape)
    key_raw = triple[:, 1].reshape(head_shape)
    queries = place_query(query_raw, cosine, sine_table, growth).astype(jnp.bfloat16)
    keyed = place_key(key_raw, cosine, sine_table, growth).astype(jnp.bfloat16)
    valued = triple[:, 2].reshape(head_shape).astype(jnp.bfloat16)
    start_state = (
        jnp.full((head_count, local_count), NEGATIVE, jnp.float32),
        jnp.zeros((head_count, local_count), jnp.float32),
        jnp.zeros((head_count, local_count, HDIM), jnp.float32),
    )
    key_part = lax.all_gather(keyed.reshape(local_count, head_width), "seq", axis=0, tiled=True)
    value_part = lax.all_gather(valued.reshape(local_count, head_width), "seq", axis=0, tiled=True)
    piece_rows = key_part.shape[0]
    key_rows = jnp.arange(piece_rows, dtype=jnp.int32)
    key_docs = doc_of(key_rows, starts)
    skipped = (jnp.int32(0) > last_row) | (key_docs[piece_rows - 1] < first_doc)

    def attend_compute(state):
        running_max, running_sum, summed = state
        key_block = key_part.reshape(piece_rows, head_count, HDIM)
        value_block = value_part.reshape(piece_rows, head_count, HDIM)
        allowed = (
            (key_rows[None, :] <= token_rows[:, None]) & (key_docs[None, :] == doc_ids[:, None])
        )[None]
        scores = jnp.einsum("qhd,khd->hqk", queries, key_block, preferred_element_type=jnp.float32)
        scores = jnp.where(allowed, scores, NEGATIVE)
        newest = jnp.maximum(running_max, jnp.max(scores, axis=-1))
        weights_raw = jnp.where(allowed, jnp.exp(scores - newest[..., None]), 0.0)
        running_sum = jnp.sum(weights_raw, axis=-1)
        summed = jnp.einsum(
            "hqk,khd->hqd",
            weights_raw.astype(jnp.bfloat16),
            value_block,
            preferred_element_type=jnp.float32,
        )
        return (newest, running_sum, summed)

    running_max, running_sum, summed = lax.cond(skipped, keep_state, attend_compute, start_state)
    mixture = jnp.transpose(summed / running_sum[..., None], (1, 0, 2)).reshape(
        local_count, head_width
    )
    log_total = running_max + jnp.log(running_sum)
    inner_out, inner_normed, inner_scale = norm_split(mixture, inner_gain, inner_bias, D)
    combined_in = inner_out.astype(jnp.bfloat16)
    middle = (
        stream
        + branch_total(
            lax.dot_general(
                combined_in, full_combine, CONTRACT_LAST, preferred_element_type=jnp.float32
            )
        )
        + combine_bias
    )
    second_out, second_normed, second_scale = norm_full(middle, second_gain, second_bias)
    expand_in = second_out.astype(jnp.bfloat16)
    raised = jnp.dot(expand_in, full_expand, preferred_element_type=jnp.float32) + expand_bias
    active, gelu_back = jax.vjp(gelu_exact, raised)
    hidden_out, hidden_normed, hidden_scale = norm_split(active, hidden_gain, hidden_bias, FF)
    shrink_in = hidden_out.astype(jnp.bfloat16)
    output = (
        middle
        + branch_total(
            lax.dot_general(
                shrink_in, full_shrink, CONTRACT_LAST, preferred_element_type=jnp.float32
            )
        )
        + shrink_bias
    )
    back_project, back_combine, back_expand, back_shrink = (
        lax.all_gather(project, "seq", axis=0, tiled=True),
        lax.all_gather(combine, "seq", axis=0, tiled=True),
        lax.all_gather(expand, "seq", axis=0, tiled=True),
        lax.all_gather(shrink, "seq", axis=0, tiled=True),
    )
    shrink_bias_grad = jnp.sum(out_grad, axis=0)
    low_out = out_grad.astype(jnp.bfloat16)
    shrink_term = lax.dot_general(
        low_out, shrink_in, CONTRACT_FIRST, preferred_element_type=jnp.float32
    )
    hidden_grad = jnp.dot(low_out, back_shrink, preferred_element_type=jnp.float32)
    hidden_gain_grad = jnp.sum(hidden_grad * hidden_normed, axis=0)
    hidden_bias_grad = jnp.sum(hidden_grad, axis=0)
    active_grad = norm_split_back(hidden_grad, hidden_normed, hidden_scale, hidden_gain, FF)
    (raised_grad,) = gelu_back(active_grad)
    expand_bias_grad = jnp.sum(raised_grad, axis=0)
    low_raised = raised_grad.astype(jnp.bfloat16)
    expand_term = lax.dot_general(
        expand_in, low_raised, CONTRACT_FIRST, preferred_element_type=jnp.float32
    )
    second_grad = branch_total(
        lax.dot_general(low_raised, back_expand, CONTRACT_LAST, preferred_element_type=jnp.float32)
    )
    second_gain_grad = jnp.sum(second_grad * second_normed, axis=0)
    second_bias_grad = jnp.sum(second_grad, axis=0)
    middle_grad = out_grad + norm_full_back(second_grad, second_normed, second_scale, second_gain)
    combine_bias_grad = jnp.sum(middle_grad, axis=0)
    low_middle = middle_grad.astype(jnp.bfloat16)
    combine_term = lax.dot_general(
        low_middle, combined_in, CONTRACT_FIRST, preferred_element_type=jnp.float32
    )
    inner_grad = jnp.dot(low_middle, back_combine, preferred_element_type=jnp.float32)
    inner_gain_grad = jnp.sum(inner_grad * inner_normed, axis=0)
    inner_bias_grad = jnp.sum(inner_grad, axis=0)
    mixture_grad = norm_split_back(inner_grad, inner_normed, inner_scale, inner_gain, D)
    low_mixture = mixture_grad.astype(jnp.bfloat16)
    low_mixture3 = low_mixture.reshape(head_shape)
    delta = jnp.sum(low_mixture3.astype(jnp.float32) * mixture.reshape(head_shape), axis=-1)
    delta_heads = delta.T
    zero_heads = jnp.zeros(head_shape, jnp.float32)
    query_key_part = lax.all_gather(
        keyed.reshape(local_count, head_width), "seq", axis=0, tiled=True
    )
    query_value_part = lax.all_gather(
        valued.reshape(local_count, head_width), "seq", axis=0, tiled=True
    )
    query_piece_rows = query_key_part.shape[0]
    query_key_rows = jnp.arange(query_piece_rows, dtype=jnp.int32)
    query_key_docs = doc_of(query_key_rows, starts)
    skipped = (jnp.int32(0) > last_row) | (query_key_docs[query_piece_rows - 1] < first_doc)

    def query_compute(gathered):
        key_block = query_key_part.reshape(query_piece_rows, head_count, HDIM)
        value_block = query_value_part.reshape(query_piece_rows, head_count, HDIM)
        allowed = (
            (query_key_rows[None, :] <= token_rows[:, None])
            & (query_key_docs[None, :] == doc_ids[:, None])
        )[None]
        scores = jnp.einsum("qhd,khd->hqk", queries, key_block, preferred_element_type=jnp.float32)
        probability = jnp.where(allowed, jnp.exp(scores - log_total[..., None]), 0.0)
        pushes = jnp.einsum(
            "qhd,khd->hqk", low_mixture3, value_block, preferred_element_type=jnp.float32
        )
        dscore = (probability * (pushes - delta_heads[..., None])).astype(jnp.bfloat16)
        return jnp.einsum("hqk,khd->qhd", dscore, key_block, preferred_element_type=jnp.float32)

    query_grad3 = lax.cond(skipped, keep_state, query_compute, zero_heads)
    query_part = lax.all_gather(
        queries.astype(jnp.float32).reshape(local_count, head_width), "seq", axis=0, tiled=True
    )
    pull_part = lax.all_gather(low_mixture.astype(jnp.float32), "seq", axis=0, tiled=True)
    total_part = lax.all_gather(log_total.T, "seq", axis=0, tiled=True)
    delta_part = lax.all_gather(delta, "seq", axis=0, tiled=True)
    key_piece_rows = query_part.shape[0]
    query_rows = jnp.arange(key_piece_rows, dtype=jnp.int32)
    query_docs = doc_of(query_rows, starts)
    skipped = (query_rows[key_piece_rows - 1] < first_row) | (query_docs[0] > last_doc)

    def key_compute(state):
        query_block = query_part.astype(jnp.bfloat16).reshape(key_piece_rows, head_count, HDIM)
        pull_block = pull_part.astype(jnp.bfloat16).reshape(key_piece_rows, head_count, HDIM)
        allowed = (
            (token_rows[None, :] <= query_rows[:, None]) & (doc_ids[None, :] == query_docs[:, None])
        )[None]
        scores = jnp.einsum("qhd,khd->hqk", query_block, keyed, preferred_element_type=jnp.float32)
        probability = jnp.where(allowed, jnp.exp(scores - total_part.T[..., None]), 0.0)
        pushes = jnp.einsum("qhd,khd->hqk", pull_block, valued, preferred_element_type=jnp.float32)
        dscore = (probability * (pushes - delta_part.T[..., None])).astype(jnp.bfloat16)
        key_acc = jnp.einsum(
            "hqk,qhd->khd", dscore, query_block, preferred_element_type=jnp.float32
        )
        value_acc = jnp.einsum(
            "hqk,qhd->khd",
            probability.astype(jnp.bfloat16),
            pull_block,
            preferred_element_type=jnp.float32,
        )
        return (key_acc, value_acc)

    key_grad3, value_grad3 = lax.cond(skipped, keep_state, key_compute, (zero_heads, zero_heads))
    _, query_back = jax.vjp(
        partial(place_query, cosine=cosine, sine_table=sine_table, growth=growth), query_raw
    )
    _, key_back = jax.vjp(
        partial(place_key, cosine=cosine, sine_table=sine_table, growth=growth), key_raw
    )
    (query_grad,) = query_back(query_grad3)
    (key_grad,) = key_back(key_grad3)
    triple_grad = jnp.stack(
        [
            query_grad.reshape(local_count, head_width),
            key_grad.reshape(local_count, head_width),
            value_grad3.reshape(local_count, head_width),
        ],
        axis=1,
    )
    project_bias_grad = jnp.sum(triple_grad, axis=0)
    low_triple = triple_grad.astype(jnp.bfloat16)
    project_term = jnp.einsum(
        "td,tch->dch", normed_in, low_triple, preferred_element_type=jnp.float32
    )
    first_grad = branch_total(
        jnp.einsum("tch,dch->td", low_triple, back_project, preferred_element_type=jnp.float32)
    )
    first_gain_grad = jnp.sum(first_grad * first_normed, axis=0)
    first_bias_grad = jnp.sum(first_grad, axis=0)
    stream_grad = middle_grad + norm_full_back(first_grad, first_normed, first_scale, first_gain)
    project_grad, combine_grad, expand_grad, shrink_grad = (
        lax.psum_scatter(project_term, "seq", scatter_dimension=0, tiled=True),
        lax.psum_scatter(combine_term, "seq", scatter_dimension=0, tiled=True),
        lax.psum_scatter(expand_term, "seq", scatter_dimension=0, tiled=True),
        lax.psum_scatter(shrink_term, "seq", scatter_dimension=0, tiled=True),
    )
    (
        first_gain_grad,
        first_bias_grad,
        project_bias_grad,
        inner_gain_grad,
        inner_bias_grad,
        combine_bias_grad,
        second_gain_grad,
        second_bias_grad,
        expand_bias_grad,
        hidden_gain_grad,
        hidden_bias_grad,
        shrink_bias_grad,
    ) = lax.psum(
        (
            first_gain_grad,
            first_bias_grad,
            project_bias_grad,
            inner_gain_grad,
            inner_bias_grad,
            combine_bias_grad,
            second_gain_grad,
            second_bias_grad,
            expand_bias_grad,
            hidden_gain_grad,
            hidden_bias_grad,
            shrink_bias_grad,
        ),
        "seq",
    )
    return (
        output,
        stream_grad,
        project_grad,
        project_bias_grad,
        combine_grad,
        combine_bias_grad,
        expand_grad,
        expand_bias_grad,
        shrink_grad,
        shrink_bias_grad,
        first_gain_grad,
        first_bias_grad,
        inner_gain_grad,
        inner_bias_grad,
        second_gain_grad,
        second_bias_grad,
        hidden_gain_grad,
        hidden_bias_grad,
    )


BF = jnp.bfloat16
F32 = jnp.float32
GRID = (4, 2, 2)
SEQ = 16
ALIGNED = (((0,), (0,)), ((), ()))
PLAIN = (((1,), (0,)), ((), ()))
HOPS = {
    "x": [(i, i ^ 1) for i in range(SEQ)],
    "y": [(i, i ^ 2) for i in range(SEQ)],
    "xy": [(i, i ^ 3) for i in range(SEQ)],
    "z1": [(i, (i + 4) % SEQ) for i in range(SEQ)],
    "z2": [(i, (i + 8) % SEQ) for i in range(SEQ)],
    "z3": [(i, (i + 12) % SEQ) for i in range(SEQ)],
}
COLUMN = ("z1", "z2", "z3")


def fits_heads(mesh):
    return mesh.shape["seq"] == SEQ and mesh.shape["tp"] == 2


def hop(values, way):
    if way == "t":
        return lax.ppermute(values, "tp", [(0, 1), (1, 0)])
    return lax.ppermute(values, "seq", HOPS[way])


def after(first, *later):
    return lax.optimization_barrier((first,) + later)


def gather_along(values, way, axis):
    return jnp.stack([values, hop(values, way)], axis=axis)


def gather_column(own):
    return jnp.stack([own] + [hop(own, way) for way in COLUMN])


def gather_plane(column, midway=None):
    half = column.shape[2] // 2
    left = gather_along(column[:, :, :half], "x", 1)
    right = gather_along(column[:, :, half:], "y", 1)
    done = None
    if midway is not None:
        left, right, done = midway(left, right)
    mine = [gather_along(left, "y", 1), gather_along(right, "x", 2)]
    mine = [piece.reshape(-1, half) for piece in mine]
    if midway is not None:
        mine[0], mine[1], *done = after(mine[0], mine[1], *done)
    return mine + [hop(piece, "t") for piece in mine], done


def gather_small(values):
    return gather_along(gather_along(gather_column(values), "x", 1), "y", 1)


def add_low(first, second):
    return (first.astype(F32) + second.astype(F32)).astype(BF)


def fold(values, way, axis):
    near = lax.index_in_dim(values, 0, axis, keepdims=False)
    far = lax.index_in_dim(values, 1, axis, keepdims=False)
    return add_low(near, hop(far, way))


def scatter_pair(low, own, others):
    return [
        (dot(low, weights, own[0]) + hop(other, "t").astype(F32)).astype(BF)
        for weights, other in zip(own[1], others, strict=True)
    ]


def scatter_wide(pair):
    shape = GRID + (-1, pair[0].shape[1])
    return [fold(pair[0].reshape(shape), "y", 1), fold(pair[1].reshape(shape), "x", 2)]


def scatter_narrow(halves):
    return jnp.concatenate([fold(halves[0], "x", 1), fold(halves[1], "y", 1)], axis=2)


def scatter_plane(pair):
    return scatter_narrow(scatter_wide(pair))


def scatter_column(slabs):
    total = slabs[0].astype(F32)
    for i in range(1, 4):
        total = total + lax.optimization_barrier(hop(slabs[i], COLUMN[3 - i])).astype(F32)
    return total


def swap_by(flag, values, axis):
    return jnp.where(flag == 0, values, jnp.flip(values, axis))


def own_half(side, values, axis=-1):
    left, right = jnp.split(values, 2, axis=axis)
    return jnp.where(side == 0, left, right)


def join_halves(side, mine, other, axis=-1):
    return jnp.concatenate(
        [jnp.where(side == 0, mine, other), jnp.where(side == 0, other, mine)], axis=axis
    )


def turn_halves(side, values, axis=0):
    left, right = jnp.split(values, 2, axis=axis)
    return jnp.concatenate(
        [jnp.where(side == 0, left, right), jnp.where(side == 0, right, left)], axis=axis
    )


def token_sum(values):
    shape = values.shape
    values = (values + hop(values, "t")).reshape((shape[0],) + GRID + (-1,))
    moved = [jnp.flip(hop(values, "x"), 3), jnp.flip(hop(values, "y"), 2)]
    values = values + moved[0] + moved[1] + jnp.flip(hop(values, "xy"), (2, 3))
    moved = [jnp.roll(hop(values, COLUMN[i]), i + 1, 1) for i in range(3)]
    return (values + moved[0] + moved[1] + moved[2]).reshape(shape)


def seq_sum(values):
    values = values + hop(values, "x") + hop(values, "y") + hop(values, "xy")
    return values + hop(values, "z1") + hop(values, "z2") + hop(values, "z3")


def pair_sum(values):
    return values + hop(values, "t")


def dot(first, second, dims):
    return lax.dot_general(first, second, dims, preferred_element_type=F32)


BLOCK = 512
CHUNK = 256
SPARE = 16
KERNEL_BYTES = 48 * 1024 * 1024


def attend_kernel(
    order_ref, first_ref, second_ref, third_ref, fourth_ref, weights_ref, bias_ref,
    cosine_ref, sine_ref, growth_ref, begin_ref, kept_ref, mixture_ref, sent_ref, log_ref, wide,
):
    step = pl.program_id(0)
    part = first_ref.shape[1]
    rows = mixture_ref.shape[2]
    raw = bias_ref[...]
    for index, piece in enumerate((first_ref, second_ref, third_ref, fourth_ref)):
        raw = raw + dot(
            weights_ref[:, index * part : (index + 1) * part], piece[...], CONTRACT_LAST
        )
    for block in range(CHUNK // rows):
        place = order_ref[step * (CHUNK // rows) + block] * rows
        wide[:, pl.ds(pl.multiple_of(place, rows), rows)] = raw[:, block * rows : (block + 1) * rows]

    @pl.when(step == pl.num_programs(0) - 1)
    def _():
        attend_head(
            cosine_ref, sine_ref, growth_ref, begin_ref, kept_ref, mixture_ref, sent_ref, log_ref,
            wide,
        )


def attend_head(
    cosine_ref, sine_ref, growth_ref, begin_ref, kept_ref, mixture_ref, sent_ref, log_ref, wide
):
    tokens = wide.shape[1]
    half = HDIM // 2
    rows = tokens // SEQ
    cosine, sine, growth = cosine_ref[...], sine_ref[...], growth_ref[...]
    first, second = wide[0:half, :], wide[half:HDIM, :]
    scaled = growth * HDIM ** (-0.5)
    kept_ref[0:half, :] = ((first * cosine - second * sine) * scaled).astype(BF)
    kept_ref[half:HDIM, :] = ((second * cosine + first * sine) * scaled).astype(BF)
    first, second = wide[HDIM : HDIM + half, :], wide[HDIM + half : 2 * HDIM, :]
    kept_ref[HDIM : HDIM + half, :] = ((first * cosine - second * sine) / growth).astype(BF)
    kept_ref[HDIM + half : 2 * HDIM, :] = ((second * cosine + first * sine) / growth).astype(BF)
    kept_ref[2 * HDIM :, :] = wide[2 * HDIM :, :].astype(BF)
    key_rows = lax.broadcasted_iota(jnp.int32, (BLOCK, BLOCK), 0)
    query_rows = lax.broadcasted_iota(jnp.int32, (BLOCK, BLOCK), 1)
    spare = lax.broadcasted_iota(jnp.int32, (SPARE, BLOCK), 0)
    for i in range(tokens // BLOCK):
        columns = slice(i * BLOCK, (i + 1) * BLOCK)
        queries = kept_ref[0:HDIM, columns]
        begin = begin_ref[:, columns]
        largest = jnp.full((1, BLOCK), NEGATIVE, F32)
        total = jnp.zeros((1, BLOCK), F32)
        summed = jnp.zeros((HDIM, BLOCK), F32)
        for j in range(i, -1, -1):
            place = slice(j * BLOCK, (j + 1) * BLOCK)
            scores = dot(kept_ref[HDIM : 2 * HDIM, place], queries, ALIGNED)
            allowed = key_rows + j * BLOCK >= begin
            if j == i:
                allowed = allowed & (key_rows <= query_rows)
            scores = jnp.where(allowed, scores, NEGATIVE)
            newest = jnp.maximum(largest, jnp.max(scores, axis=0, keepdims=True))
            weights = jnp.exp(scores - newest)
            shrunk = jnp.exp(largest - newest)
            total = total * shrunk + jnp.sum(weights, axis=0, keepdims=True)
            summed = summed * shrunk + dot(
                kept_ref[2 * HDIM :, place], weights.astype(BF), PLAIN
            )
            largest = newest
        mixture = summed / total
        average = jnp.mean(mixture, axis=0, keepdims=True)
        high = average.astype(BF).astype(F32)
        low = (average - high).astype(BF).astype(F32)
        tail = jnp.where(spare == 0, high, jnp.where(spare == 1, low, average - high - low))
        sent = jnp.concatenate([mixture - average, jnp.where(spare < 3, tail, 0.0)], axis=0).astype(BF)
        for block in range(BLOCK // rows):
            place = slice(block * rows, (block + 1) * rows)
            mixture_ref[i * (BLOCK // rows) + block] = mixture[:, place]
            sent_ref[i * (BLOCK // rows) + block] = sent[:, place]
        log_ref[:, columns] = largest + jnp.log(total)


def retreat_kernel(
    order_ref, kept_ref, pull_ref, mixture_ref, log_ref, cosine_ref, sine_ref, growth_ref, begin_ref,
    low_ref, bias_ref, pulls, delta, query_sum, key_sum, value_sum,
):
    tokens = kept_ref.shape[1]
    half = HDIM // 2
    rows = tokens // SEQ
    for block in range(SEQ):
        place = slice(block * rows, (block + 1) * rows)
        pulls[:, place] = pull_ref[block]
        delta[:, place] = jnp.sum(
            pull_ref[block].astype(F32) * mixture_ref[block], axis=0, keepdims=True
        )
    key_rows = lax.broadcasted_iota(jnp.int32, (BLOCK, BLOCK), 0)
    query_rows = lax.broadcasted_iota(jnp.int32, (BLOCK, BLOCK), 1)
    for i in range(tokens // BLOCK):
        columns = slice(i * BLOCK, (i + 1) * BLOCK)
        queries = kept_ref[0:HDIM, columns]
        pull = pulls[:, columns]
        begin = begin_ref[:, columns]
        logs = log_ref[:, columns]
        offset = delta[:, columns]
        query_part = jnp.zeros((HDIM, BLOCK), F32)
        for j in range(i + 1):
            place = slice(j * BLOCK, (j + 1) * BLOCK)
            keys = kept_ref[HDIM : 2 * HDIM, place]
            scores = dot(keys, queries, ALIGNED)
            allowed = key_rows + j * BLOCK >= begin
            if j == i:
                allowed = allowed & (key_rows <= query_rows)
            chance = jnp.where(allowed, jnp.exp(scores - logs), 0.0)
            pushes = dot(kept_ref[2 * HDIM :, place], pull, ALIGNED)
            dscore = (chance * (pushes - offset)).astype(BF)
            query_part = query_part + dot(keys, dscore, PLAIN)
            key_part = dot(queries, dscore, CONTRACT_LAST)
            value_part = dot(pull, chance.astype(BF), CONTRACT_LAST)
            if j == i:
                key_sum[:, place] = key_part
                value_sum[:, place] = value_part
            else:
                key_sum[:, place] += key_part
                value_sum[:, place] += value_part
        query_sum[:, columns] = query_part
    cosine, sine, growth = cosine_ref[...], sine_ref[...], growth_ref[...]
    scaled = growth * HDIM ** (-0.5)
    first, second = query_sum[0:half, :] * scaled, query_sum[half:, :] * scaled
    pieces = [first * cosine + second * sine, second * cosine - first * sine]
    first, second = key_sum[0:half, :] / growth, key_sum[half:, :] / growth
    pieces += [first * cosine + second * sine, second * cosine - first * sine]
    pieces += [value_sum[0:half, :], value_sum[half:, :]]
    for index, piece in enumerate(pieces):
        lanes = slice(index * half, (index + 1) * half)
        bias_ref[lanes, :] = jnp.sum(piece, axis=1, keepdims=True)
        low = piece.astype(BF)
        for block in range(SEQ):
            place = pl.ds(pl.multiple_of(order_ref[block] * rows, rows), rows)
            low_ref[lanes, place] = low[:, block * rows : (block + 1) * rows]


def whole(count):
    return [pl.BlockSpec(memory_space=pltpu.VMEM) for _ in range(count)]


def attend(order, pieces, weights, bias, cosine, sine, growth, begin):
    tokens, part = pieces[0].shape
    depth = weights.shape[1]
    table = still((HDIM // 2, tokens))
    return pl.pallas_call(
        attend_kernel,
        grid_spec=pltpu.PrefetchScalarGridSpec(
            num_scalar_prefetch=1,
            grid=(tokens // CHUNK,),
            in_specs=[pl.BlockSpec((CHUNK, part), lambda i, order: (i, 0)) for _ in pieces]
            + [still((3 * HDIM, depth)), still((3 * HDIM, 1)), table, table, table, still((1, tokens))],
            out_specs=(
                still((3 * HDIM, tokens)),
                still((SEQ, HDIM, tokens // SEQ)),
                still((SEQ, HDIM + SPARE, tokens // SEQ)),
                still((1, tokens)),
            ),
            scratch_shapes=[pltpu.VMEM((3 * HDIM, tokens), F32)],
        ),
        out_shape=(
            jax.ShapeDtypeStruct((3 * HDIM, tokens), BF),
            jax.ShapeDtypeStruct((SEQ, HDIM, tokens // SEQ), F32),
            jax.ShapeDtypeStruct((SEQ, HDIM + SPARE, tokens // SEQ), BF),
            jax.ShapeDtypeStruct((1, tokens), F32),
        ),
        compiler_params=pltpu.CompilerParams(vmem_limit_bytes=KERNEL_BYTES),
        cost_estimate=pl.CostEstimate(
            flops=2 * tokens * tokens * HDIM, bytes_accessed=2 * tokens * depth,
            transcendentals=tokens * tokens // 2,
        ),
    )(order, *pieces, weights, bias, cosine, sine, growth, begin)


def retreat(order, kept, pull, mixture, logs, cosine, sine, growth, begin):
    tokens = kept.shape[1]
    return pl.pallas_call(
        retreat_kernel,
        out_shape=(
            jax.ShapeDtypeStruct((3 * HDIM, tokens), BF),
            jax.ShapeDtypeStruct((3 * HDIM, 1), F32),
        ),
        in_specs=[pl.BlockSpec(memory_space=pltpu.SMEM)] + whole(8),
        out_specs=tuple(whole(2)),
        scratch_shapes=[
            pltpu.VMEM((HDIM, tokens), BF),
            pltpu.VMEM((1, tokens), F32),
            pltpu.VMEM((HDIM, tokens), F32),
            pltpu.VMEM((HDIM, tokens), F32),
            pltpu.VMEM((HDIM, tokens), F32),
        ],
        compiler_params=pltpu.CompilerParams(vmem_limit_bytes=KERNEL_BYTES),
        cost_estimate=pl.CostEstimate(
            flops=5 * tokens * tokens * HDIM, bytes_accessed=8 * 192 * tokens,
            transcendentals=tokens * tokens // 2,
        ),
    )(order, kept, pull, mixture, logs, cosine, sine, growth, begin)


def enter_kernel(
    first_ref, second_ref, third_ref, fourth_ref, grad_ref, expand_ref, shift_ref, gain_ref,
    active_ref, slope_ref, stats_ref,
):
    part = first_ref.shape[1]
    raised = shift_ref[...]
    for index, piece in enumerate((first_ref, second_ref, third_ref, fourth_ref)):
        raised = raised + dot(piece[...], expand_ref[index * part : (index + 1) * part, :], PLAIN)
    chance = 0.5 * (1.0 + lax.erf(raised * math.sqrt(0.5)))
    active = raised * chance
    active_ref[...] = active
    slope_ref[...] = chance + raised * jnp.exp(raised * raised * -0.5) * (1.0 / math.sqrt(2.0 * math.pi))
    scaled = grad_ref[...] * gain_ref[...]
    lane = lax.broadcasted_iota(jnp.int32, (CHUNK, 128), 1)
    columns = jnp.zeros((CHUNK, 128), F32)
    for index, values in enumerate((active, active * active, scaled, scaled * active)):
        columns = jnp.where(lane == index, jnp.sum(values, axis=1, keepdims=True), columns)
    stats_ref[...] = columns.T[0:8, :]


def leave_kernel(
    active_ref, slope_ref, grad_ref, stats_ref, expand_ref, gain_ref, shift_ref,
    shrunk_ref, low_ref, first_ref, second_ref, sums_ref,
):
    @pl.when(pl.program_id(0) == 0)
    def _():
        sums_ref[...] = jnp.zeros_like(sums_ref)

    columns = jnp.concatenate([stats_ref[...], jnp.zeros((120, CHUNK), F32)], axis=0).T
    average, scale, grad_mean, cross_mean = (columns[:, i : i + 1] for i in range(4))
    hidden_grad = grad_ref[...]
    normed = (active_ref[...] - average) * scale
    shrunk_ref[...] = (normed * gain_ref[...] + shift_ref[...]).astype(BF)
    raised_grad = (
        scale * (hidden_grad * gain_ref[...] - grad_mean - normed * cross_mean) * slope_ref[...]
    )
    low = raised_grad.astype(BF)
    low_ref[...] = low
    sums_ref[0:1, :] += jnp.sum(hidden_grad * normed, axis=0, keepdims=True)
    sums_ref[1:2, :] += jnp.sum(hidden_grad, axis=0, keepdims=True)
    sums_ref[2:3, :] += jnp.sum(raised_grad, axis=0, keepdims=True)
    part = first_ref.shape[1]
    for index, out_ref in enumerate((first_ref, second_ref)):
        out_ref[...] = dot(
            low, expand_ref[index * part : (index + 1) * part, :], CONTRACT_LAST
        ).astype(BF)


def still(shape):
    return pl.BlockSpec(shape, lambda *_: (0,) * len(shape))


def enter(pieces, grad, expand_mine, shift, gain):
    tokens, part = pieces[0].shape
    depth, units = expand_mine.shape
    block = pl.BlockSpec((CHUNK, units), lambda i: (i, 0))
    wide = jax.ShapeDtypeStruct((tokens, units), F32)
    return pl.pallas_call(
        enter_kernel,
        grid=(tokens // CHUNK,),
        in_specs=[pl.BlockSpec((CHUNK, part), lambda i: (i, 0)) for _ in pieces]
        + [block, still((depth, units)), still((1, units)), still((1, units))],
        out_specs=(block, block, pl.BlockSpec((8, CHUNK), lambda i: (0, i))),
        out_shape=(wide, wide, jax.ShapeDtypeStruct((8, tokens), F32)),
        compiler_params=pltpu.CompilerParams(vmem_limit_bytes=KERNEL_BYTES),
        cost_estimate=pl.CostEstimate(
            flops=2 * tokens * depth * units, bytes_accessed=6 * tokens * depth, transcendentals=0
        ),
    )(*pieces, grad, expand_mine, shift, gain)


def leave(active, slope, grad, stats, expand_other, gain, shift):
    tokens, units = active.shape
    depth = expand_other.shape[0]
    block = pl.BlockSpec((CHUNK, units), lambda i: (i, 0))
    piece = pl.BlockSpec((CHUNK, depth // 2), lambda i: (i, 0))
    low = jax.ShapeDtypeStruct((tokens, units), BF)
    partial_sum = jax.ShapeDtypeStruct((tokens, depth // 2), BF)
    return pl.pallas_call(
        leave_kernel,
        grid=(tokens // CHUNK,),
        in_specs=[block, block, block, pl.BlockSpec((8, CHUNK), lambda i: (0, i))]
        + [still((depth, units)), still((1, units)), still((1, units))],
        out_specs=(block, block, piece, piece, still((8, units))),
        out_shape=(low, low) + (partial_sum,) * 2 + (jax.ShapeDtypeStruct((8, units), F32),),
        compiler_params=pltpu.CompilerParams(vmem_limit_bytes=KERNEL_BYTES),
        cost_estimate=pl.CostEstimate(
            flops=2 * tokens * depth * units, bytes_accessed=6 * tokens * depth, transcendentals=0
        ),
    )(active, slope, grad, stats, expand_other, gain, shift)


def to_owners(values):
    return lax.all_to_all(values, "seq", split_axis=0, concat_axis=0, tiled=True)


def by_owner(weights, rows):
    return jnp.transpose(weights.reshape(rows, SEQ, -1), (1, 0, 2))


def columns_of(moved, side):
    return turn_halves(side, moved.reshape(-1, moved.shape[2]))


def by_row_owner(pieces, side):
    full = turn_halves(side, jnp.concatenate(pieces, axis=0))
    return full.reshape(SEQ, -1, full.shape[1])


def rows_of(moved):
    return jnp.transpose(moved, (1, 0, 2)).reshape(moved.shape[1], -1).astype(F32)


def head_shards(
    stream,
    doc_ids,
    project,
    project_bias,
    combine,
    combine_bias,
    expand,
    expand_bias,
    shrink,
    shrink_bias,
    first_gain,
    first_bias,
    inner_gain,
    inner_bias,
    second_gain,
    second_bias,
    hidden_gain,
    hidden_bias,
    out_grad,
):
    rows = stream.shape[0]
    tokens = SEQ * rows
    head_width = project.shape[2]
    width = expand.shape[1] // SEQ
    spot = lax.axis_index("seq")
    side = lax.axis_index("tp")
    spot_z, spot_y, spot_x = spot // 4, (spot // 2) % 2, spot % 2
    blocks = jnp.arange(SEQ, dtype=jnp.int32)
    order = (
        ((spot_z - blocks // 4) % 4) * 4 + (spot_y ^ ((blocks // 2) % 2)) * 2 + (spot_x ^ (blocks % 2))
    )

    def mine(values, axis=-1):
        return own_half(side, values, axis)

    def my_units(vector, size):
        return lax.dynamic_slice_in_dim(vector, spot * size, size, axis=-1)

    first_out, first_normed, first_scale = norm_full(stream, first_gain, first_bias)
    normed_column = gather_column(mine(first_out.astype(BF)))
    docs_near = gather_small(doc_ids[None, :]).reshape(SEQ, rows)
    full_combine = lax.all_gather(combine, "seq", axis=0, tiled=True)
    out_grad_mine = mine(out_grad)
    low_out = lax.all_gather(out_grad_mine.astype(BF), "seq", axis=0, tiled=True)
    normed_column, project_own = after(
        normed_column,
        jnp.transpose(project.reshape(rows, 3, SEQ, HDIM), (2, 1, 3, 0)).reshape(
            SEQ, 3 * HDIM, rows
        ),
    )
    normed_pieces, _ = gather_plane(normed_column)
    project_moved = to_owners(project_own)
    project_mine = turn_halves(
        side, jnp.transpose(project_moved, (1, 0, 2)).reshape(3 * HDIM, tokens), axis=1
    )
    project_pieces = jnp.split(project_mine, 4, axis=1)

    docs = docs_near[order].reshape(tokens)
    member = (docs[:, None] == jnp.arange(DOCS, dtype=jnp.int32)[None, :]).astype(jnp.int32)
    counts = jnp.sum(member, axis=0)
    starts = jnp.cumsum(counts) - counts
    begin = jnp.sum(member * starts[None, :], axis=1)
    positions = jnp.arange(tokens, dtype=jnp.int32) - begin
    column = jnp.arange(HDIM // 2, dtype=F32)
    frequency = jnp.exp(column * (-2.0 * math.log(10000.0) / HDIM))
    base_ratio = (2.0 * column + 0.4 * HDIM) / (1.4 * HDIM)
    location = positions.astype(F32)
    phase_angle = frequency[:, None] * location[None, :]
    cosine, sine = jnp.cos(phase_angle), jnp.sin(phase_angle)
    growth = jnp.exp(
        jnp.log(base_ratio)[:, None] * ((location - tokens // 2) / SCALE_BASE)[None, :]
    )
    begin = begin[None, :]

    head_bias = my_units(project_bias, HDIM).reshape(3 * HDIM, 1)
    kept, mixture, sent, logs = attend(
        order, normed_pieces, project_mine, head_bias, cosine, sine, growth, begin
    )

    sent = to_owners(sent).astype(F32)
    averages = jnp.sum(sent[:, HDIM : HDIM + 3], axis=1, keepdims=True)
    spread = (sent[:, :HDIM] + averages).reshape(head_width, rows)
    sums = pair_sum(jnp.stack([jnp.sum(spread, axis=0), jnp.sum(spread * spread, axis=0)]))
    average = sums[0:1] / D
    inner_scale = lax.rsqrt(sums[1:2] / D - average * average + EPSILON)
    inner_normed = (spread - average) * inner_scale
    combined_in = (inner_normed * inner_gain[:, None] + inner_bias[:, None]).astype(BF)
    branch = dot(combined_in, full_combine, (((0,), (1,)), ((), ())))
    left, right = jnp.split(branch, 2, axis=1)
    branch = jnp.where(side == 0, left, right) + hop(jnp.where(side == 0, right, left), "t")
    middle = mine(stream) + branch + mine(combine_bias)
    sums = pair_sum(jnp.stack([jnp.sum(middle, axis=1), jnp.sum(middle * middle, axis=1)]))
    average = (sums[0] / D)[:, None]
    second_scale = lax.rsqrt((sums[1] / D)[:, None] - average * average + EPSILON)
    second_normed = (middle - average) * second_scale
    gain_half, bias_half = mine(second_gain), mine(second_bias)
    expand_column = gather_column((second_normed * gain_half + bias_half).astype(BF))
    expand_column, shrink_own = after(expand_column, by_owner(shrink, rows))
    shrink_moved = to_owners(shrink_own)

    def pull_back(left, right):
        left, right, units, expand_own = after(left, right, shrink_moved, by_owner(expand, rows))
        _, near = after(left, low_out)
        shrink_mine = columns_of(units, side)
        low = [near, hop(near, "t")]
        grad = sum(
            dot(piece, part, PLAIN)
            for piece, part in zip(low, jnp.split(shrink_mine, 2, axis=0), strict=True)
        )
        grad = grad.reshape(SEQ, rows, width)[order].reshape(tokens, width)
        return left, right, (low[0], low[1], grad, shrink_mine, to_owners(expand_own))

    expand_pieces, midway = gather_plane(expand_column, pull_back)
    low_out, (hidden_grad, shrink_mine) = midway[:2], midway[2:4]
    expand_mine = columns_of(midway[4], side)

    unit_gain, unit_bias = my_units(hidden_gain, width)[None, :], my_units(hidden_bias, width)[None, :]
    active, slope, sums = enter(
        expand_pieces, hidden_grad, expand_mine, my_units(expand_bias, width)[None, :], unit_gain
    )
    sums, combined_late = after(token_sum(sums[0:4]), combined_in.T)
    full_combined = lax.all_gather(combined_late, "seq", axis=0, tiled=True)
    average = sums[0:1] / FF
    hidden_scale = lax.rsqrt(sums[1:2] / FF - average * average + EPSILON)
    grad_mean = sums[2:3] / FF
    cross_mean = hidden_scale * (sums[3:4] / FF - average * grad_mean)
    stats = jnp.concatenate(
        [average, hidden_scale, grad_mean, cross_mean, jnp.zeros((4, tokens), F32)]
    )
    expand_parts = jnp.split(expand_mine, 4, axis=0)
    left = leave(
        active, slope, hidden_grad, stats, expand_mine[expand_mine.shape[0] // 2 :], unit_gain, unit_bias
    )
    pair, shrink_in, low_raised = after(
        scatter_pair(left[1], (CONTRACT_LAST, expand_parts[:2]), left[2:4]), left[0], left[1]
    )
    shrink_far = shrink_in.reshape(SEQ, rows, width)[order].reshape(tokens, width)
    shrink_term = by_row_owner(
        [dot(piece, shrink_far, CONTRACT_FIRST).astype(BF) for piece in low_out], side
    )
    halves, shrink_in = after(scatter_wide(pair), shrink_in)
    slabs, shrink_moved = after(scatter_narrow(halves), to_owners(shrink_term))
    shrink_grad = rows_of(shrink_moved)
    second_grad = scatter_column(slabs)
    expand_term = by_row_owner(
        [dot(piece, low_raised, CONTRACT_FIRST).astype(BF) for piece in expand_pieces], side
    )
    shrink_parts = jnp.split(shrink_mine, 4, axis=0)
    others = [dot(shrink_in, weights, CONTRACT_LAST).astype(BF) for weights in shrink_parts[2:]]
    output_pair = scatter_pair(shrink_in, (CONTRACT_LAST, shrink_parts[:2]), others)
    second_grad, expand_term, output_pair = after(second_grad, expand_term, output_pair)
    expand_moved = to_owners(expand_term)
    output_halves = scatter_wide(output_pair)

    scaled = second_grad * gain_half
    sums = pair_sum(jnp.stack([jnp.sum(scaled, axis=1), jnp.sum(scaled * second_normed, axis=1)]))
    middle_grad = out_grad_mine + second_scale * (
        scaled - (sums[0] / D)[:, None] - second_normed * (sums[1] / D)[:, None]
    )
    low_middle = middle_grad.astype(BF)
    low_middle = join_halves(side, low_middle, hop(low_middle, "t"))
    inner_grad = dot(full_combine, low_middle, (((0,), (1,)), ((), ())))
    scaled = inner_grad * inner_gain[:, None]
    sums = pair_sum(jnp.stack([jnp.sum(scaled, axis=0), jnp.sum(scaled * inner_normed, axis=0)]))
    mixture_grad = inner_scale * (scaled - sums[0:1] / D - inner_normed * (sums[1:2] / D))
    mixture_grad, expand_moved, output_halves, full_combined = after(
        mixture_grad.astype(BF).reshape(SEQ, HDIM, rows), expand_moved, output_halves, full_combined
    )
    expand_grad = rows_of(expand_moved)
    pull, low_middle, output_slabs = after(
        to_owners(mixture_grad), low_middle, scatter_narrow(output_halves)
    )
    output = middle + scatter_column(output_slabs) + mine(shrink_bias)
    moved = to_owners(by_owner(low_middle, rows))

    low_triple, head_sums = retreat(
        order, kept, pull, mixture, logs, cosine, sine, growth, begin
    )
    others = [dot(low_triple, weights, CONTRACT_FIRST).astype(BF) for weights in project_pieces[2:]]
    others, moved, output = after(others, moved, output)
    combine_grad = dot(moved.reshape(tokens, -1), full_combined, CONTRACT_FIRST)
    pair = scatter_pair(low_triple, (CONTRACT_FIRST, project_pieces[:2]), others)
    term = turn_halves(
        side,
        jnp.concatenate(
            [dot(low_triple, piece, PLAIN).astype(BF) for piece in normed_pieces], axis=1
        ),
        axis=1,
    )
    pair[0], term = after(pair[0], term)
    moved = to_owners(jnp.transpose(term.reshape(3 * HDIM, SEQ, rows), (1, 0, 2)))
    slabs, moved = after(scatter_plane(pair), moved)
    first_grad = scatter_column(slabs)
    project_grad = jnp.transpose(moved.reshape(SEQ, 3, HDIM, rows), (3, 1, 0, 2)).reshape(
        rows, 3, head_width
    ).astype(F32)
    normed_half = mine(first_normed)
    scaled = first_grad * mine(first_gain)
    sums = pair_sum(jnp.stack([jnp.sum(scaled, axis=1), jnp.sum(scaled * normed_half, axis=1)]))
    stream_grad = middle_grad + first_scale * (
        scaled - (sums[0] / D)[:, None] - normed_half * (sums[1] / D)[:, None]
    )

    unit_sums = lax.dynamic_update_slice(
        jnp.zeros((3, SEQ * width), F32), left[4][0:3], (0, spot * width)
    )
    head_sums = lax.dynamic_update_slice(
        jnp.zeros((3, head_width), F32), head_sums.reshape(3, HDIM), (0, spot * HDIM)
    )
    early = [
        jnp.sum(out_grad_mine, axis=0),
        jnp.sum(second_grad * second_normed, axis=0),
        jnp.sum(second_grad, axis=0),
        jnp.sum(middle_grad, axis=0),
        jnp.sum(inner_grad * inner_normed, axis=1),
        jnp.sum(inner_grad, axis=1),
    ]
    early = seq_sum(
        jnp.concatenate([jnp.stack(early), head_sums, unit_sums.reshape(-1, head_width)])
    )
    late = seq_sum(jnp.stack([jnp.sum(first_grad * normed_half, axis=0), jnp.sum(first_grad, axis=0)]))
    halves = join_halves(side, early[:4], hop(early[:4], "t"))
    late = join_halves(side, late, hop(late, "t"))
    project_bias_grad = early[6:9]
    unit_sums = early[9:].reshape(3, SEQ * width)
    return (
        join_halves(side, output, hop(output, "t")),
        join_halves(side, stream_grad, hop(stream_grad, "t")),
        project_grad,
        project_bias_grad,
        combine_grad,
        halves[3],
        expand_grad,
        unit_sums[2],
        shrink_grad,
        halves[0],
        late[0],
        late[1],
        early[4],
        early[5],
        halves[1],
        halves[2],
        unit_sums[0],
        unit_sums[1],
    )


def solution(mesh):
    plan = head_shards if fits_heads(mesh) else shards
    return jax.shard_map(
        plan,
        mesh=mesh,
        in_specs=(
            P("seq", None),
            P("seq"),
            P("seq", None, "tp"),
            P(None, "tp"),
            P("seq", "tp"),
            P(),
            P("seq", "tp"),
            P("tp"),
            P("seq", "tp"),
            P(),
            P(),
            P(),
            P("tp"),
            P("tp"),
            P(),
            P(),
            P("tp"),
            P("tp"),
            P("seq", None),
        ),
        out_specs=(
            P("seq", None),
            P("seq", None),
            P("seq", None, "tp"),
            P(None, "tp"),
            P("seq", "tp"),
            P(),
            P("seq", "tp"),
            P("tp"),
            P("seq", "tp"),
            P(),
            P(),
            P(),
            P("tp"),
            P("tp"),
            P(),
            P(),
            P("tp"),
            P("tp"),
        ),
        check_vma=False,
    )
```

```python
from functools import partial
import math

import jax
import jax.numpy as jnp
from jax import lax
from jax.experimental import pallas as pl
from jax.experimental.pallas import tpu as pltpu
from jax.sharding import PartitionSpec as P

D = 2048
HDIM = 64
FF = 8192
DOCS = 5
SCALE_BASE = 512


EPSILON = 1e-05
NEGATIVE = -1e30
CONTRACT_LAST = (((1,), (1,)), ((), ()))
CONTRACT_FIRST = (((0,), (0,)), ((), ()))


def doubled(values_in):
    return jnp.concatenate([values_in, values_in], axis=-1)


def tables(positions, center):
    half_dim = HDIM // 2
    column = jnp.arange(half_dim, dtype=jnp.float32)
    frequency = jnp.exp(column * (-2.0 * math.log(10000.0) / HDIM))
    base_ratio = (2.0 * column + 0.4 * HDIM) / (1.4 * HDIM)
    location = positions.astype(jnp.float32)
    phase_angle = location[:, None] * frequency[None, :]
    exponent = ((location - center) / SCALE_BASE)[:, None] * jnp.log(base_ratio)[None, :]
    return (
        doubled(jnp.cos(phase_angle)),
        doubled(jnp.sin(phase_angle)),
        doubled(jnp.exp(exponent)),
    )


def turn_pairs(values, cosine, sine_table):
    half_dim = values.shape[-1] // 2
    swapped = jnp.concatenate([-values[..., half_dim:], values[..., :half_dim]], axis=-1)
    return values * cosine[:, None, :] + swapped * sine_table[:, None, :]


def place_query(values, cosine, sine_table, growth):
    return turn_pairs(values, cosine, sine_table) * growth[:, None, :] * HDIM ** (-0.5)


def place_key(values, cosine, sine_table, growth):
    return turn_pairs(values, cosine, sine_table) / growth[:, None, :]


def norm_full(values, gain_vector, shift_vector):
    average = jnp.mean(values, axis=-1, keepdims=True)
    inv_scale = lax.rsqrt(
        jnp.mean(values * values, axis=-1, keepdims=True) - average * average + EPSILON
    )
    normed = (values - average) * inv_scale
    return (normed * gain_vector + shift_vector, normed, inv_scale)


def norm_full_back(incoming, normed, inv_scale, gain_vector):
    scaled_grad = incoming * gain_vector
    first_mean = jnp.mean(scaled_grad, axis=-1, keepdims=True)
    cross_mean = jnp.mean(scaled_grad * normed, axis=-1, keepdims=True)
    return inv_scale * (scaled_grad - first_mean - normed * cross_mean)


def split_sums(first_term, second_term):
    return lax.psum((first_term, second_term), "tp")


def norm_split(values, gain_vector, shift_vector, full_width):
    totals, squares = split_sums(
        jnp.sum(values, axis=-1, keepdims=True), jnp.sum(values * values, axis=-1, keepdims=True)
    )
    average = totals / full_width
    inv_scale = lax.rsqrt(squares / full_width - average * average + EPSILON)
    normed = (values - average) * inv_scale
    return (normed * gain_vector + shift_vector, normed, inv_scale)


def norm_split_back(incoming, normed, inv_scale, gain_vector, full_width):
    scaled_grad = incoming * gain_vector
    totals, crossed = split_sums(
        jnp.sum(scaled_grad, axis=-1, keepdims=True),
        jnp.sum(scaled_grad * normed, axis=-1, keepdims=True),
    )
    return inv_scale * (scaled_grad - totals / full_width - normed * (crossed / full_width))


def branch_total(values):
    return lax.psum(values, "tp")


def doc_of(token_rows, starts):
    return jnp.sum((token_rows[:, None] >= starts[None, 1:]).astype(jnp.int32), axis=1)


def keep_state(state_in):
    return state_in


def gelu_exact(values):
    return jax.nn.gelu(values, approximate=False)


def shards(
    stream,
    doc_ids,
    project,
    project_bias,
    combine,
    combine_bias,
    expand,
    expand_bias,
    shrink,
    shrink_bias,
    first_gain,
    first_bias,
    inner_gain,
    inner_bias,
    second_gain,
    second_bias,
    hidden_gain,
    hidden_bias,
    out_grad,
):
    local_count = stream.shape[0]
    head_width = project.shape[2]
    head_count = head_width // HDIM
    token_rows = lax.axis_index("seq") * local_count + jnp.arange(local_count, dtype=jnp.int32)
    center = lax.axis_size("seq") * local_count // 2
    member = (doc_ids[:, None] == jnp.arange(DOCS, dtype=jnp.int32)[None, :]).astype(jnp.int32)
    counts = lax.psum(jnp.sum(member, axis=0), "seq")
    starts = jnp.cumsum(counts) - counts
    positions = token_rows - jnp.sum(member * starts[None, :], axis=1)
    cosine, sine_table, growth = tables(positions, center)
    first_row = token_rows[0]
    last_row = token_rows[local_count - 1]
    first_doc = doc_ids[0]
    last_doc = doc_ids[local_count - 1]
    full_project, full_combine, full_expand, full_shrink = (
        lax.all_gather(project, "seq", axis=0, tiled=True),
        lax.all_gather(combine, "seq", axis=0, tiled=True),
        lax.all_gather(expand, "seq", axis=0, tiled=True),
        lax.all_gather(shrink, "seq", axis=0, tiled=True),
    )
    first_out, first_normed, first_scale = norm_full(stream, first_gain, first_bias)
    normed_in = first_out.astype(jnp.bfloat16)
    triple = (
        jnp.einsum("td,dch->tch", normed_in, full_project, preferred_element_type=jnp.float32)
        + project_bias[None]
    )
    head_shape = (local_count, head_count, HDIM)
    query_raw = triple[:, 0].reshape(head_shape)
    key_raw = triple[:, 1].reshape(head_shape)
    queries = place_query(query_raw, cosine, sine_table, growth).astype(jnp.bfloat16)
    keyed = place_key(key_raw, cosine, sine_table, growth).astype(jnp.bfloat16)
    valued = triple[:, 2].reshape(head_shape).astype(jnp.bfloat16)
    start_state = (
        jnp.full((head_count, local_count), NEGATIVE, jnp.float32),
        jnp.zeros((head_count, local_count), jnp.float32),
        jnp.zeros((head_count, local_count, HDIM), jnp.float32),
    )
    key_part = lax.all_gather(keyed.reshape(local_count, head_width), "seq", axis=0, tiled=True)
    value_part = lax.all_gather(valued.reshape(local_count, head_width), "seq", axis=0, tiled=True)
    piece_rows = key_part.shape[0]
    key_rows = jnp.arange(piece_rows, dtype=jnp.int32)
    key_docs = doc_of(key_rows, starts)
    skipped = (jnp.int32(0) > last_row) | (key_docs[piece_rows - 1] < first_doc)

    def attend_compute(state):
        running_max, running_sum, summed = state
        key_block = key_part.reshape(piece_rows, head_count, HDIM)
        value_block = value_part.reshape(piece_rows, head_count, HDIM)
        allowed = (
            (key_rows[None, :] <= token_rows[:, None]) & (key_docs[None, :] == doc_ids[:, None])
        )[None]
        scores = jnp.einsum("qhd,khd->hqk", queries, key_block, preferred_element_type=jnp.float32)
        scores = jnp.where(allowed, scores, NEGATIVE)
        newest = jnp.maximum(running_max, jnp.max(scores, axis=-1))
        weights_raw = jnp.where(allowed, jnp.exp(scores - newest[..., None]), 0.0)
        running_sum = jnp.sum(weights_raw, axis=-1)
        summed = jnp.einsum(
            "hqk,khd->hqd",
            weights_raw.astype(jnp.bfloat16),
            value_block,
            preferred_element_type=jnp.float32,
        )
        return (newest, running_sum, summed)

    running_max, running_sum, summed = lax.cond(skipped, keep_state, attend_compute, start_state)
    mixture = jnp.transpose(summed / running_sum[..., None], (1, 0, 2)).reshape(
        local_count, head_width
    )
    log_total = running_max + jnp.log(running_sum)
    inner_out, inner_normed, inner_scale = norm_split(mixture, inner_gain, inner_bias, D)
    combined_in = inner_out.astype(jnp.bfloat16)
    middle = (
        stream
        + branch_total(
            lax.dot_general(
                combined_in, full_combine, CONTRACT_LAST, preferred_element_type=jnp.float32
            )
        )
        + combine_bias
    )
    second_out, second_normed, second_scale = norm_full(middle, second_gain, second_bias)
    expand_in = second_out.astype(jnp.bfloat16)
    raised = jnp.dot(expand_in, full_expand, preferred_element_type=jnp.float32) + expand_bias
    active, gelu_back = jax.vjp(gelu_exact, raised)
    hidden_out, hidden_normed, hidden_scale = norm_split(active, hidden_gain, hidden_bias, FF)
    shrink_in = hidden_out.astype(jnp.bfloat16)
    output = (
        middle
        + branch_total(
            lax.dot_general(
                shrink_in, full_shrink, CONTRACT_LAST, preferred_element_type=jnp.float32
            )
        )
        + shrink_bias
    )
    back_project, back_combine, back_expand, back_shrink = (
        lax.all_gather(project, "seq", axis=0, tiled=True),
        lax.all_gather(combine, "seq", axis=0, tiled=True),
        lax.all_gather(expand, "seq", axis=0, tiled=True),
        lax.all_gather(shrink, "seq", axis=0, tiled=True),
    )
    shrink_bias_grad = jnp.sum(out_grad, axis=0)
    low_out = out_grad.astype(jnp.bfloat16)
    shrink_term = lax.dot_general(
        low_out, shrink_in, CONTRACT_FIRST, preferred_element_type=jnp.float32
    )
    hidden_grad = jnp.dot(low_out, back_shrink, preferred_element_type=jnp.float32)
    hidden_gain_grad = jnp.sum(hidden_grad * hidden_normed, axis=0)
    hidden_bias_grad = jnp.sum(hidden_grad, axis=0)
    active_grad = norm_split_back(hidden_grad, hidden_normed, hidden_scale, hidden_gain, FF)
    (raised_grad,) = gelu_back(active_grad)
    expand_bias_grad = jnp.sum(raised_grad, axis=0)
    low_raised = raised_grad.astype(jnp.bfloat16)
    expand_term = lax.dot_general(
        expand_in, low_raised, CONTRACT_FIRST, preferred_element_type=jnp.float32
    )
    second_grad = branch_total(
        lax.dot_general(low_raised, back_expand, CONTRACT_LAST, preferred_element_type=jnp.float32)
    )
    second_gain_grad = jnp.sum(second_grad * second_normed, axis=0)
    second_bias_grad = jnp.sum(second_grad, axis=0)
    middle_grad = out_grad + norm_full_back(second_grad, second_normed, second_scale, second_gain)
    combine_bias_grad = jnp.sum(middle_grad, axis=0)
    low_middle = middle_grad.astype(jnp.bfloat16)
    combine_term = lax.dot_general(
        low_middle, combined_in, CONTRACT_FIRST, preferred_element_type=jnp.float32
    )
    inner_grad = jnp.dot(low_middle, back_combine, preferred_element_type=jnp.float32)
    inner_gain_grad = jnp.sum(inner_grad * inner_normed, axis=0)
    inner_bias_grad = jnp.sum(inner_grad, axis=0)
    mixture_grad = norm_split_back(inner_grad, inner_normed, inner_scale, inner_gain, D)
    low_mixture = mixture_grad.astype(jnp.bfloat16)
    low_mixture3 = low_mixture.reshape(head_shape)
    delta = jnp.sum(low_mixture3.astype(jnp.float32) * mixture.reshape(head_shape), axis=-1)
    delta_heads = delta.T
    zero_heads = jnp.zeros(head_shape, jnp.float32)
    query_key_part = lax.all_gather(
        keyed.reshape(local_count, head_width), "seq", axis=0, tiled=True
    )
    query_value_part = lax.all_gather(
        valued.reshape(local_count, head_width), "seq", axis=0, tiled=True
    )
    query_piece_rows = query_key_part.shape[0]
    query_key_rows = jnp.arange(query_piece_rows, dtype=jnp.int32)
    query_key_docs = doc_of(query_key_rows, starts)
    skipped = (jnp.int32(0) > last_row) | (query_key_docs[query_piece_rows - 1] < first_doc)

    def query_compute(gathered):
        key_block = query_key_part.reshape(query_piece_rows, head_count, HDIM)
        value_block = query_value_part.reshape(query_piece_rows, head_count, HDIM)
        allowed = (
            (query_key_rows[None, :] <= token_rows[:, None])
            & (query_key_docs[None, :] == doc_ids[:, None])
        )[None]
        scores = jnp.einsum("qhd,khd->hqk", queries, key_block, preferred_element_type=jnp.float32)
        probability = jnp.where(allowed, jnp.exp(scores - log_total[..., None]), 0.0)
        pushes = jnp.einsum(
            "qhd,khd->hqk", low_mixture3, value_block, preferred_element_type=jnp.float32
        )
        dscore = (probability * (pushes - delta_heads[..., None])).astype(jnp.bfloat16)
        return jnp.einsum("hqk,khd->qhd", dscore, key_block, preferred_element_type=jnp.float32)

    query_grad3 = lax.cond(skipped, keep_state, query_compute, zero_heads)
    query_part = lax.all_gather(
        queries.astype(jnp.float32).reshape(local_count, head_width), "seq", axis=0, tiled=True
    )
    pull_part = lax.all_gather(low_mixture.astype(jnp.float32), "seq", axis=0, tiled=True)
    total_part = lax.all_gather(log_total.T, "seq", axis=0, tiled=True)
    delta_part = lax.all_gather(delta, "seq", axis=0, tiled=True)
    key_piece_rows = query_part.shape[0]
    query_rows = jnp.arange(key_piece_rows, dtype=jnp.int32)
    query_docs = doc_of(query_rows, starts)
    skipped = (query_rows[key_piece_rows - 1] < first_row) | (query_docs[0] > last_doc)

    def key_compute(state):
        query_block = query_part.astype(jnp.bfloat16).reshape(key_piece_rows, head_count, HDIM)
        pull_block = pull_part.astype(jnp.bfloat16).reshape(key_piece_rows, head_count, HDIM)
        allowed = (
            (token_rows[None, :] <= query_rows[:, None]) & (doc_ids[None, :] == query_docs[:, None])
        )[None]
        scores = jnp.einsum("qhd,khd->hqk", query_block, keyed, preferred_element_type=jnp.float32)
        probability = jnp.where(allowed, jnp.exp(scores - total_part.T[..., None]), 0.0)
        pushes = jnp.einsum("qhd,khd->hqk", pull_block, valued, preferred_element_type=jnp.float32)
        dscore = (probability * (pushes - delta_part.T[..., None])).astype(jnp.bfloat16)
        key_acc = jnp.einsum(
            "hqk,qhd->khd", dscore, query_block, preferred_element_type=jnp.float32
        )
        value_acc = jnp.einsum(
            "hqk,qhd->khd",
            probability.astype(jnp.bfloat16),
            pull_block,
            preferred_element_type=jnp.float32,
        )
        return (key_acc, value_acc)

    key_grad3, value_grad3 = lax.cond(skipped, keep_state, key_compute, (zero_heads, zero_heads))
    _, query_back = jax.vjp(
        partial(place_query, cosine=cosine, sine_table=sine_table, growth=growth), query_raw
    )
    _, key_back = jax.vjp(
        partial(place_key, cosine=cosine, sine_table=sine_table, growth=growth), key_raw
    )
    (query_grad,) = query_back(query_grad3)
    (key_grad,) = key_back(key_grad3)
    triple_grad = jnp.stack(
        [
            query_grad.reshape(local_count, head_width),
            key_grad.reshape(local_count, head_width),
            value_grad3.reshape(local_count, head_width),
        ],
        axis=1,
    )
    project_bias_grad = jnp.sum(triple_grad, axis=0)
    low_triple = triple_grad.astype(jnp.bfloat16)
    project_term = jnp.einsum(
        "td,tch->dch", normed_in, low_triple, preferred_element_type=jnp.float32
    )
    first_grad = branch_total(
        jnp.einsum("tch,dch->td", low_triple, back_project, preferred_element_type=jnp.float32)
    )
    first_gain_grad = jnp.sum(first_grad * first_normed, axis=0)
    first_bias_grad = jnp.sum(first_grad, axis=0)
    stream_grad = middle_grad + norm_full_back(first_grad, first_normed, first_scale, first_gain)
    project_grad, combine_grad, expand_grad, shrink_grad = (
        lax.psum_scatter(project_term, "seq", scatter_dimension=0, tiled=True),
        lax.psum_scatter(combine_term, "seq", scatter_dimension=0, tiled=True),
        lax.psum_scatter(expand_term, "seq", scatter_dimension=0, tiled=True),
        lax.psum_scatter(shrink_term, "seq", scatter_dimension=0, tiled=True),
    )
    (
        first_gain_grad,
        first_bias_grad,
        project_bias_grad,
        inner_gain_grad,
        inner_bias_grad,
        combine_bias_grad,
        second_gain_grad,
        second_bias_grad,
        expand_bias_grad,
        hidden_gain_grad,
        hidden_bias_grad,
        shrink_bias_grad,
    ) = lax.psum(
        (
            first_gain_grad,
            first_bias_grad,
            project_bias_grad,
            inner_gain_grad,
            inner_bias_grad,
            combine_bias_grad,
            second_gain_grad,
            second_bias_grad,
            expand_bias_grad,
            hidden_gain_grad,
            hidden_bias_grad,
            shrink_bias_grad,
        ),
        "seq",
    )
    return (
        output,
        stream_grad,
        project_grad,
        project_bias_grad,
        combine_grad,
        combine_bias_grad,
        expand_grad,
        expand_bias_grad,
        shrink_grad,
        shrink_bias_grad,
        first_gain_grad,
        first_bias_grad,
        inner_gain_grad,
        inner_bias_grad,
        second_gain_grad,
        second_bias_grad,
        hidden_gain_grad,
        hidden_bias_grad,
    )


BF = jnp.bfloat16
F32 = jnp.float32
GRID = (4, 2, 2)
SEQ = 16
ALIGNED = (((0,), (0,)), ((), ()))
PLAIN = (((1,), (0,)), ((), ()))
HOPS = {
    "x": [(i, i ^ 1) for i in range(SEQ)],
    "y": [(i, i ^ 2) for i in range(SEQ)],
    "xy": [(i, i ^ 3) for i in range(SEQ)],
    "z1": [(i, (i + 4) % SEQ) for i in range(SEQ)],
    "z2": [(i, (i + 8) % SEQ) for i in range(SEQ)],
    "z3": [(i, (i + 12) % SEQ) for i in range(SEQ)],
}
COLUMN = ("z1", "z2", "z3")


def fits_heads(mesh):
    return mesh.shape["seq"] == SEQ and mesh.shape["tp"] == 2


def hop(values, way):
    if way == "t":
        return lax.ppermute(values, "tp", [(0, 1), (1, 0)])
    return lax.ppermute(values, "seq", HOPS[way])


def after(first, *later):
    return lax.optimization_barrier((first,) + later)


def gather_along(values, way, axis):
    return jnp.stack([values, hop(values, way)], axis=axis)


def gather_column(own):
    return jnp.stack([own] + [hop(own, way) for way in COLUMN])


def gather_plane(column, midway=None):
    half = column.shape[2] // 2
    left = gather_along(column[:, :, :half], "x", 1)
    right = gather_along(column[:, :, half:], "y", 1)
    done = None
    if midway is not None:
        left, right, done = midway(left, right)
    mine = [gather_along(left, "y", 1), gather_along(right, "x", 2)]
    mine = [piece.reshape(-1, half) for piece in mine]
    if midway is not None:
        mine[0], mine[1], *done = after(mine[0], mine[1], *done)
    return mine + [hop(piece, "t") for piece in mine], done


def gather_small(values):
    return gather_along(gather_along(gather_column(values), "x", 1), "y", 1)


def add_low(first, second):
    return (first.astype(F32) + second.astype(F32)).astype(BF)


def fold(values, way, axis):
    near = lax.index_in_dim(values, 0, axis, keepdims=False)
    far = lax.index_in_dim(values, 1, axis, keepdims=False)
    return add_low(near, hop(far, way))


def scatter_pair(low, own, others):
    return [
        (dot(low, weights, own[0]) + hop(other, "t").astype(F32)).astype(BF)
        for weights, other in zip(own[1], others, strict=True)
    ]


def scatter_wide(pair):
    shape = GRID + (-1, pair[0].shape[1])
    return [fold(pair[0].reshape(shape), "y", 1), fold(pair[1].reshape(shape), "x", 2)]


def scatter_narrow(halves):
    return jnp.concatenate([fold(halves[0], "x", 1), fold(halves[1], "y", 1)], axis=2)


def scatter_plane(pair):
    return scatter_narrow(scatter_wide(pair))


def scatter_column(slabs):
    total = slabs[0].astype(F32)
    for i in range(1, 4):
        total = total + lax.optimization_barrier(hop(slabs[i], COLUMN[3 - i])).astype(F32)
    return total


def swap_by(flag, values, axis):
    return jnp.where(flag == 0, values, jnp.flip(values, axis))


def own_half(side, values, axis=-1):
    left, right = jnp.split(values, 2, axis=axis)
    return jnp.where(side == 0, left, right)


def join_halves(side, mine, other, axis=-1):
    return jnp.concatenate(
        [jnp.where(side == 0, mine, other), jnp.where(side == 0, other, mine)], axis=axis
    )


def turn_halves(side, values, axis=0):
    left, right = jnp.split(values, 2, axis=axis)
    return jnp.concatenate(
        [jnp.where(side == 0, left, right), jnp.where(side == 0, right, left)], axis=axis
    )


def token_sum(values):
    shape = values.shape
    values = (values + hop(values, "t")).reshape((shape[0],) + GRID + (-1,))
    moved = [jnp.flip(hop(values, "x"), 3), jnp.flip(hop(values, "y"), 2)]
    values = values + moved[0] + moved[1] + jnp.flip(hop(values, "xy"), (2, 3))
    moved = [jnp.roll(hop(values, COLUMN[i]), i + 1, 1) for i in range(3)]
    return (values + moved[0] + moved[1] + moved[2]).reshape(shape)


def seq_sum(values):
    values = values + hop(values, "x") + hop(values, "y") + hop(values, "xy")
    return values + hop(values, "z1") + hop(values, "z2") + hop(values, "z3")


def pair_sum(values):
    return values + hop(values, "t")


def dot(first, second, dims):
    return lax.dot_general(first, second, dims, preferred_element_type=F32)


BLOCK = 512
CHUNK = 256
SPARE = 16
KERNEL_BYTES = 48 * 1024 * 1024


def attend_kernel(
    order_ref, first_ref, second_ref, third_ref, fourth_ref, weights_ref, bias_ref,
    cosine_ref, sine_ref, growth_ref, begin_ref, kept_ref, mixture_ref, sent_ref, log_ref, wide,
):
    step = pl.program_id(0)
    part = first_ref.shape[1]
    rows = mixture_ref.shape[2]
    raw = bias_ref[...]
    for index, piece in enumerate((first_ref, second_ref, third_ref, fourth_ref)):
        raw = raw + dot(
            weights_ref[:, index * part : (index + 1) * part], piece[...], CONTRACT_LAST
        )
    for block in range(CHUNK // rows):
        place = order_ref[step * (CHUNK // rows) + block] * rows
        wide[:, pl.ds(pl.multiple_of(place, rows), rows)] = raw[:, block * rows : (block + 1) * rows]

    @pl.when(step == pl.num_programs(0) - 1)
    def _():
        attend_head(
            cosine_ref, sine_ref, growth_ref, begin_ref, kept_ref, mixture_ref, sent_ref, log_ref,
            wide,
        )


def attend_head(
    cosine_ref, sine_ref, growth_ref, begin_ref, kept_ref, mixture_ref, sent_ref, log_ref, wide
):
    tokens = wide.shape[1]
    half = HDIM // 2
    rows = tokens // SEQ
    cosine, sine, growth = cosine_ref[...], sine_ref[...], growth_ref[...]
    first, second = wide[0:half, :], wide[half:HDIM, :]
    scaled = growth * HDIM ** (-0.5)
    kept_ref[0:half, :] = ((first * cosine - second * sine) * scaled).astype(BF)
    kept_ref[half:HDIM, :] = ((second * cosine + first * sine) * scaled).astype(BF)
    first, second = wide[HDIM : HDIM + half, :], wide[HDIM + half : 2 * HDIM, :]
    kept_ref[HDIM : HDIM + half, :] = ((first * cosine - second * sine) / growth).astype(BF)
    kept_ref[HDIM + half : 2 * HDIM, :] = ((second * cosine + first * sine) / growth).astype(BF)
    kept_ref[2 * HDIM :, :] = wide[2 * HDIM :, :].astype(BF)
    key_rows = lax.broadcasted_iota(jnp.int32, (BLOCK, BLOCK), 0)
    query_rows = lax.broadcasted_iota(jnp.int32, (BLOCK, BLOCK), 1)
    spare = lax.broadcasted_iota(jnp.int32, (SPARE, BLOCK), 0)
    for i in range(tokens // BLOCK):
        columns = slice(i * BLOCK, (i + 1) * BLOCK)
        queries = kept_ref[0:HDIM, columns]
        begin = begin_ref[:, columns]
        largest = jnp.full((1, BLOCK), NEGATIVE, F32)
        total = jnp.zeros((1, BLOCK), F32)
        summed = jnp.zeros((HDIM, BLOCK), F32)
        for j in range(i, -1, -1):
            place = slice(j * BLOCK, (j + 1) * BLOCK)
            scores = dot(kept_ref[HDIM : 2 * HDIM, place], queries, ALIGNED)
            allowed = key_rows + j * BLOCK >= begin
            if j == i:
                allowed = allowed & (key_rows <= query_rows)
            scores = jnp.where(allowed, scores, NEGATIVE)
            newest = jnp.maximum(largest, jnp.max(scores, axis=0, keepdims=True))
            weights = jnp.exp(scores - newest)
            shrunk = jnp.exp(largest - newest)
            total = total * shrunk + jnp.sum(weights, axis=0, keepdims=True)
            summed = summed * shrunk + dot(
                kept_ref[2 * HDIM :, place], weights.astype(BF), PLAIN
            )
            largest = newest
        mixture = summed / total
        average = jnp.mean(mixture, axis=0, keepdims=True)
        high = average.astype(BF).astype(F32)
        low = (average - high).astype(BF).astype(F32)
        tail = jnp.where(spare == 0, high, jnp.where(spare == 1, low, average - high - low))
        sent = jnp.concatenate([mixture - average, jnp.where(spare < 3, tail, 0.0)], axis=0).astype(BF)
        for block in range(BLOCK // rows):
            place = slice(block * rows, (block + 1) * rows)
            mixture_ref[i * (BLOCK // rows) + block] = mixture[:, place]
            sent_ref[i * (BLOCK // rows) + block] = sent[:, place]
        log_ref[:, columns] = largest + jnp.log(total)


def retreat_kernel(
    order_ref, kept_ref, pull_ref, mixture_ref, log_ref, cosine_ref, sine_ref, growth_ref, begin_ref,
    low_ref, bias_ref, pulls, delta, query_sum, key_sum, value_sum,
):
    tokens = kept_ref.shape[1]
    half = HDIM // 2
    rows = tokens // SEQ
    for block in range(SEQ):
        place = slice(block * rows, (block + 1) * rows)
        pulls[:, place] = pull_ref[block]
        delta[:, place] = jnp.sum(
            pull_ref[block].astype(F32) * mixture_ref[block], axis=0, keepdims=True
        )
    key_rows = lax.broadcasted_iota(jnp.int32, (BLOCK, BLOCK), 0)
    query_rows = lax.broadcasted_iota(jnp.int32, (BLOCK, BLOCK), 1)
    for i in range(tokens // BLOCK):
        columns = slice(i * BLOCK, (i + 1) * BLOCK)
        queries = kept_ref[0:HDIM, columns]
        pull = pulls[:, columns]
        begin = begin_ref[:, columns]
        logs = log_ref[:, columns]
        offset = delta[:, columns]
        query_part = jnp.zeros((HDIM, BLOCK), F32)
        for j in range(i + 1):
            place = slice(j * BLOCK, (j + 1) * BLOCK)
            keys = kept_ref[HDIM : 2 * HDIM, place]
            scores = dot(keys, queries, ALIGNED)
            allowed = key_rows + j * BLOCK >= begin
            if j == i:
                allowed = allowed & (key_rows <= query_rows)
            chance = jnp.where(allowed, jnp.exp(scores - logs), 0.0)
            pushes = dot(kept_ref[2 * HDIM :, place], pull, ALIGNED)
            dscore = (chance * (pushes - offset)).astype(BF)
            query_part = query_part + dot(keys, dscore, PLAIN)
            key_part = dot(queries, dscore, CONTRACT_LAST)
            value_part = dot(pull, chance.astype(BF), CONTRACT_LAST)
            if j == i:
                key_sum[:, place] = key_part
                value_sum[:, place] = value_part
            else:
                key_sum[:, place] += key_part
                value_sum[:, place] += value_part
        query_sum[:, columns] = query_part
    cosine, sine, growth = cosine_ref[...], sine_ref[...], growth_ref[...]
    scaled = growth * HDIM ** (-0.5)
    first, second = query_sum[0:half, :] * scaled, query_sum[half:, :] * scaled
    pieces = [first * cosine + second * sine, second * cosine - first * sine]
    first, second = key_sum[0:half, :] / growth, key_sum[half:, :] / growth
    pieces += [first * cosine + second * sine, second * cosine - first * sine]
    pieces += [value_sum[0:half, :], value_sum[half:, :]]
    for index, piece in enumerate(pieces):
        lanes = slice(index * half, (index + 1) * half)
        bias_ref[lanes, :] = jnp.sum(piece, axis=1, keepdims=True)
        low = piece.astype(BF)
        for block in range(SEQ):
            place = pl.ds(pl.multiple_of(order_ref[block] * rows, rows), rows)
            low_ref[lanes, place] = low[:, block * rows : (block + 1) * rows]


def whole(count):
    return [pl.BlockSpec(memory_space=pltpu.VMEM) for _ in range(count)]


def attend(order, pieces, weights, bias, cosine, sine, growth, begin):
    tokens, part = pieces[0].shape
    depth = weights.shape[1]
    table = still((HDIM // 2, tokens))
    return pl.pallas_call(
        attend_kernel,
        grid_spec=pltpu.PrefetchScalarGridSpec(
            num_scalar_prefetch=1,
            grid=(tokens // CHUNK,),
            in_specs=[pl.BlockSpec((CHUNK, part), lambda i, order: (i, 0)) for _ in pieces]
            + [still((3 * HDIM, depth)), still((3 * HDIM, 1)), table, table, table, still((1, tokens))],
            out_specs=(
                still((3 * HDIM, tokens)),
                still((SEQ, HDIM, tokens // SEQ)),
                still((SEQ, HDIM + SPARE, tokens // SEQ)),
                still((1, tokens)),
            ),
            scratch_shapes=[pltpu.VMEM((3 * HDIM, tokens), F32)],
        ),
        out_shape=(
            jax.ShapeDtypeStruct((3 * HDIM, tokens), BF),
            jax.ShapeDtypeStruct((SEQ, HDIM, tokens // SEQ), F32),
            jax.ShapeDtypeStruct((SEQ, HDIM + SPARE, tokens // SEQ), BF),
            jax.ShapeDtypeStruct((1, tokens), F32),
        ),
        compiler_params=pltpu.CompilerParams(vmem_limit_bytes=KERNEL_BYTES),
        cost_estimate=pl.CostEstimate(
            flops=2 * tokens * tokens * HDIM, bytes_accessed=2 * tokens * depth,
            transcendentals=tokens * tokens // 2,
        ),
    )(order, *pieces, weights, bias, cosine, sine, growth, begin)


def retreat(order, kept, pull, mixture, logs, cosine, sine, growth, begin):
    tokens = kept.shape[1]
    return pl.pallas_call(
        retreat_kernel,
        out_shape=(
            jax.ShapeDtypeStruct((3 * HDIM, tokens), BF),
            jax.ShapeDtypeStruct((3 * HDIM, 1), F32),
        ),
        in_specs=[pl.BlockSpec(memory_space=pltpu.SMEM)] + whole(8),
        out_specs=tuple(whole(2)),
        scratch_shapes=[
            pltpu.VMEM((HDIM, tokens), BF),
            pltpu.VMEM((1, tokens), F32),
            pltpu.VMEM((HDIM, tokens), F32),
            pltpu.VMEM((HDIM, tokens), F32),
            pltpu.VMEM((HDIM, tokens), F32),
        ],
        compiler_params=pltpu.CompilerParams(vmem_limit_bytes=KERNEL_BYTES),
        cost_estimate=pl.CostEstimate(
            flops=5 * tokens * tokens * HDIM, bytes_accessed=8 * 192 * tokens,
            transcendentals=tokens * tokens // 2,
        ),
    )(order, kept, pull, mixture, logs, cosine, sine, growth, begin)


def enter_kernel(
    first_ref, second_ref, third_ref, fourth_ref, grad_ref, expand_ref, shift_ref, gain_ref,
    active_ref, slope_ref, stats_ref,
):
    part = first_ref.shape[1]
    raised = shift_ref[...]
    for index, piece in enumerate((first_ref, second_ref, third_ref, fourth_ref)):
        raised = raised + dot(piece[...], expand_ref[index * part : (index + 1) * part, :], PLAIN)
    chance = 0.5 * (1.0 + lax.erf(raised * math.sqrt(0.5)))
    active = raised * chance
    active_ref[...] = active
    slope_ref[...] = chance + raised * jnp.exp(raised * raised * -0.5) * (1.0 / math.sqrt(2.0 * math.pi))
    scaled = grad_ref[...] * gain_ref[...]
    lane = lax.broadcasted_iota(jnp.int32, (CHUNK, 128), 1)
    columns = jnp.zeros((CHUNK, 128), F32)
    for index, values in enumerate((active, active * active, scaled, scaled * active)):
        columns = jnp.where(lane == index, jnp.sum(values, axis=1, keepdims=True), columns)
    stats_ref[...] = columns.T[0:8, :]


def leave_kernel(
    active_ref, slope_ref, grad_ref, stats_ref, expand_ref, gain_ref, shift_ref,
    shrunk_ref, low_ref, first_ref, second_ref, sums_ref,
):
    @pl.when(pl.program_id(0) == 0)
    def _():
        sums_ref[...] = jnp.zeros_like(sums_ref)

    columns = jnp.concatenate([stats_ref[...], jnp.zeros((120, CHUNK), F32)], axis=0).T
    average, scale, grad_mean, cross_mean = (columns[:, i : i + 1] for i in range(4))
    hidden_grad = grad_ref[...]
    normed = (active_ref[...] - average) * scale
    shrunk_ref[...] = (normed * gain_ref[...] + shift_ref[...]).astype(BF)
    raised_grad = (
        scale * (hidden_grad * gain_ref[...] - grad_mean - normed * cross_mean) * slope_ref[...]
    )
    low = raised_grad.astype(BF)
    low_ref[...] = low
    sums_ref[0:1, :] += jnp.sum(hidden_grad * normed, axis=0, keepdims=True)
    sums_ref[1:2, :] += jnp.sum(hidden_grad, axis=0, keepdims=True)
    sums_ref[2:3, :] += jnp.sum(raised_grad, axis=0, keepdims=True)
    part = first_ref.shape[1]
    for index, out_ref in enumerate((first_ref, second_ref)):
        out_ref[...] = dot(
            low, expand_ref[index * part : (index + 1) * part, :], CONTRACT_LAST
        ).astype(BF)


def still(shape):
    return pl.BlockSpec(shape, lambda *_: (0,) * len(shape))


def enter(pieces, grad, expand_mine, shift, gain):
    tokens, part = pieces[0].shape
    depth, units = expand_mine.shape
    block = pl.BlockSpec((CHUNK, units), lambda i: (i, 0))
    wide = jax.ShapeDtypeStruct((tokens, units), F32)
    return pl.pallas_call(
        enter_kernel,
        grid=(tokens // CHUNK,),
        in_specs=[pl.BlockSpec((CHUNK, part), lambda i: (i, 0)) for _ in pieces]
        + [block, still((depth, units)), still((1, units)), still((1, units))],
        out_specs=(block, block, pl.BlockSpec((8, CHUNK), lambda i: (0, i))),
        out_shape=(wide, wide, jax.ShapeDtypeStruct((8, tokens), F32)),
        compiler_params=pltpu.CompilerParams(vmem_limit_bytes=KERNEL_BYTES),
        cost_estimate=pl.CostEstimate(
            flops=2 * tokens * depth * units, bytes_accessed=6 * tokens * depth, transcendentals=0
        ),
    )(*pieces, grad, expand_mine, shift, gain)


def leave(active, slope, grad, stats, expand_other, gain, shift):
    tokens, units = active.shape
    depth = expand_other.shape[0]
    block = pl.BlockSpec((CHUNK, units), lambda i: (i, 0))
    piece = pl.BlockSpec((CHUNK, depth // 2), lambda i: (i, 0))
    low = jax.ShapeDtypeStruct((tokens, units), BF)
    partial_sum = jax.ShapeDtypeStruct((tokens, depth // 2), BF)
    return pl.pallas_call(
        leave_kernel,
        grid=(tokens // CHUNK,),
        in_specs=[block, block, block, pl.BlockSpec((8, CHUNK), lambda i: (0, i))]
        + [still((depth, units)), still((1, units)), still((1, units))],
        out_specs=(block, block, piece, piece, still((8, units))),
        out_shape=(low, low) + (partial_sum,) * 2 + (jax.ShapeDtypeStruct((8, units), F32),),
        compiler_params=pltpu.CompilerParams(vmem_limit_bytes=KERNEL_BYTES),
        cost_estimate=pl.CostEstimate(
            flops=2 * tokens * depth * units, bytes_accessed=6 * tokens * depth, transcendentals=0
        ),
    )(active, slope, grad, stats, expand_other, gain, shift)


def to_owners(values):
    return lax.all_to_all(values, "seq", split_axis=0, concat_axis=0, tiled=True)


def by_owner(weights, rows):
    return jnp.transpose(weights.reshape(rows, SEQ, -1), (1, 0, 2))


def columns_of(moved, side):
    return turn_halves(side, moved.reshape(-1, moved.shape[2]))


def by_row_owner(pieces, side):
    full = turn_halves(side, jnp.concatenate(pieces, axis=0))
    return full.reshape(SEQ, -1, full.shape[1])


def rows_of(moved):
    return jnp.transpose(moved, (1, 0, 2)).reshape(moved.shape[1], -1).astype(F32)


def head_shards(
    stream,
    doc_ids,
    project,
    project_bias,
    combine,
    combine_bias,
    expand,
    expand_bias,
    shrink,
    shrink_bias,
    first_gain,
    first_bias,
    inner_gain,
    inner_bias,
    second_gain,
    second_bias,
    hidden_gain,
    hidden_bias,
    out_grad,
):
    rows = stream.shape[0]
    tokens = SEQ * rows
    head_width = project.shape[2]
    width = expand.shape[1] // SEQ
    spot = lax.axis_index("seq")
    side = lax.axis_index("tp")
    spot_z, spot_y, spot_x = spot // 4, (spot // 2) % 2, spot % 2
    blocks = jnp.arange(SEQ, dtype=jnp.int32)
    order = (
        ((spot_z - blocks // 4) % 4) * 4 + (spot_y ^ ((blocks // 2) % 2)) * 2 + (spot_x ^ (blocks % 2))
    )

    def mine(values, axis=-1):
        return own_half(side, values, axis)

    def my_units(vector, size):
        return lax.dynamic_slice_in_dim(vector, spot * size, size, axis=-1)

    first_out, first_normed, first_scale = norm_full(stream, first_gain, first_bias)
    normed_column = gather_column(mine(first_out.astype(BF)))
    docs_near = gather_small(doc_ids[None, :]).reshape(SEQ, rows)
    full_combine = lax.all_gather(combine, "seq", axis=0, tiled=True)
    out_grad_mine = mine(out_grad)
    low_out = lax.all_gather(out_grad_mine.astype(BF), "seq", axis=0, tiled=True)
    normed_column, project_own = after(
        normed_column,
        jnp.transpose(project.reshape(rows, 3, SEQ, HDIM), (2, 1, 3, 0)).reshape(
            SEQ, 3 * HDIM, rows
        ),
    )
    normed_pieces, _ = gather_plane(normed_column)
    project_moved = to_owners(project_own)
    project_mine = turn_halves(
        side, jnp.transpose(project_moved, (1, 0, 2)).reshape(3 * HDIM, tokens), axis=1
    )
    project_pieces = jnp.split(project_mine, 4, axis=1)

    docs = docs_near[order].reshape(tokens)
    member = (docs[:, None] == jnp.arange(DOCS, dtype=jnp.int32)[None, :]).astype(jnp.int32)
    counts = jnp.sum(member, axis=0)
    starts = jnp.cumsum(counts) - counts
    begin = jnp.sum(member * starts[None, :], axis=1)
    positions = jnp.arange(tokens, dtype=jnp.int32) - begin
    column = jnp.arange(HDIM // 2, dtype=F32)
    frequency = jnp.exp(column * (-2.0 * math.log(10000.0) / HDIM))
    base_ratio = (2.0 * column + 0.4 * HDIM) / (1.4 * HDIM)
    location = positions.astype(F32)
    phase_angle = frequency[:, None] * location[None, :]
    cosine, sine = jnp.cos(phase_angle), jnp.sin(phase_angle)
    growth = jnp.exp(
        jnp.log(base_ratio)[:, None] * ((location - tokens // 2) / SCALE_BASE)[None, :]
    )
    begin = begin[None, :]

    head_bias = my_units(project_bias, HDIM).reshape(3 * HDIM, 1)
    kept, mixture, sent, logs = attend(
        order, normed_pieces, project_mine, head_bias, cosine, sine, growth, begin
    )

    sent = to_owners(sent).astype(F32)
    averages = jnp.sum(sent[:, HDIM : HDIM + 3], axis=1, keepdims=True)
    spread = (sent[:, :HDIM] + averages).reshape(head_width, rows)
    sums = pair_sum(jnp.stack([jnp.sum(spread, axis=0), jnp.sum(spread * spread, axis=0)]))
    average = sums[0:1] / D
    inner_scale = lax.rsqrt(sums[1:2] / D - average * average + EPSILON)
    inner_normed = (spread - average) * inner_scale
    combined_in = (inner_normed * inner_gain[:, None] + inner_bias[:, None]).astype(BF)
    branch = dot(combined_in, full_combine, (((0,), (1,)), ((), ())))
    left, right = jnp.split(branch, 2, axis=1)
    branch = jnp.where(side == 0, left, right) + hop(jnp.where(side == 0, right, left), "t")
    middle = mine(stream) + branch + mine(combine_bias)
    sums = pair_sum(jnp.stack([jnp.sum(middle, axis=1), jnp.sum(middle * middle, axis=1)]))
    average = (sums[0] / D)[:, None]
    second_scale = lax.rsqrt((sums[1] / D)[:, None] - average * average + EPSILON)
    second_normed = (middle - average) * second_scale
    gain_half, bias_half = mine(second_gain), mine(second_bias)
    expand_column = gather_column((second_normed * gain_half + bias_half).astype(BF))
    expand_column, shrink_own = after(expand_column, by_owner(shrink, rows))
    shrink_moved = to_owners(shrink_own)

    def pull_back(left, right):
        left, right, units, expand_own = after(left, right, shrink_moved, by_owner(expand, rows))
        _, near = after(left, low_out)
        shrink_mine = columns_of(units, side)
        low = [near, hop(near, "t")]
        grad = sum(
            dot(piece, part, PLAIN)
            for piece, part in zip(low, jnp.split(shrink_mine, 2, axis=0), strict=True)
        )
        grad = grad.reshape(SEQ, rows, width)[order].reshape(tokens, width)
        return left, right, (low[0], low[1], grad, shrink_mine, to_owners(expand_own))

    expand_pieces, midway = gather_plane(expand_column, pull_back)
    low_out, (hidden_grad, shrink_mine) = midway[:2], midway[2:4]
    expand_mine = columns_of(midway[4], side)

    unit_gain, unit_bias = my_units(hidden_gain, width)[None, :], my_units(hidden_bias, width)[None, :]
    active, slope, sums = enter(
        expand_pieces, hidden_grad, expand_mine, my_units(expand_bias, width)[None, :], unit_gain
    )
    sums, combined_late = after(token_sum(sums[0:4]), combined_in.T)
    full_combined = lax.all_gather(combined_late, "seq", axis=0, tiled=True)
    average = sums[0:1] / FF
    hidden_scale = lax.rsqrt(sums[1:2] / FF - average * average + EPSILON)
    grad_mean = sums[2:3] / FF
    cross_mean = hidden_scale * (sums[3:4] / FF - average * grad_mean)
    stats = jnp.concatenate(
        [average, hidden_scale, grad_mean, cross_mean, jnp.zeros((4, tokens), F32)]
    )
    expand_parts = jnp.split(expand_mine, 4, axis=0)
    left = leave(
        active, slope, hidden_grad, stats, expand_mine[expand_mine.shape[0] // 2 :], unit_gain, unit_bias
    )
    pair, shrink_in, low_raised = after(
        scatter_pair(left[1], (CONTRACT_LAST, expand_parts[:2]), left[2:4]), left[0], left[1]
    )
    shrink_far = shrink_in.reshape(SEQ, rows, width)[order].reshape(tokens, width)
    shrink_term = by_row_owner(
        [dot(piece, shrink_far, CONTRACT_FIRST).astype(BF) for piece in low_out], side
    )
    halves, shrink_in, low_raised = after(scatter_wide(pair), shrink_in, low_raised)
    slabs, shrink_moved = after(scatter_narrow(halves), to_owners(shrink_term))
    shrink_grad = rows_of(shrink_moved)
    second_grad = scatter_column(slabs)
    expand_term = by_row_owner(
        [dot(piece, low_raised, CONTRACT_FIRST).astype(BF) for piece in expand_pieces], side
    )
    shrink_parts = jnp.split(shrink_mine, 4, axis=0)
    others = [dot(shrink_in, weights, CONTRACT_LAST).astype(BF) for weights in shrink_parts[2:]]
    output_pair = scatter_pair(shrink_in, (CONTRACT_LAST, shrink_parts[:2]), others)
    second_grad, expand_term, output_pair = after(second_grad, expand_term, output_pair)
    expand_moved = to_owners(expand_term)
    output_halves = scatter_wide(output_pair)

    scaled = second_grad * gain_half
    sums = pair_sum(jnp.stack([jnp.sum(scaled, axis=1), jnp.sum(scaled * second_normed, axis=1)]))
    middle_grad = out_grad_mine + second_scale * (
        scaled - (sums[0] / D)[:, None] - second_normed * (sums[1] / D)[:, None]
    )
    low_middle = middle_grad.astype(BF)
    low_middle = join_halves(side, low_middle, hop(low_middle, "t"))
    inner_grad = dot(full_combine, low_middle, (((0,), (1,)), ((), ())))
    scaled = inner_grad * inner_gain[:, None]
    sums = pair_sum(jnp.stack([jnp.sum(scaled, axis=0), jnp.sum(scaled * inner_normed, axis=0)]))
    mixture_grad = inner_scale * (scaled - sums[0:1] / D - inner_normed * (sums[1:2] / D))
    mixture_grad, expand_moved, output_halves, full_combined = after(
        mixture_grad.astype(BF).reshape(SEQ, HDIM, rows), expand_moved, output_halves, full_combined
    )
    expand_grad = rows_of(expand_moved)
    pull, low_middle, output_slabs = after(
        to_owners(mixture_grad), low_middle, scatter_narrow(output_halves)
    )
    output = middle + scatter_column(output_slabs) + mine(shrink_bias)
    moved = to_owners(by_owner(low_middle, rows))

    low_triple, head_sums = retreat(
        order, kept, pull, mixture, logs, cosine, sine, growth, begin
    )
    others = [dot(low_triple, weights, CONTRACT_FIRST).astype(BF) for weights in project_pieces[2:]]
    others, moved, output = after(others, moved, output)
    combine_grad = dot(moved.reshape(tokens, -1), full_combined, CONTRACT_FIRST)
    pair = scatter_pair(low_triple, (CONTRACT_FIRST, project_pieces[:2]), others)
    term = turn_halves(
        side,
        jnp.concatenate(
            [dot(low_triple, piece, PLAIN).astype(BF) for piece in normed_pieces], axis=1
        ),
        axis=1,
    )
    pair[0], term = after(pair[0], term)
    moved = to_owners(jnp.transpose(term.reshape(3 * HDIM, SEQ, rows), (1, 0, 2)))
    slabs, moved = after(scatter_plane(pair), moved)
    first_grad = scatter_column(slabs)
    project_grad = jnp.transpose(moved.reshape(SEQ, 3, HDIM, rows), (3, 1, 0, 2)).reshape(
        rows, 3, head_width
    ).astype(F32)
    normed_half = mine(first_normed)
    scaled = first_grad * mine(first_gain)
    sums = pair_sum(jnp.stack([jnp.sum(scaled, axis=1), jnp.sum(scaled * normed_half, axis=1)]))
    stream_grad = middle_grad + first_scale * (
        scaled - (sums[0] / D)[:, None] - normed_half * (sums[1] / D)[:, None]
    )

    unit_sums = lax.dynamic_update_slice(
        jnp.zeros((3, SEQ * width), F32), left[4][0:3], (0, spot * width)
    )
    head_sums = lax.dynamic_update_slice(
        jnp.zeros((3, head_width), F32), head_sums.reshape(3, HDIM), (0, spot * HDIM)
    )
    early = [
        jnp.sum(out_grad_mine, axis=0),
        jnp.sum(second_grad * second_normed, axis=0),
        jnp.sum(second_grad, axis=0),
        jnp.sum(middle_grad, axis=0),
        jnp.sum(inner_grad * inner_normed, axis=1),
        jnp.sum(inner_grad, axis=1),
    ]
    early = seq_sum(
        jnp.concatenate([jnp.stack(early), head_sums, unit_sums.reshape(-1, head_width)])
    )
    late = seq_sum(jnp.stack([jnp.sum(first_grad * normed_half, axis=0), jnp.sum(first_grad, axis=0)]))
    halves = join_halves(side, early[:4], hop(early[:4], "t"))
    late = join_halves(side, late, hop(late, "t"))
    project_bias_grad = early[6:9]
    unit_sums = early[9:].reshape(3, SEQ * width)
    return (
        join_halves(side, output, hop(output, "t")),
        join_halves(side, stream_grad, hop(stream_grad, "t")),
        project_grad,
        project_bias_grad,
        combine_grad,
        halves[3],
        expand_grad,
        unit_sums[2],
        shrink_grad,
        halves[0],
        late[0],
        late[1],
        early[4],
        early[5],
        halves[1],
        halves[2],
        unit_sums[0],
        unit_sums[1],
    )


def solution(mesh):
    plan = head_shards if fits_heads(mesh) else shards
    return jax.shard_map(
        plan,
        mesh=mesh,
        in_specs=(
            P("seq", None),
            P("seq"),
            P("seq", None, "tp"),
            P(None, "tp"),
            P("seq", "tp"),
            P(),
            P("seq", "tp"),
            P("tp"),
            P("seq", "tp"),
            P(),
            P(),
            P(),
            P("tp"),
            P("tp"),
            P(),
            P(),
            P("tp"),
            P("tp"),
            P("seq", None),
        ),
        out_specs=(
            P("seq", None),
            P("seq", None),
            P("seq", None, "tp"),
            P(None, "tp"),
            P("seq", "tp"),
            P(),
            P("seq", "tp"),
            P("tp"),
            P("seq", "tp"),
            P(),
            P(),
            P(),
            P("tp"),
            P("tp"),
            P(),
            P(),
            P("tp"),
            P("tp"),
        ),
        check_vma=False,
    )
```
